256 devices in a mesh: sp: 32 (over z, y_lo, core), flt: 8 (over x, y_hi).
Axes of the slice: x: 4, y: 4 (y_hi: 2, y_lo: 2; y = y_hi * 2 + y_lo), z: 8, core: 2. Of those that a mesh axis runs over, the one named last changes fastest.
Arguments:
- activations: bfloat16 [64, 64, 8, 256], P('sp', 'flt'), may hold values from -6 to 6
- w_first: bfloat16 [256, 3, 3, 3, 256], P('flt'), may hold values from -0.078125 to 0.078125
- w_second: bfloat16 [256, 3, 3, 3, 256], P('flt'), may hold values from -0.078125 to 0.078125
- cotangent: bfloat16 [32, 32, 4, 256], P('sp', 'flt'), may hold values from -6 to 6
Outputs:
- section_out: float32 [32, 32, 4, 256], P('sp', 'flt')
- grad_input: float32 [64, 64, 8, 256], P('sp', 'flt')
- grad_first: float32 [256, 3, 3, 3, 256], P('flt')
- grad_second: float32 [256, 3, 3, 3, 256], P('flt')
The draws below stay inside these ranges and needn't reach their ends.
All inputs are finite; a program needn't handle non-finite values.
Results may differ from the reference program's by a relative error of at most 0.0045.
Values may be sent and summed in bfloat16 or wider, within the bound.
No kernel may reach another device: no remote copies, remote signals or barrier semaphores. Data moves between devices by JAX's collectives and lax.ppermute only.
A program may use at most 64 MiB of HBM per device.

```python
import jax
import jax.numpy as jnp
from jax import lax

C = 256
Z = 8
X = 64
Y = 64


def block_scale(own_key, shape, shards, least, largest):
    def one(axis_at, shards_of):
        draws = jax.random.uniform(jax.random.fold_in(jax.random.fold_in(own_key, 6), axis_at), (shards_of,), jnp.float32, least / len(shards), largest / len(shards))
        return jnp.repeat(jnp.exp(draws), shape[axis_at] // shards_of).reshape((-1,) + (1,) * (len(shape) - axis_at - 1))

    level = one(*shards[0])
    for cut in shards[1:]:
        level = level * one(*cut)
    return level


def gaussian(key, dims, spread, bound, pieces=(), held_as=jnp.bfloat16):
    entries = spread * jax.random.normal(key, dims, jnp.float32)
    if pieces:
        entries = entries * block_scale(key, dims, pieces, -0.22, 0.18)
    return jnp.clip(entries, -bound, bound).astype(held_as)


def setup_inputs(seed: int = 0) -> dict:
    seeds = jax.random.split(jax.random.key(seed), 5)
    return {
        "activations": gaussian(seeds[0], (X, Y, Z, C), 1.0, 6.0, ((0, 32), (1, 8))),
        "w_first": gaussian(seeds[1], (C, 3, 3, 3, C), (27 * C) ** -0.5, 0.078125, ((0, 8),)),
        "w_second": gaussian(seeds[2], (C, 3, 3, 3, C), (27 * C) ** -0.5, 0.078125, ((0, 8),)),
        "cotangent": gaussian(seeds[3], (X // 2, Y // 2, Z // 2, C), 1.0, 6.0, ((0, 32), (1, 8))),
    }


def as_taps(kernel):
    return jnp.transpose(kernel, (1, 2, 3, 4, 0))

def conv_same(field, kernel):
    return lax.conv_general_dilated(field[None].astype(jnp.float32), as_taps(kernel).astype(jnp.float32), (1, 1, 1), ((1, 1), (1, 1), (1, 1)), dimension_numbers=('NDHWC', 'DHWIO', 'NDHWC'), precision=lax.Precision.HIGHEST)[0]

def conv_down(field, kernel):
    return lax.conv_general_dilated(field[None].astype(jnp.float32), as_taps(kernel).astype(jnp.float32), (2, 2, 2), ((1, 0), (1, 0), (1, 0)), dimension_numbers=('NDHWC', 'DHWIO', 'NDHWC'), precision=lax.Precision.HIGHEST)[0]

def silu_slope(value):
    sig = jax.nn.sigmoid(value)
    return sig * (1.0 + value * (1.0 - sig))

def reference(activations, w_first, w_second, cotangent):
    first_pre = conv_same(activations, w_first)
    hidden = jax.nn.silu(first_pre).astype(jnp.bfloat16)
    second_pre = conv_down(hidden, w_second)
    section_out = jax.nn.silu(second_pre)
    second_err = (cotangent.astype(jnp.float32) * silu_slope(second_pre)).astype(jnp.bfloat16)
    unused_two, back_two = jax.vjp(conv_down, hidden.astype(jnp.float32), w_second.astype(jnp.float32))
    hidden_err, grad_second = back_two(second_err.astype(jnp.float32))
    first_err = (hidden_err * silu_slope(first_pre)).astype(jnp.bfloat16)
    unused_one, back_one = jax.vjp(conv_same, activations.astype(jnp.float32), w_first.astype(jnp.float32))
    grad_input, grad_first = back_one(first_err.astype(jnp.float32))
    return (section_out, grad_input, grad_first, grad_second)
```

```python
import jax
import jax.numpy as jnp
from jax import lax
from jax.experimental import pallas as pl
from jax.experimental.pallas import tpu as pltpu
from jax.sharding import Mesh
from jax.sharding import PartitionSpec as P

SP = ("sp_z", "sp_y", "core")
CHIPS = ("sp_z", "sp_y")
bf16, f32 = jnp.bfloat16, jnp.float32

ROWS = 256
X_ROWS, COT_ROWS, W_ROWS = 256, 32, 288
PACK = X_ROWS + COT_ROWS + W_ROWS
GRAD_ROWS, GRAD_PAD = 1728, 1792
NT = (((1,), (1,)), ((), ()))
NN = (((1,), (0,)), ((), ()))
TN = (((0,), (0,)), ((), ()))


def dot(a, b, dims):
    return lax.dot_general(a, b, dims, preferred_element_type=f32)


def kernel_call(body, outs, flops, *args, scratch=()):
    vmem = pl.BlockSpec(memory_space=pltpu.VMEM)
    moved = sum(a.size * a.dtype.itemsize for a in (*args, *outs))
    return pl.pallas_call(
        body,
        out_shape=outs,
        in_specs=[vmem] * len(args),
        out_specs=[vmem] * len(outs),
        scratch_shapes=scratch,
        compiler_params=pltpu.CompilerParams(vmem_limit_bytes=32 << 20),
        cost_estimate=pl.CostEstimate(flops=flops, bytes_accessed=moved, transcendentals=0),
    )(*args)


def shape(dims, dtype):
    return jax.ShapeDtypeStruct(dims, dtype)


def lanes(rows):
    return lax.broadcasted_iota(jnp.int32, (rows, 128), 1)


def cells(rows):
    return lax.rem(lax.broadcasted_iota(jnp.int32, (rows, 128), 0), 8)


def before(v):
    return jnp.where(cells(v.shape[0]) == 0, 0.0, pltpu.roll(v, 1, 0))


def after(v):
    return jnp.where(cells(v.shape[0]) == 7, 0.0, pltpu.roll(v, v.shape[0] - 1, 0))


def rotated(v, slots):
    by = (32 * slots) % 128
    return pltpu.roll(v, by, 1) if by else v


def three(a, b, c):
    lane = lanes(a.shape[0])
    return jnp.where(lane < 32, a, jnp.where(lane < 64, b, jnp.where(lane < 96, c, 0.0)))


def row_down(v):
    return jnp.concatenate([jnp.zeros((8, v.shape[1]), v.dtype), v[:-8]], 0)


def row_up(v):
    return jnp.concatenate([v[8:], jnp.zeros((8, v.shape[1]), v.dtype)], 0)


def tap_sum(first, middle, last):
    lane = lanes(ROWS)
    t = jnp.where(lane < 32, first, jnp.where(lane < 64, middle, last))
    return t + rotated(t, -1) + rotated(t, -2)


def pair_of(pieces):
    lane = lanes(ROWS)
    v = pieces[0]
    for slot in (1, 2, 3):
        v = jnp.where(lane < 32 * slot, v, rotated(pieces[slot], slot))
    return v


def sigmoid(v):
    return jax.nn.sigmoid(v)


def silu_slope(v):
    s = sigmoid(v)
    return s * (1.0 + v * (1.0 - s))


def pack_inputs(x, w, cot, out):
    for f in range(8):
        for h in (0, 1):
            out[f, h * 128 : h * 128 + 128, :] = x[:, h * 128 : h * 128 + 128]
            at = X_ROWS + h * 16
            out[f, at : at + 16, :] = cot[:, h * 128 : h * 128 + 128]
    for k in range(9):
        for h in (0, 1):
            taps = [
                w[(3 * k + t) * 32 : (3 * k + t) * 32 + 32, h * 128 : h * 128 + 128].astype(f32)
                for t in range(3)
            ]
            for m in range(4):
                v = three(*(rotated(taps[t], t - m) for t in range(3)))
                at = X_ROWS + COT_ROWS + k * 32
                out[4 * h + m, at : at + 32, :] = v.astype(bf16)


def prepare_first(w, wide, tall):
    zero = jnp.zeros((32, 256), bf16)
    for k0 in range(3):
        for k1 in range(3):
            for t in range(4):
                at = ((k0 * 3 + k1) * 3 + t) * 32
                v = w[at : at + 32, :] if t < 3 else zero
                wide[k0 * 128 + t * 32 : k0 * 128 + t * 32 + 32, k1 * 256 : k1 * 256 + 256] = v
                row = (k0 * 3 + k1) * 128 + t * 32
                tall[row : row + 32, :] = v


def first_conv(got, wide, low, high, field, window):
    parts = {}
    for h in (0, 1):
        for p in (0, 1):
            blocks = ([], [])
            for g in range(8):
                at = h * 128 + p * 64
                v = got[g, at : at + 64, :].astype(f32).reshape(4, 2, 8, 128)
                for par in (0, 1):
                    blocks[par].append(v[:, par].reshape(32, 128))
            for par in (0, 1):
                parts[p, par, h] = jnp.concatenate(blocks[par], 0)
    for p in (0, 1):
        for h in (0, 1):
            even, odd = parts[p, 0, h], parts[p, 1, h]
            sources = ((row_down(odd), even, odd), (even, odd, row_up(even)))
            for par in (0, 1):
                at = (2 * p + par) * ROWS
                for k1 in range(3):
                    lane = k1 * 256 + h * 128
                    window[at : at + ROWS, lane : lane + 128] = sources[par][k1].astype(bf16)
                field[at : at + ROWS, h * 128 : h * 128 + 128] = sources[par][1].astype(bf16)
    sums = [dot(window[i * ROWS : i * ROWS + ROWS, :], wide[...], NT) for i in range(4)]
    pieces = []
    for plane in range(4):
        for par in (0, 1):
            terms = [
                sums[2 * p + par][:, k0 * 128 : k0 * 128 + 128]
                for p in (0, 1)
                for k0 in range(3)
                if p - k0 + 2 == plane
            ]
            v = terms[0] if len(terms) == 1 else terms[0] + terms[1]
            pieces.append(tap_sum(before(v), v, after(v)))
    low[...] = pair_of(pieces[:4])
    high[...] = pair_of(pieces[4:])


def gather_second(got, w2):
    for g in range(8):
        for k in range(9):
            at = X_ROWS + COT_ROWS + k * 32
            w2[g * 32 : g * 32 + 32, k * 128 : k * 128 + 128] = got[g, at : at + 32, :]


def at_first_plane():
    return sum(lax.axis_index(name) for name in SP) == 0


def without_edge(v):
    return jnp.where(jnp.logical_and(at_first_plane(), lanes(ROWS) < 64), 0.0, v)


def second_conv(low, high, below, above, w2, pre, window, out, full):
    pairs = [low[...] + below[...], high[...] + above[...]]
    pre[0:ROWS, :] = pairs[0]
    pre[ROWS:, :] = pairs[1]
    hidden = [v * sigmoid(v) for v in pairs]
    hidden[0] = without_edge(hidden[0])
    hidden = [v.astype(bf16).astype(f32) for v in hidden]
    shifted = [(before(v), v, after(v)) for v in hidden]
    for plane in range(3):
        pair = shifted[plane // 2]
        for par in (0, 1):
            slot = (plane % 2) * 2 + par
            v = three(*(rotated(pair[t], t - slot) for t in range(3)))
            at = (plane * 3 + 1 + par) * 128
            window[:, at : at + 128] = v.astype(bf16)
            if par:
                window[:, plane * 384 : plane * 384 + 128] = row_down(v).astype(bf16)
    total = dot(window[...], w2[...], NT)
    for h in (0, 1):
        full[h] = total[:, h * 128 : h * 128 + 128]
        v = full[h, pl.ds(0, 128, 2), :].astype(bf16)
        for g in range(8):
            out[g, :, h * 128 : h * 128 + 128] = v


def second_error(parts, got, section, err):
    for h in (0, 1):
        lane = slice(h * 128, h * 128 + 128)
        v = parts[0, :, lane].astype(f32)
        for g in range(1, 8):
            v = v + parts[g, :, lane].astype(f32)
        cot = jnp.concatenate(
            [got[g, X_ROWS + h * 16 : X_ROWS + h * 16 + 16, :].astype(f32) for g in range(8)], 0
        )
        section[:, lane] = v * sigmoid(v)
        err[:, lane] = (cot * silu_slope(v)).astype(bf16)


def spread_out(err, full):
    halves = []
    for h in (0, 1):
        full[h] = jnp.zeros((ROWS, 128), f32)
        full[h, pl.ds(0, 128, 2), :] = err[:, h * 128 : h * 128 + 128].astype(f32)
        halves.append(full[h])
    return jnp.concatenate(halves, 1)


def second_grad(err, window, out, full):
    spread = spread_out(err, full).astype(bf16)
    grad = dot(spread, window[...], TN)
    for g in range(8):
        for k in range(9):
            v = grad[g * 32 : g * 32 + 32, k * 128 : k * 128 + 128]
            out[g, k * 32 : k * 32 + 32, :] = v.astype(bf16)


def first_error(own, below, above, w2, pre, field, window, out, full):
    spread, ahead = [], []
    for err in (below, own, above):
        v = spread_out(err, full)
        spread.append(v.astype(bf16))
        ahead.append(row_up(v).astype(bf16))
    pieces = []
    for plane in range(4):
        both, extra = None, None
        for q, k0 in (((0, 2), (1, 0)), ((1, 1),), ((1, 2), (2, 0)), ((2, 1),))[plane]:
            at = k0 * 384
            a = dot(spread[q], w2[:, at + 128 : at + 384], NN)
            b = dot(ahead[q], w2[:, at : at + 128], NN)
            both = a if both is None else both + a
            extra = b if extra is None else extra + b
        for v in (both[:, :128], both[:, 128:] + extra):
            pieces.append(tap_sum(after(v), v, before(v)))
    errs = [pair_of(pieces[:4]), pair_of(pieces[4:])]
    errs = [errs[i] * silu_slope(pre[i * ROWS : i * ROWS + ROWS, :]) for i in (0, 1)]
    errs[0] = without_edge(errs[0])
    errs = [v.astype(bf16).astype(f32) for v in errs]
    shifted = [(after(v), v, before(v)) for v in errs]
    for plane in range(4):
        pair = shifted[plane // 2]
        taps = [
            three(*(rotated(pair[t], t - (plane % 2) * 2 - par) for t in range(3)))
            for par in (0, 1)
        ]
        even, odd = taps
        sources = ((odd, even, row_down(odd)), (row_up(even), odd, even))
        for par in (0, 1):
            for k1 in range(3):
                v = sources[par][k1].astype(bf16)
                for k0 in range(3):
                    target = plane + k0 - 1
                    if target in (1, 2):
                        at = (2 * (target - 1) + par) * ROWS
                        lane = (k0 * 3 + k1) * 128
                        window[at : at + ROWS, lane : lane + 128] = v
    grad = dot(window[...], field[...], TN)
    for h in (0, 1):
        for k in range(9):
            at = h * 864 + k * 96
            v = grad[k * 128 : k * 128 + 96, h * 128 : h * 128 + 128]
            out[at : at + 96, :] = v.astype(bf16)
    out[GRAD_ROWS:, :] = jnp.zeros((GRAD_PAD - GRAD_ROWS, 128), bf16)


def input_grad(window, tall, out):
    for p in (0, 1):
        even = dot(window[2 * p * ROWS : (2 * p + 1) * ROWS, :], tall[...], NN)
        odd = dot(window[(2 * p + 1) * ROWS : (2 * p + 2) * ROWS, :], tall[...], NN)
        for g in range(8):
            a = even[g * 32 : g * 32 + 32].reshape(4, 1, 8, 256)
            b = odd[g * 32 : g * 32 + 32].reshape(4, 1, 8, 256)
            v = jnp.concatenate([a, b], 1).reshape(64, 256)
            out[g, p * 64 : p * 64 + 64, :] = v.astype(bf16)


def split_grads(first, second, kept, sent):
    lane = lanes(32)
    core = lax.axis_index("core")

    def store(at, size, a, b):
        kept[at : at + size, :] = jnp.where(core == 0, a, b).astype(bf16)
        sent[at : at + size, :] = jnp.where(core == 0, b, a).astype(bf16)

    for h in (0, 1):
        for k in range(9):
            blocks = [second[4 * h + m, k * 32 : k * 32 + 32, :].astype(f32) for m in range(4)]
            for t in range(3):
                v = rotated(blocks[0], -t)
                for m in (1, 2, 3):
                    v = jnp.where(lane < 32 * m, v, rotated(blocks[m], m - t))
                at = h * 864 + (3 * k + t) * 32
                store(at, 32, first[at : at + 32, :].astype(f32), v)
    kept[GRAD_ROWS:, :] = jnp.zeros((GRAD_PAD - GRAD_ROWS, 128), bf16)
    sent[GRAD_ROWS:, :] = jnp.zeros((GRAD_PAD - GRAD_ROWS, 128), bf16)


def add_core(kept, came, out):
    v = kept[...].astype(f32) + came[...].astype(f32)
    out[...] = v.astype(bf16).reshape(16, GRAD_PAD // 16, 128)


def add_chips(parts, out):
    v = parts[0].astype(f32)
    for i in range(1, 16):
        v = v + parts[i].astype(f32)
    v = v.astype(bf16)
    for i in range(16):
        out[i] = v


def finish_grads(own, other, first, second):
    core = lax.axis_index("core")
    for h in (0, 1):
        lane = slice(h * 128, h * 128 + 128)
        a = own[h * 864 : h * 864 + 864, :].astype(f32)
        b = other[h * 864 : h * 864 + 864, :].astype(f32)
        first[:, lane] = jnp.where(core == 0, a, b)
        second[:, lane] = jnp.where(core == 0, b, a)


def add_parts(parts, out):
    v = parts[0].astype(f32)
    for g in range(1, 8):
        v = v + parts[g].astype(f32)
    out[...] = v


def exchange(v, axis):
    return lax.all_to_all(v, axis, 0, 0, tiled=True)


def upward(v):
    n = lax.axis_size(SP)
    return lax.ppermute(v, SP, [(i, i + 1) for i in range(n - 1)])


def downward(v):
    n = lax.axis_size(SP)
    return lax.ppermute(v, SP, [(i + 1, i) for i in range(n - 1)])


def swapped(v):
    return lax.ppermute(v, "core", [(0, 1), (1, 0)])


def as_rows(w):
    return jnp.transpose(w, (1, 2, 3, 0, 4)).reshape(864, 256)


def as_filters(rows):
    return jnp.transpose(rows.reshape(3, 3, 3, 32, 256), (3, 0, 1, 2, 4))


def per_device(activations, w_first, w_second, cotangent):
    spread_scratch = [pltpu.VMEM((2, ROWS, 128), f32)]
    wide, tall = kernel_call(
        prepare_first, [shape((384, 768), bf16), shape((1152, 256), bf16)], 0, as_rows(w_first)
    )
    (packed,) = kernel_call(
        pack_inputs,
        [shape((8, PACK, 128), bf16)],
        0,
        activations.reshape(128, 256),
        as_rows(w_second),
        cotangent.reshape(16, 256),
    )
    got = exchange(packed, "flt")
    low, high, field = kernel_call(
        first_conv,
        [shape((ROWS, 128), f32), shape((ROWS, 128), f32), shape((1024, 256), bf16)],
        2 * 1024 * 768 * 384,
        got,
        wide,
        scratch=[pltpu.VMEM((1024, 768), bf16)],
    )
    below, above = upward(high), downward(low)
    (w2,) = kernel_call(gather_second, [shape((256, 1152), bf16)], 0, got)
    pre, hidden_window, partial = kernel_call(
        second_conv,
        [shape((512, 128), f32), shape((ROWS, 1152), bf16), shape((8, 128, 256), bf16)],
        2 * 256 * 1152 * 256,
        low,
        high,
        below,
        above,
        w2,
        scratch=spread_scratch,
    )
    parts = exchange(partial, "flt")
    section, err = kernel_call(
        second_error, [shape((128, 256), f32), shape((128, 256), bf16)], 0, parts, got
    )
    err_below, err_above = upward(err), downward(err)
    (grad_second,) = kernel_call(
        second_grad,
        [shape((8, 288, 128), bf16)],
        2 * 256 * 1152 * 256,
        err,
        hidden_window,
        scratch=spread_scratch,
    )
    grad_second = exchange(grad_second, "flt")
    window, grad_first = kernel_call(
        first_error,
        [shape((1024, 1152), bf16), shape((GRAD_PAD, 128), bf16)],
        2 * 1024 * 1152 * 256 + 2 * 256 * 256 * 384 * 6,
        err,
        err_below,
        err_above,
        w2,
        pre,
        field,
        scratch=spread_scratch,
    )
    kept, sent = kernel_call(
        split_grads, [shape((GRAD_PAD, 128), bf16)] * 2, 0, grad_first, grad_second
    )
    came = swapped(sent)
    (inner,) = kernel_call(
        input_grad, [shape((8, 128, 256), bf16)], 2 * 1024 * 1152 * 256, window, tall
    )
    chunk = shape((16, GRAD_PAD // 16, 128), bf16)
    (mine,) = kernel_call(add_core, [chunk], 0, kept, came)
    (mine,) = kernel_call(add_chips, [chunk], 0, exchange(mine, CHIPS))
    inner = exchange(inner, "flt")
    mine = exchange(mine, CHIPS).reshape(GRAD_PAD, 128)
    grads = kernel_call(
        finish_grads, [shape((864, 256), f32)] * 2, 0, mine, swapped(mine)
    )
    (grad_input,) = kernel_call(add_parts, [shape((128, 256), f32)], 0, inner)
    row = lax.axis_index("flt") * 16
    section_out = lax.dynamic_slice_in_dim(section, row, 16, 0).reshape(1, 4, 4, 256)
    return (section_out, grad_input.reshape(2, 8, 8, 256), *(as_filters(g) for g in grads))


def solution(mesh):
    torus = Mesh(mesh.devices.reshape(8, 2, 2, mesh.shape["flt"]), (*SP, "flt"))
    whole = P("flt", None, None, None, None)
    rows = P(SP, "flt", None, None)
    return jax.shard_map(
        per_device,
        mesh=torus,
        in_specs=(rows, whole, whole, rows),
        out_specs=(rows, rows, whole, whole),
        check_vma=False,
    )
```

```python
import jax
import jax.numpy as jnp
from jax import lax
from jax.experimental import pallas as pl
from jax.experimental.pallas import tpu as pltpu
from jax.sharding import Mesh
from jax.sharding import PartitionSpec as P

SP = ("sp_z", "sp_y", "core")
CHIPS = ("sp_z", "sp_y")
FLT = ("flt_x", "flt_y")
bf16, f32 = jnp.bfloat16, jnp.float32

ROWS = 256
X_ROWS, COT_ROWS, W_ROWS = 256, 32, 288
PACK = X_ROWS + COT_ROWS + W_ROWS
GRAD_ROWS, GRAD_PAD = 1728, 1792
NT = (((1,), (1,)), ((), ()))
NN = (((1,), (0,)), ((), ()))
TN = (((0,), (0,)), ((), ()))


def dot(a, b, dims):
    return lax.dot_general(a, b, dims, preferred_element_type=f32)


def kernel_call(body, outs, flops, *args, scratch=(), space=pltpu.VMEM, limit=16):
    vmem = pl.BlockSpec(memory_space=pltpu.VMEM)
    moved = sum(a.size * a.dtype.itemsize for a in (*args, *outs))
    return pl.pallas_call(
        body,
        out_shape=outs,
        in_specs=[pl.BlockSpec(memory_space=space)] * len(args),
        out_specs=[vmem] * len(outs),
        scratch_shapes=scratch,
        compiler_params=pltpu.CompilerParams(vmem_limit_bytes=limit << 20),
        cost_estimate=pl.CostEstimate(flops=flops, bytes_accessed=moved, transcendentals=0),
    )(*args)


def shape(dims, dtype):
    return jax.ShapeDtypeStruct(dims, dtype)


def lanes(rows):
    return lax.broadcasted_iota(jnp.int32, (rows, 128), 1)


def cells(rows):
    return lax.rem(lax.broadcasted_iota(jnp.int32, (rows, 128), 0), 8)


def before(v):
    return jnp.where(cells(v.shape[0]) == 0, 0.0, pltpu.roll(v, 1, 0))


def after(v):
    return jnp.where(cells(v.shape[0]) == 7, 0.0, pltpu.roll(v, v.shape[0] - 1, 0))


def rotated(v, slots):
    by = (32 * slots) % 128
    return pltpu.roll(v, by, 1) if by else v


def three(a, b, c):
    lane = lanes(a.shape[0])
    return jnp.where(lane < 32, a, jnp.where(lane < 64, b, jnp.where(lane < 96, c, 0.0)))


def row_down(v):
    return jnp.concatenate([jnp.zeros((8, v.shape[1]), v.dtype), v[:-8]], 0)


def row_up(v):
    return jnp.concatenate([v[8:], jnp.zeros((8, v.shape[1]), v.dtype)], 0)


def tap_sum(first, middle, last):
    lane = lanes(ROWS)
    t = jnp.where(lane < 32, first, jnp.where(lane < 64, middle, last))
    return t + rotated(t, -1) + rotated(t, -2)


def pair_of(pieces):
    lane = lanes(ROWS)
    v = pieces[0]
    for slot in (1, 2, 3):
        v = jnp.where(lane < 32 * slot, v, rotated(pieces[slot], slot))
    return v


def sigmoid(v):
    return jax.nn.sigmoid(v)


def silu_slope(v):
    s = sigmoid(v)
    return s * (1.0 + v * (1.0 - s))


def pack_inputs(x_far, w_far, cot_far, out, x, w, cot_near, sems):
    copies = [
        pltpu.make_async_copy(far, near, sems.at[i])
        for i, (far, near) in enumerate(((x_far, x), (cot_far, cot_near), (w_far, w)))
    ]
    for copy in copies:
        copy.start()
    copies[0].wait()
    copies[1].wait()
    cot = jnp.concatenate([cot_near[0, i].astype(f32) for i in range(4)], 0).astype(bf16)
    for f in range(8):
        for h in (0, 1):
            out[f, h * 128 : h * 128 + 128, :] = x[:, h * 128 : h * 128 + 128]
            at = X_ROWS + h * 16
            out[f, at : at + 16, :] = cot[:, h * 128 : h * 128 + 128]
    copies[2].wait()
    for k in range(9):
        for h in (0, 1):
            taps = [
                w[(3 * k + t) * 32 : (3 * k + t) * 32 + 32, h * 128 : h * 128 + 128].astype(f32)
                for t in range(3)
            ]
            for m in range(4):
                v = three(*(rotated(taps[t], t - m) for t in range(3)))
                at = X_ROWS + COT_ROWS + k * 32
                out[4 * h + m, at : at + 32, :] = v.astype(bf16)


def prepare_first(w, wide, tall):
    zero = jnp.zeros((32, 256), bf16)
    for k0 in range(3):
        for k1 in range(3):
            for t in range(4):
                at = ((k0 * 3 + k1) * 3 + t) * 32
                v = w[at : at + 32, :] if t < 3 else zero
                wide[k0 * 128 + t * 32 : k0 * 128 + t * 32 + 32, k1 * 256 : k1 * 256 + 256] = v
                row = (k0 * 3 + k1) * 128 + t * 32
                tall[row : row + 32, :] = v


def first_conv(got, wide, low, high, within, across, field, window):
    parts = {}
    for h in (0, 1):
        for p in (0, 1):
            blocks = ([], [])
            for g in range(8):
                at = h * 128 + p * 64
                v = got[g, at : at + 64, :].astype(f32).reshape(4, 2, 8, 128)
                for par in (0, 1):
                    blocks[par].append(v[:, par].reshape(32, 128))
            for par in (0, 1):
                parts[p, par, h] = jnp.concatenate(blocks[par], 0)
    for p in (0, 1):
        for h in (0, 1):
            even, odd = parts[p, 0, h], parts[p, 1, h]
            sources = ((row_down(odd), even, odd), (even, odd, row_up(even)))
            for par in (0, 1):
                at = (2 * p + par) * ROWS
                for k1 in range(3):
                    lane = k1 * 256 + h * 128
                    window[at : at + ROWS, lane : lane + 128] = sources[par][k1].astype(bf16)
                field[at : at + ROWS, h * 128 : h * 128 + 128] = sources[par][1].astype(bf16)
    sums = [dot(window[i * ROWS : i * ROWS + ROWS, :], wide[...], NT) for i in range(4)]
    pieces = []
    for plane in range(4):
        for par in (0, 1):
            terms = [
                sums[2 * p + par][:, k0 * 128 : k0 * 128 + 128]
                for p in (0, 1)
                for k0 in range(3)
                if p - k0 + 2 == plane
            ]
            v = terms[0] if len(terms) == 1 else terms[0] + terms[1]
            pieces.append(tap_sum(before(v), v, after(v)))
    a, b = pair_of(pieces[:4]), pair_of(pieces[4:])
    first_core = lax.axis_index("core") == 0
    low[...] = a
    high[...] = b
    within[...] = jnp.where(first_core, b, a)
    across[...] = jnp.where(first_core, a, b)


def gather_second(got, w2):
    for g in range(8):
        for k in range(9):
            at = X_ROWS + COT_ROWS + k * 32
            w2[g * 32 : g * 32 + 32, k * 128 : k * 128 + 128] = got[g, at : at + 32, :]


def at_first_plane():
    return sum(lax.axis_index(name) for name in SP) == 0


def without_edge(v):
    return jnp.where(jnp.logical_and(at_first_plane(), lanes(ROWS) < 64), 0.0, v)


def below_above(within, across):
    first_core = lax.axis_index("core") == 0
    a, b = within[...], across[...]
    return jnp.where(first_core, b, a), jnp.where(first_core, a, b)


def second_conv(low, high, within, across, w2, pre, out, window, full):
    below, above = below_above(within, across)
    pairs = [low[...] + below, high[...] + above]
    pre[0:ROWS, :] = pairs[0]
    pre[ROWS:, :] = pairs[1]
    hidden = [v * sigmoid(v) for v in pairs]
    own = jnp.where(lanes(ROWS) < 64, rotated(hidden[0], 2), rotated(hidden[1], 2)).astype(bf16)
    for g in range(8):
        out[g, ROWS:, :] = own
    hidden[0] = without_edge(hidden[0])
    hidden = [v.astype(bf16).astype(f32) for v in hidden]
    shifted = [(before(v), v, after(v)) for v in hidden]
    for plane in range(3):
        pair = shifted[plane // 2]
        for par in (0, 1):
            slot = (plane % 2) * 2 + par
            v = three(*(rotated(pair[t], t - slot) for t in range(3)))
            at = (plane * 3 + 1 + par) * 128
            window[:, at : at + 128] = v.astype(bf16)
            if par:
                window[:, plane * 384 : plane * 384 + 128] = row_down(v).astype(bf16)
    total = dot(window[...], w2[...], NT)
    for h in (0, 1):
        full[h] = total[:, h * 128 : h * 128 + 128]
        v = full[h, pl.ds(0, 128, 2), :].astype(bf16)
        for g in range(8):
            out[g, h * 128 : h * 128 + 128, :] = v


def gather_hidden(parts, field):
    lane = lanes(ROWS)
    for h in (0, 1):
        blocks = [parts[4 * h + m, ROWS:, :].astype(f32) for m in range(4)]
        for slot in range(4):
            v = rotated(blocks[0], -slot)
            for m in (1, 2, 3):
                v = jnp.where(lane < 32 * m, v, rotated(blocks[m], m - slot))
            field[slot * ROWS : slot * ROWS + ROWS, h * 128 : h * 128 + 128] = v.astype(bf16)


def second_error(parts, got, section, err):
    for h in (0, 1):
        lane = slice(h * 128, h * 128 + 128)
        row = slice(h * 128, h * 128 + 128)
        v = parts[0, row, :].astype(f32)
        for g in range(1, 8):
            v = v + parts[g, row, :].astype(f32)
        cot = jnp.concatenate(
            [got[g, X_ROWS + h * 16 : X_ROWS + h * 16 + 16, :].astype(f32) for g in range(8)], 0
        )
        section[:, lane] = v * sigmoid(v)
        err[:, lane] = (cot * silu_slope(v)).astype(bf16)


def spread_out(err, full):
    full[...] = jnp.zeros((ROWS, 128), f32)
    full[pl.ds(0, 128, 2), :] = err
    return full[...]


def second_grad(spread, hidden):
    flt = lax.axis_index("flt_x") * 2 + lax.axis_index("flt_y")
    turn = lax.rem(8 - flt, 4) * 32
    plain, ahead = [], []
    for left, right in spread:
        v = pltpu.roll(jnp.where(flt < 4, left, right), turn, 1)
        v = three(after(v), rotated(v, 1), rotated(before(v), 2))
        plain.append(v.astype(bf16))
        ahead.append(row_up(v).astype(bf16))
    grads = []
    for k0 in range(3):
        q = 1 if k0 == 0 else 0
        for k1 in range(3):
            at = ((1 if k0 == 1 else 3) - (1 if k1 == 1 else 0)) * ROWS
            errs = (ahead if k1 == 0 else plain)[q]
            grads.append(dot(errs, hidden[at : at + ROWS, :], TN))
    return grads


def backward(own, within, across, w2, pre, field, hidden, window, kept, sent, full):
    below, above = below_above(within, across)
    spread, ahead, halves = [], [], []
    for err in (below, own[...], above):
        both = [spread_out(err[:, h * 128 : h * 128 + 128].astype(f32), full) for h in (0, 1)]
        halves.append(both)
        v = jnp.concatenate(both, 1)
        spread.append(v.astype(bf16))
        ahead.append(row_up(v).astype(bf16))
    pieces = []
    for plane in range(4):
        both, extra = None, None
        for q, k0 in (((0, 2), (1, 0)), ((1, 1),), ((1, 2), (2, 0)), ((2, 1),))[plane]:
            at = k0 * 384
            a = dot(spread[q], w2[:, at + 128 : at + 384], NN)
            b = dot(ahead[q], w2[:, at : at + 128], NN)
            both = a if both is None else both + a
            extra = b if extra is None else extra + b
        for v in (both[:, :128], both[:, 128:] + extra):
            pieces.append(tap_sum(after(v), v, before(v)))
    errs = [pair_of(pieces[:4]), pair_of(pieces[4:])]
    errs = [errs[i] * silu_slope(pre[i * ROWS : i * ROWS + ROWS, :]) for i in (0, 1)]
    errs[0] = without_edge(errs[0])
    errs = [v.astype(bf16).astype(f32) for v in errs]
    shifted = [(after(v), v, before(v)) for v in errs]
    for plane in range(4):
        pair = shifted[plane // 2]
        taps = [
            three(*(rotated(pair[t], t - (plane % 2) * 2 - par) for t in range(3)))
            for par in (0, 1)
        ]
        even, odd = taps
        sources = ((odd, even, row_down(odd)), (row_up(even), odd, even))
        for par in (0, 1):
            for k1 in range(3):
                v = sources[par][k1].astype(bf16)
                for k0 in range(3):
                    target = plane + k0 - 1
                    if target in (1, 2):
                        at = (2 * (target - 1) + par) * ROWS
                        lane = (k0 * 3 + k1) * 128
                        window[at : at + ROWS, lane : lane + 128] = v
    first = dot(window[...], field[...], TN)
    second = second_grad(halves[1:], hidden)
    first_core = lax.axis_index("core") == 0
    for h in (0, 1):
        lane = slice(h * 128, h * 128 + 128)
        for k in range(9):
            at = h * 864 + k * 96
            a, b = first[k * 128 : k * 128 + 96, lane], second[k][:96, lane]
            kept[at : at + 96, :] = jnp.where(first_core, a, b)
            sent[at : at + 96, :] = jnp.where(first_core, b, a).astype(bf16)
    kept[GRAD_ROWS:, :] = jnp.zeros((GRAD_PAD - GRAD_ROWS, 128), f32)
    sent[GRAD_ROWS:, :] = jnp.zeros((GRAD_PAD - GRAD_ROWS, 128), bf16)


def input_grad(window, tall, kept, sent):
    near = lax.axis_index("flt_y") == 0
    for p in (0, 1):
        even = dot(window[2 * p * ROWS : (2 * p + 1) * ROWS, :], tall[...], NN)
        odd = dot(window[(2 * p + 1) * ROWS : (2 * p + 2) * ROWS, :], tall[...], NN)
        blocks = []
        for g in range(8):
            a = even[g * 32 : g * 32 + 32].reshape(4, 1, 8, 256)
            b = odd[g * 32 : g * 32 + 32].reshape(4, 1, 8, 256)
            blocks.append(jnp.concatenate([a, b], 1).reshape(64, 256))
        row = slice(p * 64, p * 64 + 64)
        for x in range(4):
            a, b = blocks[2 * x], blocks[2 * x + 1]
            kept[x, row, :] = jnp.where(near, a, b)
            sent[x, row, :] = jnp.where(near, b, a).astype(bf16)


def add_second_axis(kept, came, still, sent):
    x = lax.axis_index("flt_x")
    still[0] = kept[x] + came[x].astype(f32)
    still[1] = kept[3 - x] + came[3 - x].astype(f32)
    next_to = x + 1 - 2 * lax.rem(x, 2)
    sent[0] = (kept[next_to] + came[next_to].astype(f32)).astype(bf16)
    sent[1] = (kept[3 - next_to] + came[3 - next_to].astype(f32)).astype(bf16)


def add_pairs(kept, came, still, sent):
    still[...] = kept[0] + came[0].astype(f32)
    sent[...] = (kept[1] + came[1].astype(f32)).astype(bf16)


def add_last(kept, came, out):
    out[...] = kept[...] + came[...].astype(f32)


def add_core(kept, came, out):
    v = kept[...] + came[...].astype(f32)
    out[...] = v.astype(bf16).reshape(16, GRAD_PAD // 16, 128)


def add_chips(parts, out):
    v = parts[0].astype(f32)
    for i in range(1, 16):
        v = v + parts[i].astype(f32)
    v = v.astype(bf16)
    for i in range(16):
        out[i] = v


def finish_grads(own, other, first, second):
    core = lax.axis_index("core")
    for h in (0, 1):
        lane = slice(h * 128, h * 128 + 128)
        a = own[h * 864 : h * 864 + 864, :].astype(f32)
        b = other[h * 864 : h * 864 + 864, :].astype(f32)
        first[:, lane] = jnp.where(core == 0, a, b)
        second[:, lane] = jnp.where(core == 0, b, a)


def exchange(v, axis):
    return lax.all_to_all(v, axis, 0, 0, tiled=True)


def swapped(v, axis="core"):
    n = lax.axis_size(axis)
    return lax.ppermute(v, axis, [(i, i ^ 1) for i in range(n)])


def mirrored(v, axis):
    n = lax.axis_size(axis)
    return lax.ppermute(v, axis, [(i, n - 1 - i) for i in range(n)])


def next_chip(v):
    pairs = [(i, i + 1) for i in range(1, lax.axis_size(SP) - 1, 2)]
    return lax.ppermute(v, SP, pairs + [(b, a) for a, b in pairs])


def as_rows(w):
    return jnp.transpose(w, (1, 2, 3, 0, 4)).reshape(864, 256)


def as_filters(rows):
    return jnp.transpose(rows.reshape(3, 3, 3, 32, 256), (3, 0, 1, 2, 4))


def per_device(activations, w_first, w_second, cotangent):
    wide, tall = kernel_call(
        prepare_first, [shape((384, 768), bf16), shape((1152, 256), bf16)], 0, as_rows(w_first)
    )
    (packed,) = kernel_call(
        pack_inputs,
        [shape((8, PACK, 128), bf16)],
        0,
        activations.reshape(128, 256),
        as_rows(w_second),
        cotangent,
        scratch=[
            pltpu.VMEM((128, 256), bf16),
            pltpu.VMEM((864, 256), bf16),
            pltpu.VMEM((1, 4, 4, 256), bf16),
            pltpu.SemaphoreType.DMA((3,)),
        ],
        space=pltpu.HBM,
        limit=60,
    )
    got = exchange(packed, FLT)
    pair = shape((ROWS, 128), f32)
    low, high, within, across, field = kernel_call(
        first_conv,
        [pair, pair, pair, pair, shape((1024, 256), bf16)],
        2 * 1024 * 768 * 384,
        got,
        wide,
        scratch=[pltpu.VMEM((1024, 768), bf16)],
    )
    across, within = next_chip(across), swapped(within)
    (w2,) = kernel_call(gather_second, [shape((256, 1152), bf16)], 0, got)
    pre, partial = kernel_call(
        second_conv,
        [shape((512, 128), f32), shape((8, 512, 128), bf16)],
        2 * 256 * 1152 * 256,
        low,
        high,
        within,
        across,
        w2,
        scratch=[pltpu.VMEM((ROWS, 1152), bf16), pltpu.VMEM((2, ROWS, 128), f32)],
    )
    parts = exchange(partial, FLT)
    section, err = kernel_call(
        second_error, [shape((128, 256), f32), shape((128, 256), bf16)], 0, parts, got
    )
    across, within = next_chip(err), swapped(err)
    (hidden,) = kernel_call(gather_hidden, [shape((1024, 256), bf16)], 0, parts)
    window, kept, sent = kernel_call(
        backward,
        [shape((1024, 1152), bf16), shape((GRAD_PAD, 128), f32), shape((GRAD_PAD, 128), bf16)],
        2 * 1024 * 1152 * 256 + 2 * 256 * 256 * 384 * 6,
        err,
        within,
        across,
        w2,
        pre,
        field,
        hidden,
        scratch=[pltpu.VMEM((ROWS, 128), f32)],
    )
    came = swapped(sent)
    kept_in, sent_in = kernel_call(
        input_grad,
        [shape((4, 128, 256), f32), shape((4, 128, 256), bf16)],
        2 * 1024 * 1152 * 256,
        window,
        tall,
    )
    chunk = shape((16, GRAD_PAD // 16, 128), bf16)
    (mine,) = kernel_call(add_core, [chunk], 0, kept, came)
    mine, sent_in = lax.optimization_barrier((mine, sent_in))
    came_in = swapped(sent_in, "flt_y")
    (mine,) = kernel_call(add_chips, [chunk], 0, exchange(mine, CHIPS))
    kept_in, sent_in = kernel_call(
        add_second_axis,
        [shape((2, 128, 256), f32), shape((2, 128, 256), bf16)],
        0,
        kept_in,
        came_in,
    )
    mine, sent_in = lax.optimization_barrier((mine, sent_in))
    came_in = swapped(sent_in, "flt_x")
    mine = exchange(mine, CHIPS).reshape(GRAD_PAD, 128)
    kept_in, sent_in = kernel_call(
        add_pairs, [shape((128, 256), f32), shape((128, 256), bf16)], 0, kept_in, came_in
    )
    came_in = mirrored(sent_in, "flt_x")
    (grad_input,) = kernel_call(add_last, [shape((128, 256), f32)], 0, kept_in, came_in)
    mine, grad_input = lax.optimization_barrier((mine, grad_input))
    grads = kernel_call(
        finish_grads, [shape((864, 256), f32)] * 2, 0, mine, swapped(mine)
    )
    row = lax.axis_index(FLT) * 16
    section_out = lax.dynamic_slice_in_dim(section, row, 16, 0).reshape(1, 4, 4, 256)
    return (section_out, grad_input.reshape(2, 8, 8, 256), *(as_filters(g) for g in grads))


def solution(mesh):
    torus = Mesh(mesh.devices.reshape(8, 2, 2, 4, 2), (*SP, *FLT))
    whole = P(FLT, None, None, None, None)
    rows = P(SP, FLT, None, None)
    return jax.shard_map(
        per_device,
        mesh=torus,
        in_specs=(rows, whole, whole, rows),
        out_specs=(rows, rows, whole, whole),
        check_vma=False,
    )
```

```python
import jax
import jax.numpy as jnp
from jax import lax
from jax.experimental import pallas as pl
from jax.experimental.pallas import tpu as pltpu
from jax.sharding import Mesh
from jax.sharding import PartitionSpec as P

SP = ("sp_z", "sp_y", "core")
CHIPS = ("sp_z", "sp_y")
FLT = ("flt_x", "flt_y")
bf16, f32 = jnp.bfloat16, jnp.float32

ROWS = 256
X_ROWS, COT_ROWS, W_ROWS = 256, 32, 128
PACK = X_ROWS + COT_ROWS + W_ROWS
GRAD_ROWS, GRAD_PAD = 1728, 1792
NT = (((1,), (1,)), ((), ()))
NN = (((1,), (0,)), ((), ()))
TN = (((0,), (0,)), ((), ()))


def dot(a, b, dims):
    return lax.dot_general(a, b, dims, preferred_element_type=f32)


def kernel_call(body, outs, flops, *args, scratch=(), space=pltpu.VMEM, target=pltpu.VMEM, limit=16):
    moved = sum(a.size * a.dtype.itemsize for a in (*args, *outs))
    return pl.pallas_call(
        body,
        out_shape=outs,
        in_specs=[pl.BlockSpec(memory_space=space)] * len(args),
        out_specs=[pl.BlockSpec(memory_space=target)] * len(outs),
        scratch_shapes=scratch,
        compiler_params=pltpu.CompilerParams(vmem_limit_bytes=limit << 20),
        cost_estimate=pl.CostEstimate(flops=flops, bytes_accessed=moved, transcendentals=0),
    )(*args)


def shape(dims, dtype):
    return jax.ShapeDtypeStruct(dims, dtype)


def lanes(rows):
    return lax.broadcasted_iota(jnp.int32, (rows, 128), 1)


def cells(rows):
    return lax.rem(lax.broadcasted_iota(jnp.int32, (rows, 128), 0), 8)


def before(v):
    return jnp.where(cells(v.shape[0]) == 0, 0.0, pltpu.roll(v, 1, 0))


def after(v):
    return jnp.where(cells(v.shape[0]) == 7, 0.0, pltpu.roll(v, v.shape[0] - 1, 0))


def rotated(v, slots):
    by = (32 * slots) % 128
    return pltpu.roll(v, by, 1) if by else v


def three(a, b, c):
    lane = lanes(a.shape[0])
    return jnp.where(lane < 32, a, jnp.where(lane < 64, b, jnp.where(lane < 96, c, 0.0)))


def row_down(v):
    return jnp.concatenate([jnp.zeros((8, v.shape[1]), v.dtype), v[:-8]], 0)


def row_up(v):
    return jnp.concatenate([v[8:], jnp.zeros((8, v.shape[1]), v.dtype)], 0)


def tap_sum(first, middle, last):
    lane = lanes(ROWS)
    t = jnp.where(lane < 32, first, jnp.where(lane < 64, middle, last))
    return t + rotated(t, -1) + rotated(t, -2)


def pair_of(pieces):
    lane = lanes(ROWS)
    v = pieces[0]
    for slot in (1, 2, 3):
        v = jnp.where(lane < 32 * slot, v, rotated(pieces[slot], slot))
    return v


def sigmoid(v):
    return jax.nn.sigmoid(v)


def silu_slope(v):
    s = sigmoid(v)
    return s * (1.0 + v * (1.0 - s))


def pack_inputs(x_far, w_far, cot_far, out, x, w, cot_near, sems):
    copies = [
        pltpu.make_async_copy(far, near, sems.at[i])
        for i, (far, near) in enumerate(((x_far, x), (cot_far, cot_near), (w_far, w)))
    ]
    for copy in copies:
        copy.start()
    copies[0].wait()
    copies[1].wait()
    cot = jnp.concatenate([cot_near[0, i].astype(f32) for i in range(4)], 0).astype(bf16)
    for f in range(8):
        for h in (0, 1):
            out[f, h * 128 : h * 128 + 128, :] = x[:, h * 128 : h * 128 + 128]
            at = X_ROWS + h * 16
            out[f, at : at + 16, :] = cot[:, h * 128 : h * 128 + 128]
    copies[2].wait()
    first_core = lax.axis_index("core") == 0
    lane = lanes(32)

    def block(k, m, h):
        at = pl.multiple_of(96 * k, 32)
        taps = [w[pl.ds(at + 32 * t, 32), h * 128 : h * 128 + 128].astype(f32) for t in range(3)]
        return three(*(rotated(taps[t], t - m) for t in range(3)))

    for b in range(4):
        for h in (0, 1):
            extra = w[(12 + min(b, 2)) * 32 : (13 + min(b, 2)) * 32, h * 128 : h * 128 + 128]
            extra = extra.astype(f32)
            for m in range(4):
                v = block(jnp.where(first_core, b, b + 5), m, h)
                v = jnp.where(lane < 96, v, rotated(extra, 3 - m))
                at = X_ROWS + COT_ROWS + b * 32
                out[4 * h + m, at : at + 32, :] = v.astype(bf16)


def prepare_first(w, wide, tall):
    zero = jnp.zeros((32, 256), bf16)
    for k0 in range(3):
        for k1 in range(3):
            for t in range(4):
                at = ((k0 * 3 + k1) * 3 + t) * 32
                v = w[at : at + 32, :] if t < 3 else zero
                wide[k0 * 128 + t * 32 : k0 * 128 + t * 32 + 32, k1 * 256 : k1 * 256 + 256] = v
                row = (k0 * 3 + k1) * 128 + t * 32
                tall[row : row + 32, :] = v


def first_conv(got, wide, low, high, within, across, field, part, window):
    part[...] = got[:, X_ROWS + COT_ROWS :, :]
    parts = {}
    for h in (0, 1):
        for p in (0, 1):
            blocks = ([], [])
            for g in range(8):
                at = h * 128 + p * 64
                v = got[g, at : at + 64, :].astype(f32).reshape(4, 2, 8, 128)
                for par in (0, 1):
                    blocks[par].append(v[:, par].reshape(32, 128))
            for par in (0, 1):
                parts[p, par, h] = jnp.concatenate(blocks[par], 0)
    for p in (0, 1):
        for h in (0, 1):
            even, odd = parts[p, 0, h], parts[p, 1, h]
            sources = ((row_down(odd), even, odd), (even, odd, row_up(even)))
            for par in (0, 1):
                at = (2 * p + par) * ROWS
                for k1 in range(3):
                    lane = k1 * 256 + h * 128
                    window[at : at + ROWS, lane : lane + 128] = sources[par][k1].astype(bf16)
                field[at : at + ROWS, h * 128 : h * 128 + 128] = sources[par][1].astype(bf16)
    sums = [dot(window[i * ROWS : i * ROWS + ROWS, :], wide[...], NT) for i in range(4)]
    pieces = []
    for plane in range(4):
        for par in (0, 1):
            terms = [
                sums[2 * p + par][:, k0 * 128 : k0 * 128 + 128]
                for p in (0, 1)
                for k0 in range(3)
                if p - k0 + 2 == plane
            ]
            v = terms[0] if len(terms) == 1 else terms[0] + terms[1]
            pieces.append(tap_sum(before(v), v, after(v)))
    a, b = pair_of(pieces[:4]), pair_of(pieces[4:])
    first_core = lax.axis_index("core") == 0
    low[...] = a
    high[...] = b
    within[...] = jnp.where(first_core, b, a)
    across[...] = jnp.where(first_core, a, b)


def gather_second(own, other, w2):
    first_core = lax.axis_index("core") == 0
    for g in range(8):
        row = slice(g * 32, g * 32 + 32)
        blocks = []
        for b in range(4):
            at = slice(b * 32, b * 32 + 32)
            x, y = own[g, at, :].astype(f32), other[g, at, :].astype(f32)
            early, late = jnp.where(first_core, x, y), jnp.where(first_core, y, x)
            w2[row, b * 128 : b * 128 + 128] = early.astype(bf16)
            w2[row, (b + 5) * 128 : (b + 6) * 128] = late.astype(bf16)
            blocks.append(early)
        v = three(*(rotated(blocks[t], t - 3) for t in range(3)))
        w2[row, 512:640] = v.astype(bf16)


def at_first_plane():
    return sum(lax.axis_index(name) for name in SP) == 0


def without_edge(v):
    return jnp.where(jnp.logical_and(at_first_plane(), lanes(ROWS) < 64), 0.0, v)


def below_above(within, across):
    first_core = lax.axis_index("core") == 0
    a, b = within[...], across[...]
    return jnp.where(first_core, b, a), jnp.where(first_core, a, b)


def second_conv(low, high, within, across, w2, pre, out, window, full):
    below, above = below_above(within, across)
    pairs = [low[...] + below, high[...] + above]
    pre[0:ROWS, :] = pairs[0]
    pre[ROWS:, :] = pairs[1]
    hidden = [v * sigmoid(v) for v in pairs]
    own = jnp.where(lanes(ROWS) < 64, rotated(hidden[0], 2), rotated(hidden[1], 2)).astype(bf16)
    for g in range(8):
        out[g, ROWS:, :] = own
    hidden[0] = without_edge(hidden[0])
    hidden = [v.astype(bf16).astype(f32) for v in hidden]
    shifted = [(before(v), v, after(v)) for v in hidden]
    for plane in range(3):
        pair = shifted[plane // 2]
        for par in (0, 1):
            slot = (plane % 2) * 2 + par
            v = three(*(rotated(pair[t], t - slot) for t in range(3)))
            at = (plane * 3 + 1 + par) * 128
            window[:, at : at + 128] = v.astype(bf16)
            if par:
                window[:, plane * 384 : plane * 384 + 128] = row_down(v).astype(bf16)
    total = dot(window[...], w2[...], NT)
    for h in (0, 1):
        full[h] = total[:, h * 128 : h * 128 + 128]
        v = full[h, pl.ds(0, 128, 2), :].astype(bf16)
        for g in range(8):
            out[g, h * 128 : h * 128 + 128, :] = v


def gather_hidden(parts, field):
    lane = lanes(ROWS)
    for h in (0, 1):
        blocks = [parts[4 * h + m, ROWS:, :].astype(f32) for m in range(4)]
        for slot in range(4):
            v = rotated(blocks[0], -slot)
            for m in (1, 2, 3):
                v = jnp.where(lane < 32 * m, v, rotated(blocks[m], m - slot))
            field[slot * ROWS : slot * ROWS + ROWS, h * 128 : h * 128 + 128] = v.astype(bf16)


def second_error(parts, got, section, err):
    for h in (0, 1):
        lane = slice(h * 128, h * 128 + 128)
        row = slice(h * 128, h * 128 + 128)
        v = parts[0, row, :].astype(f32)
        for g in range(1, 8):
            v = v + parts[g, row, :].astype(f32)
        cot = jnp.concatenate(
            [got[g, X_ROWS + h * 16 : X_ROWS + h * 16 + 16, :].astype(f32) for g in range(8)], 0
        )
        section[:, lane] = v * sigmoid(v)
        err[:, lane] = (cot * silu_slope(v)).astype(bf16)


def spread_out(err, full):
    full[...] = jnp.zeros((ROWS, 128), f32)
    full[pl.ds(0, 128, 2), :] = err
    return full[...]


def second_grad(spread, hidden):
    flt = lax.axis_index("flt_x") * 2 + lax.axis_index("flt_y")
    turn = lax.rem(8 - flt, 4) * 32
    plain, ahead = [], []
    for left, right in spread:
        v = pltpu.roll(jnp.where(flt < 4, left, right), turn, 1)
        v = three(after(v), rotated(v, 1), rotated(before(v), 2))
        plain.append(v.astype(bf16))
        ahead.append(row_up(v).astype(bf16))
    grads = []
    for k0 in range(3):
        q = 1 if k0 == 0 else 0
        for k1 in range(3):
            at = ((1 if k0 == 1 else 3) - (1 if k1 == 1 else 0)) * ROWS
            errs = (ahead if k1 == 0 else plain)[q]
            grads.append(dot(errs, hidden[at : at + ROWS, :], TN))
    return grads


def backward(own, within, across, w2, pre, field, hidden, window, kept, sent, full):
    below, above = below_above(within, across)
    spread, ahead, halves = [], [], []
    for err in (below, own[...], above):
        both = [spread_out(err[:, h * 128 : h * 128 + 128].astype(f32), full) for h in (0, 1)]
        halves.append(both)
        v = jnp.concatenate(both, 1)
        spread.append(v.astype(bf16))
        ahead.append(row_up(v).astype(bf16))
    pieces = []
    for plane in range(4):
        both, extra = None, None
        for q, k0 in (((0, 2), (1, 0)), ((1, 1),), ((1, 2), (2, 0)), ((2, 1),))[plane]:
            at = k0 * 384
            a = dot(spread[q], w2[:, at + 128 : at + 384], NN)
            b = dot(ahead[q], w2[:, at : at + 128], NN)
            both = a if both is None else both + a
            extra = b if extra is None else extra + b
        for v in (both[:, :128], both[:, 128:] + extra):
            pieces.append(tap_sum(after(v), v, before(v)))
    errs = [pair_of(pieces[:4]), pair_of(pieces[4:])]
    errs = [errs[i] * silu_slope(pre[i * ROWS : i * ROWS + ROWS, :]) for i in (0, 1)]
    errs[0] = without_edge(errs[0])
    errs = [v.astype(bf16).astype(f32) for v in errs]
    shifted = [(after(v), v, before(v)) for v in errs]
    for plane in range(4):
        pair = shifted[plane // 2]
        taps = [
            three(*(rotated(pair[t], t - (plane % 2) * 2 - par) for t in range(3)))
            for par in (0, 1)
        ]
        even, odd = taps
        sources = ((odd, even, row_down(odd)), (row_up(even), odd, even))
        for par in (0, 1):
            for k1 in range(3):
                v = sources[par][k1].astype(bf16)
                for k0 in range(3):
                    target = plane + k0 - 1
                    if target in (1, 2):
                        at = (2 * (target - 1) + par) * ROWS
                        lane = (k0 * 3 + k1) * 128
                        window[at : at + ROWS, lane : lane + 128] = v
    first = dot(window[...], field[...], TN)
    second = second_grad(halves[1:], hidden)
    first_core = lax.axis_index("core") == 0
    for h in (0, 1):
        lane = slice(h * 128, h * 128 + 128)
        for k in range(9):
            at = h * 864 + k * 96
            a, b = first[k * 128 : k * 128 + 96, lane], second[k][:96, lane]
            kept[at : at + 96, :] = jnp.where(first_core, a, b)
            sent[at : at + 96, :] = jnp.where(first_core, b, a).astype(bf16)
    kept[GRAD_ROWS:, :] = jnp.zeros((GRAD_PAD - GRAD_ROWS, 128), f32)
    sent[GRAD_ROWS:, :] = jnp.zeros((GRAD_PAD - GRAD_ROWS, 128), bf16)


def input_grad(window, tall, kept, sent, blocks):
    for p in (0, 1):
        even = dot(window[2 * p * ROWS : (2 * p + 1) * ROWS, :], tall[...], NN)
        odd = dot(window[(2 * p + 1) * ROWS : (2 * p + 2) * ROWS, :], tall[...], NN)
        for g in range(8):
            a = even[g * 32 : g * 32 + 32].reshape(4, 1, 8, 256)
            b = odd[g * 32 : g * 32 + 32].reshape(4, 1, 8, 256)
            v = jnp.concatenate([a, b], 1).reshape(64, 256)
            blocks[g // 2, g % 2, p * 64 : p * 64 + 64, :] = v
    x = lax.axis_index("flt_x")
    partner = x + 1 - 2 * lax.rem(x, 2)
    kept[0] = blocks[x]
    kept[1] = blocks[3 - x]
    sent[0] = blocks[partner].astype(bf16)
    sent[1] = blocks[3 - partner].astype(bf16)


def add_pairs(kept, came, still, sent):
    still[...] = kept[0] + came[0].astype(f32)
    sent[...] = (kept[1] + came[1].astype(f32)).astype(bf16)


def add_halves(kept, came, still, sent):
    y = lax.axis_index("flt_y")
    still[...] = kept[y] + came[y].astype(f32)
    sent[...] = (kept[1 - y] + came[1 - y].astype(f32)).astype(bf16)


def add_last(kept, came, out):
    out[...] = kept[...] + came[...].astype(f32)


def add_core(kept, came, out):
    v = kept[...] + came[...].astype(f32)
    out[...] = v.astype(bf16).reshape(16, GRAD_PAD // 16, 128)


def add_chips(parts, out):
    v = parts[0].astype(f32)
    for i in range(1, 16):
        v = v + parts[i].astype(f32)
    v = v.astype(bf16)
    for i in range(16):
        out[i] = v


def finish_grads(own, other, first, second, near, sems):
    core = lax.axis_index("core")

    for i, source in enumerate((own, other)):
        for h in (0, 1):
            near[i, :, h * 128 : h * 128 + 128] = source[h * 864 : h * 864 + 864, :].astype(f32)
        for c in (0, 1):

            @pl.when(core == c)
            def _(i=i, c=c):
                target = first if i == c else second
                pltpu.make_async_copy(near.at[i], target, sems.at[i]).start()

    for c in (0, 1):

        @pl.when(core == c)
        def _(c=c):
            for i in (0, 1):
                target = first if i == c else second
                pltpu.make_async_copy(near.at[i], target, sems.at[i]).wait()


def exchange(v, axis):
    return lax.all_to_all(v, axis, 0, 0, tiled=True)


def swapped(v, axis="core"):
    n = lax.axis_size(axis)
    return lax.ppermute(v, axis, [(i, i ^ 1) for i in range(n)])


def mirrored(v, axis):
    n = lax.axis_size(axis)
    return lax.ppermute(v, axis, [(i, n - 1 - i) for i in range(n)])


def next_chip(v):
    pairs = [(i, i + 1) for i in range(1, lax.axis_size(SP) - 1, 2)]
    return lax.ppermute(v, SP, pairs + [(b, a) for a, b in pairs])


def as_rows(w):
    return jnp.transpose(w, (1, 2, 3, 0, 4)).reshape(864, 256)


def as_filters(rows):
    return jnp.transpose(rows.reshape(3, 3, 3, 32, 256), (3, 0, 1, 2, 4))


def per_device(activations, w_first, w_second, cotangent):
    wide, tall = kernel_call(
        prepare_first, [shape((384, 768), bf16), shape((1152, 256), bf16)], 0, as_rows(w_first)
    )
    (packed,) = kernel_call(
        pack_inputs,
        [shape((8, PACK, 128), bf16)],
        0,
        activations.reshape(128, 256),
        as_rows(w_second),
        cotangent,
        scratch=[
            pltpu.VMEM((128, 256), bf16),
            pltpu.VMEM((864, 256), bf16),
            pltpu.VMEM((1, 4, 4, 256), bf16),
            pltpu.SemaphoreType.DMA((3,)),
        ],
        space=pltpu.HBM,
        limit=60,
    )
    got = exchange(packed, FLT)
    pair = shape((ROWS, 128), f32)
    low, high, within, across, field, part = kernel_call(
        first_conv,
        [pair, pair, pair, pair, shape((1024, 256), bf16), shape((8, W_ROWS, 128), bf16)],
        2 * 1024 * 768 * 384,
        got,
        wide,
        scratch=[pltpu.VMEM((1024, 768), bf16)],
    )
    across, within = next_chip(across), swapped(within)
    (w2,) = kernel_call(gather_second, [shape((256, 1152), bf16)], 0, part, swapped(part))
    pre, partial = kernel_call(
        second_conv,
        [shape((512, 128), f32), shape((8, 512, 128), bf16)],
        2 * 256 * 1152 * 256,
        low,
        high,
        within,
        across,
        w2,
        scratch=[pltpu.VMEM((ROWS, 1152), bf16), pltpu.VMEM((2, ROWS, 128), f32)],
    )
    parts = exchange(partial, FLT)
    section, err = kernel_call(
        second_error, [shape((128, 256), f32), shape((128, 256), bf16)], 0, parts, got
    )
    across, within = next_chip(err), swapped(err)
    (hidden,) = kernel_call(gather_hidden, [shape((1024, 256), bf16)], 0, parts)
    window, kept, sent = kernel_call(
        backward,
        [shape((1024, 1152), bf16), shape((GRAD_PAD, 128), f32), shape((GRAD_PAD, 128), bf16)],
        2 * 1024 * 1152 * 256 + 2 * 256 * 256 * 384 * 6,
        err,
        within,
        across,
        w2,
        pre,
        field,
        hidden,
        scratch=[pltpu.VMEM((ROWS, 128), f32)],
    )
    came = swapped(sent)
    kept_in, sent_in = kernel_call(
        input_grad,
        [shape((2, 2, 128, 256), f32), shape((2, 2, 128, 256), bf16)],
        2 * 1024 * 1152 * 256,
        window,
        tall,
        scratch=[pltpu.VMEM((4, 2, 128, 256), f32)],
    )
    chunk = shape((16, GRAD_PAD // 16, 128), bf16)
    (mine,) = kernel_call(add_core, [chunk], 0, kept, came)
    mine, sent_in = lax.optimization_barrier((mine, sent_in))
    came_in = swapped(sent_in, "flt_x")
    (mine,) = kernel_call(add_chips, [chunk], 0, exchange(mine, CHIPS))
    kept_in, sent_in = kernel_call(
        add_pairs, [shape((2, 128, 256), f32), shape((2, 128, 256), bf16)], 0, kept_in, came_in
    )
    mine, sent_in = lax.optimization_barrier((mine, sent_in))
    came_in = mirrored(sent_in, "flt_x")
    mine = exchange(mine, CHIPS).reshape(GRAD_PAD, 128)
    kept_in, sent_in = kernel_call(
        add_halves, [shape((128, 256), f32), shape((128, 256), bf16)], 0, kept_in, came_in
    )
    came_in = swapped(sent_in, "flt_y")
    (grad_input,) = kernel_call(add_last, [shape((128, 256), f32)], 0, kept_in, came_in)
    mine, grad_input = lax.optimization_barrier((mine, grad_input))
    grads = kernel_call(
        finish_grads,
        [shape((864, 256), f32)] * 2,
        0,
        mine,
        swapped(mine),
        scratch=[pltpu.VMEM((2, 864, 256), f32), pltpu.SemaphoreType.DMA((2,))],
        target=pltpu.HBM,
    )
    row = lax.axis_index(FLT) * 16
    section_out = lax.dynamic_slice_in_dim(section, row, 16, 0).reshape(1, 4, 4, 256)
    return (section_out, grad_input.reshape(2, 8, 8, 256), *(as_filters(g) for g in grads))


def solution(mesh):
    torus = Mesh(mesh.devices.reshape(8, 2, 2, 4, 2), (*SP, *FLT))
    whole = P(FLT, None, None, None, None)
    rows = P(SP, FLT, None, None)
    return jax.shard_map(
        per_device,
        mesh=torus,
        in_specs=(rows, whole, whole, rows),
        out_specs=(rows, rows, whole, whole),
        check_vma=False,
    )
```

```python
import jax
import jax.numpy as jnp
from jax import lax
from jax.experimental import pallas as pl
from jax.experimental.pallas import tpu as pltpu
from jax.sharding import Mesh
from jax.sharding import PartitionSpec as P

SP = ("sp_z", "sp_y", "core")
CHIPS = ("sp_z", "sp_y")
FLT = ("flt_x", "flt_y")
bf16, f32 = jnp.bfloat16, jnp.float32

ROWS = 256
X_ROWS, COT_ROWS, W_ROWS = 256, 32, 128
PACK = X_ROWS + COT_ROWS + W_ROWS
GRAD_ROWS, GRAD_PAD = 1728, 1792
NT = (((1,), (1,)), ((), ()))
NN = (((1,), (0,)), ((), ()))
TN = (((0,), (0,)), ((), ()))


def dot(a, b, dims):
    return lax.dot_general(a, b, dims, preferred_element_type=f32)


def kernel_call(
    body, outs, flops, *args, scratch=(), space=pltpu.VMEM, target=pltpu.VMEM, limit=16, alias={}
):
    spaces = [pltpu.HBM if i in alias else space for i in range(len(args))]
    moved = sum(a.size * a.dtype.itemsize for a in (*args, *outs))
    return pl.pallas_call(
        body,
        out_shape=outs,
        in_specs=[pl.BlockSpec(memory_space=s) for s in spaces],
        out_specs=[pl.BlockSpec(memory_space=target)] * len(outs),
        scratch_shapes=scratch,
        input_output_aliases=alias,
        compiler_params=pltpu.CompilerParams(vmem_limit_bytes=limit << 20),
        cost_estimate=pl.CostEstimate(flops=flops, bytes_accessed=moved, transcendentals=0),
    )(*args)


def shape(dims, dtype):
    return jax.ShapeDtypeStruct(dims, dtype)


def lanes(rows):
    return lax.broadcasted_iota(jnp.int32, (rows, 128), 1)


def cells(rows):
    return lax.rem(lax.broadcasted_iota(jnp.int32, (rows, 128), 0), 8)


def before(v):
    return jnp.where(cells(v.shape[0]) == 0, 0.0, pltpu.roll(v, 1, 0))


def after(v):
    return jnp.where(cells(v.shape[0]) == 7, 0.0, pltpu.roll(v, v.shape[0] - 1, 0))


def rotated(v, slots):
    by = (32 * slots) % 128
    return pltpu.roll(v, by, 1) if by else v


def three(a, b, c):
    lane = lanes(a.shape[0])
    return jnp.where(lane < 32, a, jnp.where(lane < 64, b, jnp.where(lane < 96, c, 0.0)))


def row_down(v):
    return jnp.concatenate([jnp.zeros((8, v.shape[1]), v.dtype), v[:-8]], 0)


def row_up(v):
    return jnp.concatenate([v[8:], jnp.zeros((8, v.shape[1]), v.dtype)], 0)


def tap_sum(first, middle, last):
    lane = lanes(ROWS)
    t = jnp.where(lane < 32, first, jnp.where(lane < 64, middle, last))
    return t + rotated(t, -1) + rotated(t, -2)


def pair_of(pieces):
    lane = lanes(ROWS)
    v = pieces[0]
    for slot in (1, 2, 3):
        v = jnp.where(lane < 32 * slot, v, rotated(pieces[slot], slot))
    return v


def sigmoid(v):
    return jax.nn.sigmoid(v)


def silu_slope(v):
    s = sigmoid(v)
    return s * (1.0 + v * (1.0 - s))


def pack_inputs(x_far, w_far, cot_far, out, x, w, cot_near, cot, blocks, sems):
    loads = [
        pltpu.make_async_copy(x_far, x, sems.at[0]),
        pltpu.make_async_copy(cot_far, cot_near, sems.at[1]),
        pltpu.make_async_copy(w_far, w, sems.at[2]),
    ]
    for copy in loads:
        copy.start()
    sent = []

    def send(source, f, at, size):
        target = out.at[f, pl.ds(at, size), :]
        copy = pltpu.make_async_copy(source, target, sems.at[3 + len(sent)])
        copy.start()
        sent.append(copy)

    loads[0].wait()
    for f in range(8):
        for h in (0, 1):
            send(x.at[:, pl.ds(h * 128, 128)], f, h * 128, 128)
    loads[1].wait()
    for h in (0, 1):
        rows = [cot_near[0, i, :, h * 128 : h * 128 + 128].astype(f32) for i in range(4)]
        cot[h * 16 : h * 16 + 16, :] = jnp.concatenate(rows, 0).astype(bf16)
    for f in range(8):
        send(cot, f, X_ROWS, COT_ROWS)
    loads[2].wait()
    first_core = lax.axis_index("core") == 0
    lane = lanes(32)

    def block(k, m, h):
        at = pl.multiple_of(96 * k, 32)
        taps = [w[pl.ds(at + 32 * t, 32), h * 128 : h * 128 + 128].astype(f32) for t in range(3)]
        return three(*(rotated(taps[t], t - m) for t in range(3)))

    for h in (0, 1):
        for b in range(4):
            extra = w[(12 + min(b, 2)) * 32 : (13 + min(b, 2)) * 32, h * 128 : h * 128 + 128]
            extra = extra.astype(f32)
            for m in range(4):
                v = block(jnp.where(first_core, b, b + 5), m, h)
                v = jnp.where(lane < 96, v, rotated(extra, 3 - m))
                blocks[4 * h + m, b * 32 : b * 32 + 32, :] = v.astype(bf16)
        for m in range(4):
            send(blocks.at[4 * h + m], 4 * h + m, X_ROWS + COT_ROWS, W_ROWS)
    for copy in sent:
        copy.wait()


def prepare_first(w, wide, tall):
    zero = jnp.zeros((32, 256), bf16)
    for k0 in range(3):
        for k1 in range(3):
            for t in range(4):
                at = ((k0 * 3 + k1) * 3 + t) * 32
                v = w[at : at + 32, :] if t < 3 else zero
                wide[k0 * 128 + t * 32 : k0 * 128 + t * 32 + 32, k1 * 256 : k1 * 256 + 256] = v
                row = (k0 * 3 + k1) * 128 + t * 32
                tall[row : row + 32, :] = v


def first_conv(got, wide, low, high, within, across, field, part, window):
    part[...] = got[:, X_ROWS + COT_ROWS :, :]
    parts = {}
    for h in (0, 1):
        for p in (0, 1):
            blocks = ([], [])
            for g in range(8):
                at = h * 128 + p * 64
                v = got[g, at : at + 64, :].astype(f32).reshape(4, 2, 8, 128)
                for par in (0, 1):
                    blocks[par].append(v[:, par].reshape(32, 128))
            for par in (0, 1):
                parts[p, par, h] = jnp.concatenate(blocks[par], 0)
    for p in (0, 1):
        for h in (0, 1):
            even, odd = parts[p, 0, h], parts[p, 1, h]
            sources = ((row_down(odd), even, odd), (even, odd, row_up(even)))
            for par in (0, 1):
                at = (2 * p + par) * ROWS
                for k1 in range(3):
                    lane = k1 * 256 + h * 128
                    window[at : at + ROWS, lane : lane + 128] = sources[par][k1].astype(bf16)
                field[at : at + ROWS, h * 128 : h * 128 + 128] = sources[par][1].astype(bf16)
    sums = [dot(window[i * ROWS : i * ROWS + ROWS, :], wide[...], NT) for i in range(4)]
    pieces = []
    for plane in range(4):
        for par in (0, 1):
            terms = [
                sums[2 * p + par][:, k0 * 128 : k0 * 128 + 128]
                for p in (0, 1)
                for k0 in range(3)
                if p - k0 + 2 == plane
            ]
            v = terms[0] if len(terms) == 1 else terms[0] + terms[1]
            pieces.append(tap_sum(before(v), v, after(v)))
    a, b = pair_of(pieces[:4]), pair_of(pieces[4:])
    first_core = lax.axis_index("core") == 0
    low[...] = a
    high[...] = b
    within[...] = jnp.where(first_core, b, a)
    across[...] = jnp.where(first_core, a, b)


def gather_second(own, other, w2):
    first_core = lax.axis_index("core") == 0
    for g in range(8):
        row = slice(g * 32, g * 32 + 32)
        blocks = []
        for b in range(4):
            at = slice(b * 32, b * 32 + 32)
            x, y = own[g, at, :].astype(f32), other[g, at, :].astype(f32)
            early, late = jnp.where(first_core, x, y), jnp.where(first_core, y, x)
            w2[row, b * 128 : b * 128 + 128] = early.astype(bf16)
            w2[row, (b + 5) * 128 : (b + 6) * 128] = late.astype(bf16)
            blocks.append(early)
        v = three(*(rotated(blocks[t], t - 3) for t in range(3)))
        w2[row, 512:640] = v.astype(bf16)


def at_first_plane():
    return sum(lax.axis_index(name) for name in SP) == 0


def without_edge(v):
    return jnp.where(jnp.logical_and(at_first_plane(), lanes(ROWS) < 64), 0.0, v)


def below_above(within, across):
    first_core = lax.axis_index("core") == 0
    a, b = within[...], across[...]
    return jnp.where(first_core, b, a), jnp.where(first_core, a, b)


def second_conv(low, high, within, across, w2, pre, out, window, full):
    below, above = below_above(within, across)
    pairs = [low[...] + below, high[...] + above]
    pre[0:ROWS, :] = pairs[0]
    pre[ROWS:, :] = pairs[1]
    hidden = [v * sigmoid(v) for v in pairs]
    own = jnp.where(lanes(ROWS) < 64, rotated(hidden[0], 2), rotated(hidden[1], 2)).astype(bf16)
    for g in range(8):
        out[g, ROWS:, :] = own
    hidden[0] = without_edge(hidden[0])
    hidden = [v.astype(bf16).astype(f32) for v in hidden]
    shifted = [(before(v), v, after(v)) for v in hidden]
    for plane in range(3):
        pair = shifted[plane // 2]
        for par in (0, 1):
            slot = (plane % 2) * 2 + par
            v = three(*(rotated(pair[t], t - slot) for t in range(3)))
            at = (plane * 3 + 1 + par) * 128
            window[:, at : at + 128] = v.astype(bf16)
            if par:
                window[:, plane * 384 : plane * 384 + 128] = row_down(v).astype(bf16)
    total = dot(window[...], w2[...], NT)
    for h in (0, 1):
        full[h] = total[:, h * 128 : h * 128 + 128]
        v = full[h, pl.ds(0, 128, 2), :].astype(bf16)
        for g in range(8):
            out[g, h * 128 : h * 128 + 128, :] = v


def gather_hidden(parts, field):
    lane = lanes(ROWS)
    for h in (0, 1):
        blocks = [parts[4 * h + m, ROWS:, :].astype(f32) for m in range(4)]
        for slot in range(4):
            v = rotated(blocks[0], -slot)
            for m in (1, 2, 3):
                v = jnp.where(lane < 32 * m, v, rotated(blocks[m], m - slot))
            field[slot * ROWS : slot * ROWS + ROWS, h * 128 : h * 128 + 128] = v.astype(bf16)


def second_error(parts, got, section, err, full):
    for h in (0, 1):
        lane = slice(h * 128, h * 128 + 128)
        row = slice(h * 128, h * 128 + 128)
        v = parts[0, row, :].astype(f32)
        for g in range(1, 8):
            v = v + parts[g, row, :].astype(f32)
        cot = jnp.concatenate(
            [got[g, X_ROWS + h * 16 : X_ROWS + h * 16 + 16, :].astype(f32) for g in range(8)], 0
        )
        full[:, lane] = v * sigmoid(v)
        err[:, lane] = (cot * silu_slope(v)).astype(bf16)
    flt = lax.axis_index("flt_x") * 2 + lax.axis_index("flt_y")
    own = full[pl.ds(pl.multiple_of(flt * 16, 16), 16), :]
    for i in range(4):
        section[0, i] = own[4 * i : 4 * i + 4]


def spread_out(err, full):
    full[...] = jnp.zeros((ROWS, 128), f32)
    full[pl.ds(0, 128, 2), :] = err
    return full[...]


def second_grad(spread, hidden):
    flt = lax.axis_index("flt_x") * 2 + lax.axis_index("flt_y")
    turn = lax.rem(8 - flt, 4) * 32
    plain, ahead = [], []
    for left, right in spread:
        v = pltpu.roll(jnp.where(flt < 4, left, right), turn, 1)
        v = three(after(v), rotated(v, 1), rotated(before(v), 2))
        plain.append(v.astype(bf16))
        ahead.append(row_up(v).astype(bf16))
    grads = []
    for k0 in range(3):
        q = 1 if k0 == 0 else 0
        for k1 in range(3):
            at = ((1 if k0 == 1 else 3) - (1 if k1 == 1 else 0)) * ROWS
            errs = (ahead if k1 == 0 else plain)[q]
            grads.append(dot(errs, hidden[at : at + ROWS, :], TN))
    return grads


def backward(own, within, across, w2, pre, field, hidden, window, kept, sent, full):
    below, above = below_above(within, across)
    spread, ahead, halves = [], [], []
    for err in (below, own[...], above):
        both = [spread_out(err[:, h * 128 : h * 128 + 128].astype(f32), full) for h in (0, 1)]
        halves.append(both)
        v = jnp.concatenate(both, 1)
        spread.append(v.astype(bf16))
        ahead.append(row_up(v).astype(bf16))
    pieces = []
    for plane in range(4):
        both, extra = None, None
        for q, k0 in (((0, 2), (1, 0)), ((1, 1),), ((1, 2), (2, 0)), ((2, 1),))[plane]:
            at = k0 * 384
            a = dot(spread[q], w2[:, at + 128 : at + 384], NN)
            b = dot(ahead[q], w2[:, at : at + 128], NN)
            both = a if both is None else both + a
            extra = b if extra is None else extra + b
        for v in (both[:, :128], both[:, 128:] + extra):
            pieces.append(tap_sum(after(v), v, before(v)))
    errs = [pair_of(pieces[:4]), pair_of(pieces[4:])]
    errs = [errs[i] * silu_slope(pre[i * ROWS : i * ROWS + ROWS, :]) for i in (0, 1)]
    errs[0] = without_edge(errs[0])
    errs = [v.astype(bf16).astype(f32) for v in errs]
    shifted = [(after(v), v, before(v)) for v in errs]
    for plane in range(4):
        pair = shifted[plane // 2]
        taps = [
            three(*(rotated(pair[t], t - (plane % 2) * 2 - par) for t in range(3)))
            for par in (0, 1)
        ]
        even, odd = taps
        sources = ((odd, even, row_down(odd)), (row_up(even), odd, even))
        for par in (0, 1):
            for k1 in range(3):
                v = sources[par][k1].astype(bf16)
                for k0 in range(3):
                    target = plane + k0 - 1
                    if target in (1, 2):
                        at = (2 * (target - 1) + par) * ROWS
                        lane = (k0 * 3 + k1) * 128
                        window[at : at + ROWS, lane : lane + 128] = v
    first = dot(window[...], field[...], TN)
    second = second_grad(halves[1:], hidden)
    first_core = lax.axis_index("core") == 0
    for h in (0, 1):
        lane = slice(h * 128, h * 128 + 128)
        for k in range(9):
            at = h * 864 + k * 96
            a, b = first[k * 128 : k * 128 + 96, lane], second[k][:96, lane]
            kept[at : at + 96, :] = jnp.where(first_core, a, b)
            sent[at : at + 96, :] = jnp.where(first_core, b, a).astype(bf16)
    kept[GRAD_ROWS:, :] = jnp.zeros((GRAD_PAD - GRAD_ROWS, 128), f32)
    sent[GRAD_ROWS:, :] = jnp.zeros((GRAD_PAD - GRAD_ROWS, 128), bf16)


def input_grad(window, tall, kept, sent, blocks):
    for p in (0, 1):
        even = dot(window[2 * p * ROWS : (2 * p + 1) * ROWS, :], tall[...], NN)
        odd = dot(window[(2 * p + 1) * ROWS : (2 * p + 2) * ROWS, :], tall[...], NN)
        for g in range(8):
            a = even[g * 32 : g * 32 + 32].reshape(4, 1, 8, 256)
            b = odd[g * 32 : g * 32 + 32].reshape(4, 1, 8, 256)
            v = jnp.concatenate([a, b], 1).reshape(64, 256)
            blocks[g // 2, g % 2, p * 64 : p * 64 + 64, :] = v
    x = lax.axis_index("flt_x")
    partner = x + 1 - 2 * lax.rem(x, 2)
    kept[0] = blocks[x]
    kept[1] = blocks[3 - x]
    sent[0] = blocks[partner].astype(bf16)
    sent[1] = blocks[3 - partner].astype(bf16)


def add_pairs(kept, came, still, sent):
    still[...] = kept[0] + came[0].astype(f32)
    sent[...] = (kept[1] + came[1].astype(f32)).astype(bf16)


def add_halves(kept, came, still, sent):
    y = lax.axis_index("flt_y")
    still[...] = kept[y] + came[y].astype(f32)
    sent[...] = (kept[1 - y] + came[1 - y].astype(f32)).astype(bf16)


def add_last(kept, came, out):
    out[...] = kept[...] + came[...].astype(f32)


def add_core(kept, came, out):
    v = kept[...] + came[...].astype(f32)
    out[...] = v.astype(bf16).reshape(16, GRAD_PAD // 16, 128)


def add_chips(parts, out):
    v = parts[0].astype(f32)
    for i in range(1, 16):
        v = v + parts[i].astype(f32)
    v = v.astype(bf16)
    for i in range(16):
        out[i] = v


def finish_part(rows, first, second, near, sems, to_first):
    pieces = [pl.ds(i * 144, 144) for i in range(6)]
    for i, piece in enumerate(pieces):
        for h in (0, 1):
            at = h * 864 + i * 144
            near[piece, h * 128 : h * 128 + 128] = rows[at : at + 144, :].astype(f32)
        for target, wanted in ((first, to_first), (second, jnp.logical_not(to_first))):

            @pl.when(wanted)
            def _(target=target):
                pltpu.make_async_copy(near.at[piece], target.at[piece], sems.at[i]).start()

    for target, wanted in ((first, to_first), (second, jnp.logical_not(to_first))):

        @pl.when(wanted)
        def _(target=target):
            for i, piece in enumerate(pieces):
                pltpu.make_async_copy(near.at[piece], target.at[piece], sems.at[i]).wait()


def finish_own(rows, first, second, near, sems):
    finish_part(rows, first, second, near, sems, lax.axis_index("core") == 0)


def finish_other(rows, first_in, second_in, first, second, near, sems):
    finish_part(rows, first, second, near, sems, lax.axis_index("core") == 1)


def exchange(v, axis):
    return lax.all_to_all(v, axis, 0, 0, tiled=True)


def swapped(v, axis="core"):
    n = lax.axis_size(axis)
    return lax.ppermute(v, axis, [(i, i ^ 1) for i in range(n)])


def mirrored(v, axis):
    n = lax.axis_size(axis)
    return lax.ppermute(v, axis, [(i, n - 1 - i) for i in range(n)])


def next_chip(v):
    pairs = [(i, i + 1) for i in range(1, lax.axis_size(SP) - 1, 2)]
    return lax.ppermute(v, SP, pairs + [(b, a) for a, b in pairs])


def as_rows(w):
    return jnp.transpose(w, (1, 2, 3, 0, 4)).reshape(864, 256)


def as_filters(rows):
    return jnp.transpose(rows.reshape(3, 3, 3, 32, 256), (3, 0, 1, 2, 4))


def per_device(activations, w_first, w_second, cotangent):
    wide, tall = kernel_call(
        prepare_first, [shape((384, 768), bf16), shape((1152, 256), bf16)], 0, as_rows(w_first)
    )
    (packed,) = kernel_call(
        pack_inputs,
        [shape((8, PACK, 128), bf16)],
        0,
        activations.reshape(128, 256),
        as_rows(w_second),
        cotangent,
        scratch=[
            pltpu.VMEM((128, 256), bf16),
            pltpu.VMEM((864, 256), bf16),
            pltpu.VMEM((1, 4, 4, 256), bf16),
            pltpu.VMEM((COT_ROWS, 128), bf16),
            pltpu.VMEM((8, W_ROWS, 128), bf16),
            pltpu.SemaphoreType.DMA((35,)),
        ],
        space=pltpu.HBM,
        target=pltpu.HBM,
        limit=60,
    )
    got = exchange(packed, FLT)
    pair = shape((ROWS, 128), f32)
    low, high, within, across, field, part = kernel_call(
        first_conv,
        [pair, pair, pair, pair, shape((1024, 256), bf16), shape((8, W_ROWS, 128), bf16)],
        2 * 1024 * 768 * 384,
        got,
        wide,
        scratch=[pltpu.VMEM((1024, 768), bf16)],
    )
    across, within = next_chip(across), swapped(within)
    (w2,) = kernel_call(gather_second, [shape((256, 1152), bf16)], 0, part, swapped(part))
    pre, partial = kernel_call(
        second_conv,
        [shape((512, 128), f32), shape((8, 512, 128), bf16)],
        2 * 256 * 1152 * 256,
        low,
        high,
        within,
        across,
        w2,
        scratch=[pltpu.VMEM((ROWS, 1152), bf16), pltpu.VMEM((2, ROWS, 128), f32)],
    )
    parts = exchange(partial, FLT)
    section_out, err = kernel_call(
        second_error,
        [shape((1, 4, 4, 256), f32), shape((128, 256), bf16)],
        0,
        parts,
        got,
        scratch=[pltpu.VMEM((128, 256), f32)],
    )
    across, within = next_chip(err), swapped(err)
    (hidden,) = kernel_call(gather_hidden, [shape((1024, 256), bf16)], 0, parts)
    window, kept, sent = kernel_call(
        backward,
        [shape((1024, 1152), bf16), shape((GRAD_PAD, 128), f32), shape((GRAD_PAD, 128), bf16)],
        2 * 1024 * 1152 * 256 + 2 * 256 * 256 * 384 * 6,
        err,
        within,
        across,
        w2,
        pre,
        field,
        hidden,
        scratch=[pltpu.VMEM((ROWS, 128), f32)],
    )
    came = swapped(sent)
    kept_in, sent_in = kernel_call(
        input_grad,
        [shape((2, 2, 128, 256), f32), shape((2, 2, 128, 256), bf16)],
        2 * 1024 * 1152 * 256,
        window,
        tall,
        scratch=[pltpu.VMEM((4, 2, 128, 256), f32)],
    )
    chunk = shape((16, GRAD_PAD // 16, 128), bf16)
    (mine,) = kernel_call(add_core, [chunk], 0, kept, came)
    mine, sent_in = lax.optimization_barrier((mine, sent_in))
    came_in = swapped(sent_in, "flt_x")
    (mine,) = kernel_call(add_chips, [chunk], 0, exchange(mine, CHIPS))
    kept_in, sent_in = kernel_call(
        add_pairs, [shape((2, 128, 256), f32), shape((2, 128, 256), bf16)], 0, kept_in, came_in
    )
    came_in = mirrored(sent_in, "flt_x")
    kept_in, sent_in = kernel_call(
        add_halves, [shape((128, 256), f32), shape((128, 256), bf16)], 0, kept_in, came_in
    )
    mine, sent_in = lax.optimization_barrier((mine, sent_in))
    came_in = swapped(sent_in, "flt_y")
    mine = exchange(mine, CHIPS).reshape(GRAD_PAD, 128)
    (grad_input,) = kernel_call(add_last, [shape((128, 256), f32)], 0, kept_in, came_in)
    mine, grad_input = lax.optimization_barrier((mine, grad_input))
    full = [shape((864, 256), f32)] * 2
    scratch = [pltpu.VMEM((864, 256), f32), pltpu.SemaphoreType.DMA((6,))]
    other = swapped(mine)
    grads = kernel_call(finish_own, full, 0, mine, scratch=scratch, target=pltpu.HBM)
    grads = kernel_call(
        finish_other, full, 0, other, *grads, scratch=scratch, target=pltpu.HBM, alias={1: 0, 2: 1}
    )
    return (section_out, grad_input.reshape(2, 8, 8, 256), *(as_filters(g) for g in grads))


def solution(mesh):
    torus = Mesh(mesh.devices.reshape(8, 2, 2, 4, 2), (*SP, *FLT))
    whole = P(FLT, None, None, None, None)
    rows = P(SP, FLT, None, None)
    return jax.shard_map(
        per_device,
        mesh=torus,
        in_specs=(rows, whole, whole, rows),
        out_specs=(rows, rows, whole, whole),
        check_vma=False,
    )
```

```python
import jax
import jax.numpy as jnp
from jax import lax
from jax.experimental import pallas as pl
from jax.experimental.pallas import tpu as pltpu
from jax.sharding import Mesh
from jax.sharding import PartitionSpec as P

SP = ("sp_z", "sp_y", "core")
CHIPS = ("sp_z", "sp_y")
FLT = ("flt_x", "flt_y")
bf16, f32 = jnp.bfloat16, jnp.float32

ROWS = 256
X_ROWS, COT_ROWS, W_ROWS = 256, 32, 128
PACK = X_ROWS + COT_ROWS + W_ROWS
GRAD_ROWS, GRAD_PAD = 1728, 1792
NT = (((1,), (1,)), ((), ()))
NN = (((1,), (0,)), ((), ()))
TN = (((0,), (0,)), ((), ()))


def dot(a, b, dims):
    return lax.dot_general(a, b, dims, preferred_element_type=f32)


def kernel_call(
    body, outs, flops, *args, scratch=(), space=pltpu.VMEM, target=pltpu.VMEM, limit=16, alias={}
):
    spaces = [pltpu.HBM if i in alias else space for i in range(len(args))]
    moved = sum(a.size * a.dtype.itemsize for a in (*args, *outs))
    return pl.pallas_call(
        body,
        out_shape=outs,
        in_specs=[pl.BlockSpec(memory_space=s) for s in spaces],
        out_specs=[pl.BlockSpec(memory_space=target)] * len(outs),
        scratch_shapes=scratch,
        input_output_aliases=alias,
        compiler_params=pltpu.CompilerParams(vmem_limit_bytes=limit << 20),
        cost_estimate=pl.CostEstimate(flops=flops, bytes_accessed=moved, transcendentals=0),
    )(*args)


def shape(dims, dtype):
    return jax.ShapeDtypeStruct(dims, dtype)


def lanes(rows):
    return lax.broadcasted_iota(jnp.int32, (rows, 128), 1)


def cells(rows):
    return lax.rem(lax.broadcasted_iota(jnp.int32, (rows, 128), 0), 8)


def before(v):
    return jnp.where(cells(v.shape[0]) == 0, 0.0, pltpu.roll(v, 1, 0))


def after(v):
    return jnp.where(cells(v.shape[0]) == 7, 0.0, pltpu.roll(v, v.shape[0] - 1, 0))


def rotated(v, slots):
    by = (32 * slots) % 128
    return pltpu.roll(v, by, 1) if by else v


def three(a, b, c):
    lane = lanes(a.shape[0])
    return jnp.where(lane < 32, a, jnp.where(lane < 64, b, jnp.where(lane < 96, c, 0.0)))


def row_down(v):
    return jnp.concatenate([jnp.zeros((8, v.shape[1]), v.dtype), v[:-8]], 0)


def row_up(v):
    return jnp.concatenate([v[8:], jnp.zeros((8, v.shape[1]), v.dtype)], 0)


def tap_sum(first, middle, last):
    lane = lanes(ROWS)
    t = jnp.where(lane < 32, first, jnp.where(lane < 64, middle, last))
    return t + rotated(t, -1) + rotated(t, -2)


def pair_of(pieces):
    lane = lanes(ROWS)
    v = pieces[0]
    for slot in (1, 2, 3):
        v = jnp.where(lane < 32 * slot, v, rotated(pieces[slot], slot))
    return v


def sigmoid(v):
    return jax.nn.sigmoid(v)


def silu_slope(v):
    s = sigmoid(v)
    return s * (1.0 + v * (1.0 - s))


def pack_inputs(x_far, w_far, cot_far, out, x, w, cot_near, cot, blocks, sems):
    loads = [
        pltpu.make_async_copy(x_far, x, sems.at[0]),
        pltpu.make_async_copy(cot_far, cot_near, sems.at[1]),
        pltpu.make_async_copy(w_far, w, sems.at[2]),
    ]
    for copy in loads:
        copy.start()
    sent = []

    def send(source, f, at, size):
        target = out.at[f, pl.ds(at, size), :]
        copy = pltpu.make_async_copy(source, target, sems.at[3 + len(sent)])
        copy.start()
        sent.append(copy)

    loads[0].wait()
    for f in range(8):
        for h in (0, 1):
            send(x.at[:, pl.ds(h * 128, 128)], f, h * 128, 128)
    loads[1].wait()
    for h in (0, 1):
        rows = [cot_near[0, i, :, h * 128 : h * 128 + 128].astype(f32) for i in range(4)]
        cot[h * 16 : h * 16 + 16, :] = jnp.concatenate(rows, 0).astype(bf16)
    for f in range(8):
        send(cot, f, X_ROWS, COT_ROWS)
    loads[2].wait()
    first_core = lax.axis_index("core") == 0
    lane = lanes(32)

    def block(k, m, h):
        at = pl.multiple_of(96 * k, 32)
        taps = [w[pl.ds(at + 32 * t, 32), h * 128 : h * 128 + 128].astype(f32) for t in range(3)]
        return three(*(rotated(taps[t], t - m) for t in range(3)))

    for h in (0, 1):
        for b in range(4):
            extra = w[(12 + min(b, 2)) * 32 : (13 + min(b, 2)) * 32, h * 128 : h * 128 + 128]
            extra = extra.astype(f32)
            for m in range(4):
                v = block(jnp.where(first_core, b, b + 5), m, h)
                v = jnp.where(lane < 96, v, rotated(extra, 3 - m))
                blocks[4 * h + m, b * 32 : b * 32 + 32, :] = v.astype(bf16)
        for m in range(4):
            send(blocks.at[4 * h + m], 4 * h + m, X_ROWS + COT_ROWS, W_ROWS)
    for copy in sent:
        copy.wait()


def prepare_first(w, wide, tall):
    zero = jnp.zeros((32, 256), bf16)
    for k0 in range(3):
        for k1 in range(3):
            for t in range(4):
                at = ((k0 * 3 + k1) * 3 + t) * 32
                v = w[at : at + 32, :] if t < 3 else zero
                wide[k0 * 128 + t * 32 : k0 * 128 + t * 32 + 32, k1 * 256 : k1 * 256 + 256] = v
                row = (k0 * 3 + k1) * 128 + t * 32
                tall[row : row + 32, :] = v


def first_conv(got, wide, low, high, within, across, field, part, window):
    part[...] = got[:, X_ROWS + COT_ROWS :, :]
    parts = {}
    for h in (0, 1):
        for p in (0, 1):
            blocks = ([], [])
            for g in range(8):
                at = h * 128 + p * 64
                v = got[g, at : at + 64, :].astype(f32).reshape(4, 2, 8, 128)
                for par in (0, 1):
                    blocks[par].append(v[:, par].reshape(32, 128))
            for par in (0, 1):
                parts[p, par, h] = jnp.concatenate(blocks[par], 0)
    for p in (0, 1):
        for h in (0, 1):
            even, odd = parts[p, 0, h], parts[p, 1, h]
            sources = ((row_down(odd), even, odd), (even, odd, row_up(even)))
            for par in (0, 1):
                at = (2 * p + par) * ROWS
                for k1 in range(3):
                    lane = k1 * 256 + h * 128
                    window[at : at + ROWS, lane : lane + 128] = sources[par][k1].astype(bf16)
                field[at : at + ROWS, h * 128 : h * 128 + 128] = sources[par][1].astype(bf16)
    sums = [dot(window[i * ROWS : i * ROWS + ROWS, :], wide[...], NT) for i in range(4)]
    pieces = []
    for plane in range(4):
        for par in (0, 1):
            terms = [
                sums[2 * p + par][:, k0 * 128 : k0 * 128 + 128]
                for p in (0, 1)
                for k0 in range(3)
                if p - k0 + 2 == plane
            ]
            v = terms[0] if len(terms) == 1 else terms[0] + terms[1]
            pieces.append(tap_sum(before(v), v, after(v)))
    a, b = pair_of(pieces[:4]), pair_of(pieces[4:])
    first_core = lax.axis_index("core") == 0
    low[...] = a
    high[...] = b
    within[...] = jnp.where(first_core, b, a)
    across[...] = jnp.where(first_core, a, b)


def gather_second(own, other, w2):
    first_core = lax.axis_index("core") == 0
    for g in range(8):
        row = slice(g * 32, g * 32 + 32)
        blocks = []
        for b in range(4):
            at = slice(b * 32, b * 32 + 32)
            x, y = own[g, at, :].astype(f32), other[g, at, :].astype(f32)
            early, late = jnp.where(first_core, x, y), jnp.where(first_core, y, x)
            w2[row, b * 128 : b * 128 + 128] = early.astype(bf16)
            w2[row, (b + 5) * 128 : (b + 6) * 128] = late.astype(bf16)
            blocks.append(early)
        v = three(*(rotated(blocks[t], t - 3) for t in range(3)))
        w2[row, 512:640] = v.astype(bf16)


def at_first_plane():
    return sum(lax.axis_index(name) for name in SP) == 0


def without_edge(v):
    return jnp.where(jnp.logical_and(at_first_plane(), lanes(ROWS) < 64), 0.0, v)


def below_above(within, across):
    first_core = lax.axis_index("core") == 0
    a, b = within[...], across[...]
    return jnp.where(first_core, b, a), jnp.where(first_core, a, b)


def second_conv(low, high, within, across, w2, pre, out, window, full):
    below, above = below_above(within, across)
    pairs = [low[...] + below, high[...] + above]
    pre[0:ROWS, :] = pairs[0]
    pre[ROWS:, :] = pairs[1]
    hidden = [v * sigmoid(v) for v in pairs]
    own = jnp.where(lanes(ROWS) < 64, rotated(hidden[0], 2), rotated(hidden[1], 2)).astype(bf16)
    for g in range(8):
        out[g, ROWS:, :] = own
    hidden[0] = without_edge(hidden[0])
    hidden = [v.astype(bf16).astype(f32) for v in hidden]
    shifted = [(before(v), v, after(v)) for v in hidden]
    for plane in range(3):
        pair = shifted[plane // 2]
        for par in (0, 1):
            slot = (plane % 2) * 2 + par
            v = three(*(rotated(pair[t], t - slot) for t in range(3)))
            at = (plane * 3 + 1 + par) * 128
            window[:, at : at + 128] = v.astype(bf16)
            if par:
                window[:, plane * 384 : plane * 384 + 128] = row_down(v).astype(bf16)
    total = dot(window[...], w2[...], NT)
    for h in (0, 1):
        full[h] = total[:, h * 128 : h * 128 + 128]
        v = full[h, pl.ds(0, 128, 2), :].astype(bf16)
        for g in range(8):
            out[g, h * 128 : h * 128 + 128, :] = v


def gather_hidden(parts, field, section):
    flt = lax.axis_index("flt_x") * 2 + lax.axis_index("flt_y")
    for h in (0, 1):
        row = pl.ds(pl.multiple_of(h * 128 + flt * 16, 16), 16)
        v = parts[0, row, :].astype(f32)
        for g in range(1, 8):
            v = v + parts[g, row, :].astype(f32)
        v = v * sigmoid(v)
        for i in range(4):
            section[0, i, :, h * 128 : h * 128 + 128] = v[4 * i : 4 * i + 4]
    lane = lanes(ROWS)
    for h in (0, 1):
        blocks = [parts[4 * h + m, ROWS:, :].astype(f32) for m in range(4)]
        for slot in range(4):
            v = rotated(blocks[0], -slot)
            for m in (1, 2, 3):
                v = jnp.where(lane < 32 * m, v, rotated(blocks[m], m - slot))
            field[slot * ROWS : slot * ROWS + ROWS, h * 128 : h * 128 + 128] = v.astype(bf16)


def second_error(parts, got, err):
    for h in (0, 1):
        lane = slice(h * 128, h * 128 + 128)
        row = slice(h * 128, h * 128 + 128)
        v = parts[0, row, :].astype(f32)
        for g in range(1, 8):
            v = v + parts[g, row, :].astype(f32)
        cot = jnp.concatenate(
            [got[g, X_ROWS + h * 16 : X_ROWS + h * 16 + 16, :].astype(f32) for g in range(8)], 0
        )
        err[:, lane] = (cot * silu_slope(v)).astype(bf16)


def spread_out(err, full):
    full[...] = jnp.zeros((ROWS, 128), f32)
    full[pl.ds(0, 128, 2), :] = err
    return full[...]


def second_grad(spread, hidden):
    flt = lax.axis_index("flt_x") * 2 + lax.axis_index("flt_y")
    turn = lax.rem(8 - flt, 4) * 32
    plain, ahead = [], []
    for left, right in spread:
        v = pltpu.roll(jnp.where(flt < 4, left, right), turn, 1)
        v = three(after(v), rotated(v, 1), rotated(before(v), 2))
        plain.append(v.astype(bf16))
        ahead.append(row_up(v).astype(bf16))
    grads = []
    for k0 in range(3):
        q = 1 if k0 == 0 else 0
        for k1 in range(3):
            at = ((1 if k0 == 1 else 3) - (1 if k1 == 1 else 0)) * ROWS
            errs = (ahead if k1 == 0 else plain)[q]
            grads.append(dot(errs, hidden[at : at + ROWS, :], TN))
    return grads


def backward(own, within, across, w2, pre, field, hidden, window, kept, sent, full):
    below, above = below_above(within, across)
    spread, ahead, halves = [], [], []
    for err in (below, own[...], above):
        both = [spread_out(err[:, h * 128 : h * 128 + 128].astype(f32), full) for h in (0, 1)]
        halves.append(both)
        v = jnp.concatenate(both, 1)
        spread.append(v.astype(bf16))
        ahead.append(row_up(v).astype(bf16))
    pieces = []
    for plane in range(4):
        both, extra = None, None
        for q, k0 in (((0, 2), (1, 0)), ((1, 1),), ((1, 2), (2, 0)), ((2, 1),))[plane]:
            at = k0 * 384
            a = dot(spread[q], w2[:, at + 128 : at + 384], NN)
            b = dot(ahead[q], w2[:, at : at + 128], NN)
            both = a if both is None else both + a
            extra = b if extra is None else extra + b
        for v in (both[:, :128], both[:, 128:] + extra):
            pieces.append(tap_sum(after(v), v, before(v)))
    errs = [pair_of(pieces[:4]), pair_of(pieces[4:])]
    errs = [errs[i] * silu_slope(pre[i * ROWS : i * ROWS + ROWS, :]) for i in (0, 1)]
    errs[0] = without_edge(errs[0])
    errs = [v.astype(bf16).astype(f32) for v in errs]
    shifted = [(after(v), v, before(v)) for v in errs]
    for plane in range(4):
        pair = shifted[plane // 2]
        taps = [
            three(*(rotated(pair[t], t - (plane % 2) * 2 - par) for t in range(3)))
            for par in (0, 1)
        ]
        even, odd = taps
        sources = ((odd, even, row_down(odd)), (row_up(even), odd, even))
        for par in (0, 1):
            for k1 in range(3):
                v = sources[par][k1].astype(bf16)
                for k0 in range(3):
                    target = plane + k0 - 1
                    if target in (1, 2):
                        at = (2 * (target - 1) + par) * ROWS
                        lane = (k0 * 3 + k1) * 128
                        window[at : at + ROWS, lane : lane + 128] = v
    first = dot(window[...], field[...], TN)
    second = second_grad(halves[1:], hidden)
    first_core = lax.axis_index("core") == 0
    for h in (0, 1):
        lane = slice(h * 128, h * 128 + 128)
        for k in range(9):
            at = h * 864 + k * 96
            a, b = first[k * 128 : k * 128 + 96, lane], second[k][:96, lane]
            kept[at : at + 96, :] = jnp.where(first_core, a, b)
            sent[at : at + 96, :] = jnp.where(first_core, b, a).astype(bf16)
    kept[GRAD_ROWS:, :] = jnp.zeros((GRAD_PAD - GRAD_ROWS, 128), f32)
    sent[GRAD_ROWS:, :] = jnp.zeros((GRAD_PAD - GRAD_ROWS, 128), bf16)


def input_grad(window, tall, kept, sent, blocks):
    for p in (0, 1):
        even = dot(window[2 * p * ROWS : (2 * p + 1) * ROWS, :], tall[...], NN)
        odd = dot(window[(2 * p + 1) * ROWS : (2 * p + 2) * ROWS, :], tall[...], NN)
        for g in range(8):
            a = even[g * 32 : g * 32 + 32].reshape(4, 1, 8, 256)
            b = odd[g * 32 : g * 32 + 32].reshape(4, 1, 8, 256)
            v = jnp.concatenate([a, b], 1).reshape(64, 256)
            blocks[g // 2, g % 2, p * 64 : p * 64 + 64, :] = v
    x = lax.axis_index("flt_x")
    partner = x + 1 - 2 * lax.rem(x, 2)
    kept[0] = blocks[x]
    kept[1] = blocks[3 - x]
    sent[0] = blocks[partner].astype(bf16)
    sent[1] = blocks[3 - partner].astype(bf16)


def add_pairs(kept, came, still, sent):
    still[...] = kept[0] + came[0].astype(f32)
    sent[...] = (kept[1] + came[1].astype(f32)).astype(bf16)


def add_halves(kept, came, still, sent):
    y = lax.axis_index("flt_y")
    still[...] = kept[y] + came[y].astype(f32)
    sent[...] = (kept[1 - y] + came[1 - y].astype(f32)).astype(bf16)


def add_last(kept, came, out):
    out[...] = kept[...] + came[...].astype(f32)


def add_core(kept, came, out):
    v = kept[...] + came[...].astype(f32)
    out[...] = v.astype(bf16).reshape(16, GRAD_PAD // 16, 128)


def add_chips(parts, out):
    v = parts[0].astype(f32)
    for i in range(1, 16):
        v = v + parts[i].astype(f32)
    v = v.astype(bf16)
    for i in range(16):
        out[i] = v


def finish_part(rows, first, second, near, sems, to_first):
    pieces = [pl.ds(i * 144, 144) for i in range(6)]
    for i, piece in enumerate(pieces):
        for h in (0, 1):
            at = h * 864 + i * 144
            near[piece, h * 128 : h * 128 + 128] = rows[at : at + 144, :].astype(f32)
        for target, wanted in ((first, to_first), (second, jnp.logical_not(to_first))):

            @pl.when(wanted)
            def _(target=target):
                pltpu.make_async_copy(near.at[piece], target.at[piece], sems.at[i]).start()

    for target, wanted in ((first, to_first), (second, jnp.logical_not(to_first))):

        @pl.when(wanted)
        def _(target=target):
            for i, piece in enumerate(pieces):
                pltpu.make_async_copy(near.at[piece], target.at[piece], sems.at[i]).wait()


def finish_own(rows, first, second, near, sems):
    finish_part(rows, first, second, near, sems, lax.axis_index("core") == 0)


def finish_other(rows, first_in, second_in, first, second, near, sems):
    finish_part(rows, first, second, near, sems, lax.axis_index("core") == 1)


def exchange(v, axis):
    return lax.all_to_all(v, axis, 0, 0, tiled=True)


def swapped(v, axis="core"):
    n = lax.axis_size(axis)
    return lax.ppermute(v, axis, [(i, i ^ 1) for i in range(n)])


def mirrored(v, axis):
    n = lax.axis_size(axis)
    return lax.ppermute(v, axis, [(i, n - 1 - i) for i in range(n)])


def next_chip(v):
    pairs = [(i, i + 1) for i in range(1, lax.axis_size(SP) - 1, 2)]
    return lax.ppermute(v, SP, pairs + [(b, a) for a, b in pairs])


def as_rows(w):
    return jnp.transpose(w, (1, 2, 3, 0, 4)).reshape(864, 256)


def as_filters(rows):
    return jnp.transpose(rows.reshape(3, 3, 3, 32, 256), (3, 0, 1, 2, 4))


def per_device(activations, w_first, w_second, cotangent):
    wide, tall = kernel_call(
        prepare_first, [shape((384, 768), bf16), shape((1152, 256), bf16)], 0, as_rows(w_first)
    )
    (packed,) = kernel_call(
        pack_inputs,
        [shape((8, PACK, 128), bf16)],
        0,
        activations.reshape(128, 256),
        as_rows(w_second),
        cotangent,
        scratch=[
            pltpu.VMEM((128, 256), bf16),
            pltpu.VMEM((864, 256), bf16),
            pltpu.VMEM((1, 4, 4, 256), bf16),
            pltpu.VMEM((COT_ROWS, 128), bf16),
            pltpu.VMEM((8, W_ROWS, 128), bf16),
            pltpu.SemaphoreType.DMA((35,)),
        ],
        space=pltpu.HBM,
        target=pltpu.HBM,
        limit=60,
    )
    got = exchange(packed, FLT)
    pair = shape((ROWS, 128), f32)
    low, high, within, across, field, part = kernel_call(
        first_conv,
        [pair, pair, pair, pair, shape((1024, 256), bf16), shape((8, W_ROWS, 128), bf16)],
        2 * 1024 * 768 * 384,
        got,
        wide,
        scratch=[pltpu.VMEM((1024, 768), bf16)],
    )
    across, within = next_chip(across), swapped(within)
    (w2,) = kernel_call(gather_second, [shape((256, 1152), bf16)], 0, part, swapped(part))
    pre, partial = kernel_call(
        second_conv,
        [shape((512, 128), f32), shape((8, 512, 128), bf16)],
        2 * 256 * 1152 * 256,
        low,
        high,
        within,
        across,
        w2,
        scratch=[pltpu.VMEM((ROWS, 1152), bf16), pltpu.VMEM((2, ROWS, 128), f32)],
    )
    parts = exchange(partial, FLT)
    (err,) = kernel_call(second_error, [shape((128, 256), bf16)], 0, parts, got)
    across, within = next_chip(err), swapped(err)
    hidden, section_out = kernel_call(
        gather_hidden, [shape((1024, 256), bf16), shape((1, 4, 4, 256), f32)], 0, parts
    )
    window, kept, sent = kernel_call(
        backward,
        [shape((1024, 1152), bf16), shape((GRAD_PAD, 128), f32), shape((GRAD_PAD, 128), bf16)],
        2 * 1024 * 1152 * 256 + 2 * 256 * 256 * 384 * 6,
        err,
        within,
        across,
        w2,
        pre,
        field,
        hidden,
        scratch=[pltpu.VMEM((ROWS, 128), f32)],
    )
    came = swapped(sent)
    kept_in, sent_in = kernel_call(
        input_grad,
        [shape((2, 2, 128, 256), f32), shape((2, 2, 128, 256), bf16)],
        2 * 1024 * 1152 * 256,
        window,
        tall,
        scratch=[pltpu.VMEM((4, 2, 128, 256), f32)],
    )
    chunk = shape((16, GRAD_PAD // 16, 128), bf16)
    (mine,) = kernel_call(add_core, [chunk], 0, kept, came)
    mine, sent_in = lax.optimization_barrier((mine, sent_in))
    came_in = swapped(sent_in, "flt_x")
    (mine,) = kernel_call(add_chips, [chunk], 0, exchange(mine, CHIPS))
    kept_in, sent_in = kernel_call(
        add_pairs, [shape((2, 128, 256), f32), shape((2, 128, 256), bf16)], 0, kept_in, came_in
    )
    came_in = mirrored(sent_in, "flt_x")
    kept_in, sent_in = kernel_call(
        add_halves, [shape((128, 256), f32), shape((128, 256), bf16)], 0, kept_in, came_in
    )
    mine, sent_in = lax.optimization_barrier((mine, sent_in))
    came_in = swapped(sent_in, "flt_y")
    mine = exchange(mine, CHIPS).reshape(GRAD_PAD, 128)
    (grad_input,) = kernel_call(add_last, [shape((128, 256), f32)], 0, kept_in, came_in)
    mine, grad_input = lax.optimization_barrier((mine, grad_input))
    full = [shape((864, 256), f32)] * 2
    scratch = [pltpu.VMEM((864, 256), f32), pltpu.SemaphoreType.DMA((6,))]
    other = swapped(mine)
    grads = kernel_call(finish_own, full, 0, mine, scratch=scratch, target=pltpu.HBM)
    grads = kernel_call(
        finish_other, full, 0, other, *grads, scratch=scratch, target=pltpu.HBM, alias={1: 0, 2: 1}
    )
    return (section_out, grad_input.reshape(2, 8, 8, 256), *(as_filters(g) for g in grads))


def solution(mesh):
    torus = Mesh(mesh.devices.reshape(8, 2, 2, 4, 2), (*SP, *FLT))
    whole = P(FLT, None, None, None, None)
    rows = P(SP, FLT, None, None)
    return jax.shard_map(
        per_device,
        mesh=torus,
        in_specs=(rows, whole, whole, rows),
        out_specs=(rows, rows, whole, whole),
        check_vma=False,
    )
```

```python
import jax
import jax.numpy as jnp
from jax import lax
from jax.experimental import pallas as pl
from jax.experimental.pallas import tpu as pltpu
from jax.sharding import Mesh
from jax.sharding import PartitionSpec as P

SP = ("sp_z", "sp_y", "core")
CHIPS = ("sp_z", "sp_y")
FLT = ("flt_x", "flt_y")
bf16, f32 = jnp.bfloat16, jnp.float32

ROWS = 256
X_ROWS, COT_ROWS, W_ROWS = 256, 32, 128
PACK = X_ROWS + COT_ROWS + W_ROWS
GRAD_ROWS, GRAD_PAD = 1728, 1792
NT = (((1,), (1,)), ((), ()))
NN = (((1,), (0,)), ((), ()))
TN = (((0,), (0,)), ((), ()))


def dot(a, b, dims):
    return lax.dot_general(a, b, dims, preferred_element_type=f32)


def kernel_call(
    body, outs, flops, *args, scratch=(), space=pltpu.VMEM, target=pltpu.VMEM, limit=16, alias={}
):
    spaces = [pltpu.HBM if i in alias else space for i in range(len(args))]
    moved = sum(a.size * a.dtype.itemsize for a in (*args, *outs))
    return pl.pallas_call(
        body,
        out_shape=outs,
        in_specs=[pl.BlockSpec(memory_space=s) for s in spaces],
        out_specs=[pl.BlockSpec(memory_space=target)] * len(outs),
        scratch_shapes=scratch,
        input_output_aliases=alias,
        compiler_params=pltpu.CompilerParams(vmem_limit_bytes=limit << 20),
        cost_estimate=pl.CostEstimate(flops=flops, bytes_accessed=moved, transcendentals=0),
    )(*args)


def shape(dims, dtype):
    return jax.ShapeDtypeStruct(dims, dtype)


def lanes(rows):
    return lax.broadcasted_iota(jnp.int32, (rows, 128), 1)


def cells(rows):
    return lax.rem(lax.broadcasted_iota(jnp.int32, (rows, 128), 0), 8)


def before(v):
    return jnp.where(cells(v.shape[0]) == 0, 0.0, pltpu.roll(v, 1, 0))


def after(v):
    return jnp.where(cells(v.shape[0]) == 7, 0.0, pltpu.roll(v, v.shape[0] - 1, 0))


def rotated(v, slots):
    by = (32 * slots) % 128
    return pltpu.roll(v, by, 1) if by else v


def three(a, b, c):
    lane = lanes(a.shape[0])
    return jnp.where(lane < 32, a, jnp.where(lane < 64, b, jnp.where(lane < 96, c, 0.0)))


def row_down(v):
    return jnp.concatenate([jnp.zeros((8, v.shape[1]), v.dtype), v[:-8]], 0)


def row_up(v):
    return jnp.concatenate([v[8:], jnp.zeros((8, v.shape[1]), v.dtype)], 0)


def tap_sum(first, middle, last):
    lane = lanes(ROWS)
    t = jnp.where(lane < 32, first, jnp.where(lane < 64, middle, last))
    return t + rotated(t, -1) + rotated(t, -2)


def pair_of(pieces):
    lane = lanes(ROWS)
    v = pieces[0]
    for slot in (1, 2, 3):
        v = jnp.where(lane < 32 * slot, v, rotated(pieces[slot], slot))
    return v


def sigmoid(v):
    return jax.nn.sigmoid(v)


def silu_slope(v):
    s = sigmoid(v)
    return s * (1.0 + v * (1.0 - s))


def pack_inputs(x_far, w_far, cot_far, out, x, w, cot_near, cot, blocks, sems):
    loads = [
        pltpu.make_async_copy(x_far, x, sems.at[0]),
        pltpu.make_async_copy(cot_far, cot_near, sems.at[1]),
        pltpu.make_async_copy(w_far, w, sems.at[2]),
    ]
    for copy in loads:
        copy.start()
    sent = []

    def send(source, f, at, size):
        target = out.at[f, pl.ds(at, size), :]
        copy = pltpu.make_async_copy(source, target, sems.at[3 + len(sent)])
        copy.start()
        sent.append(copy)

    loads[0].wait()
    for f in range(8):
        for h in (0, 1):
            send(x.at[:, pl.ds(h * 128, 128)], f, h * 128, 128)
    loads[1].wait()
    for h in (0, 1):
        rows = [cot_near[0, i, :, h * 128 : h * 128 + 128].astype(f32) for i in range(4)]
        cot[h * 16 : h * 16 + 16, :] = jnp.concatenate(rows, 0).astype(bf16)
    for f in range(8):
        send(cot, f, X_ROWS, COT_ROWS)
    loads[2].wait()
    first_core = lax.axis_index("core") == 0
    lane = lanes(32)

    def block(k, m, h):
        at = pl.multiple_of(96 * k, 32)
        taps = [w[pl.ds(at + 32 * t, 32), h * 128 : h * 128 + 128].astype(f32) for t in range(3)]
        return three(*(rotated(taps[t], t - m) for t in range(3)))

    for h in (0, 1):
        for b in range(4):
            extra = w[(12 + min(b, 2)) * 32 : (13 + min(b, 2)) * 32, h * 128 : h * 128 + 128]
            extra = extra.astype(f32)
            for m in range(4):
                v = block(jnp.where(first_core, b, b + 5), m, h)
                v = jnp.where(lane < 96, v, rotated(extra, 3 - m))
                blocks[4 * h + m, b * 32 : b * 32 + 32, :] = v.astype(bf16)
        for m in range(4):
            send(blocks.at[4 * h + m], 4 * h + m, X_ROWS + COT_ROWS, W_ROWS)
    for copy in sent:
        copy.wait()


def prepare_first(w, wide, tall):
    zero = jnp.zeros((32, 256), bf16)
    for k0 in range(3):
        for k1 in range(3):
            for t in range(4):
                at = ((k0 * 3 + k1) * 3 + t) * 32
                v = w[at : at + 32, :] if t < 3 else zero
                wide[k0 * 128 + t * 32 : k0 * 128 + t * 32 + 32, k1 * 256 : k1 * 256 + 256] = v
                row = (k0 * 3 + k1) * 128 + t * 32
                tall[row : row + 32, :] = v


def first_conv(got, wide, low, high, within, across, field, part, window):
    part[...] = got[:, X_ROWS + COT_ROWS :, :]
    parts = {}
    for h in (0, 1):
        for p in (0, 1):
            blocks = ([], [])
            for g in range(8):
                at = h * 128 + p * 64
                v = got[g, at : at + 64, :].astype(f32).reshape(4, 2, 8, 128)
                for par in (0, 1):
                    blocks[par].append(v[:, par].reshape(32, 128))
            for par in (0, 1):
                parts[p, par, h] = jnp.concatenate(blocks[par], 0)
    for p in (0, 1):
        for h in (0, 1):
            even, odd = parts[p, 0, h], parts[p, 1, h]
            sources = ((row_down(odd), even, odd), (even, odd, row_up(even)))
            for par in (0, 1):
                at = (2 * p + par) * ROWS
                for k1 in range(3):
                    lane = k1 * 256 + h * 128
                    window[at : at + ROWS, lane : lane + 128] = sources[par][k1].astype(bf16)
                field[at : at + ROWS, h * 128 : h * 128 + 128] = sources[par][1].astype(bf16)
    sums = [dot(window[i * ROWS : i * ROWS + ROWS, :], wide[...], NT) for i in range(4)]
    pieces = []
    for plane in range(4):
        for par in (0, 1):
            terms = [
                sums[2 * p + par][:, k0 * 128 : k0 * 128 + 128]
                for p in (0, 1)
                for k0 in range(3)
                if p - k0 + 2 == plane
            ]
            v = terms[0] if len(terms) == 1 else terms[0] + terms[1]
            pieces.append(tap_sum(before(v), v, after(v)))
    a, b = pair_of(pieces[:4]), pair_of(pieces[4:])
    first_core = lax.axis_index("core") == 0
    low[...] = a
    high[...] = b
    within[...] = jnp.where(first_core, b, a)
    across[...] = jnp.where(first_core, a, b)


def gather_second(own, other, w2):
    first_core = lax.axis_index("core") == 0
    for g in range(8):
        row = slice(g * 32, g * 32 + 32)
        blocks = []
        for b in range(4):
            at = slice(b * 32, b * 32 + 32)
            x, y = own[g, at, :].astype(f32), other[g, at, :].astype(f32)
            early, late = jnp.where(first_core, x, y), jnp.where(first_core, y, x)
            w2[row, b * 128 : b * 128 + 128] = early.astype(bf16)
            w2[row, (b + 5) * 128 : (b + 6) * 128] = late.astype(bf16)
            blocks.append(early)
        v = three(*(rotated(blocks[t], t - 3) for t in range(3)))
        w2[row, 512:640] = v.astype(bf16)


def at_first_plane():
    return sum(lax.axis_index(name) for name in SP) == 0


def without_edge(v):
    return jnp.where(jnp.logical_and(at_first_plane(), lanes(ROWS) < 64), 0.0, v)


def below_above(within, across):
    first_core = lax.axis_index("core") == 0
    a, b = within[...], across[...]
    return jnp.where(first_core, b, a), jnp.where(first_core, a, b)


def second_conv(low, high, within, across, w2, pre, out, window, full):
    below, above = below_above(within, across)
    pairs = [low[...] + below, high[...] + above]
    pre[0:ROWS, :] = pairs[0]
    pre[ROWS:, :] = pairs[1]
    hidden = [v * sigmoid(v) for v in pairs]
    own = jnp.where(lanes(ROWS) < 64, rotated(hidden[0], 2), rotated(hidden[1], 2)).astype(bf16)
    for g in range(8):
        out[g, ROWS:, :] = own
    hidden[0] = without_edge(hidden[0])
    hidden = [v.astype(bf16).astype(f32) for v in hidden]
    shifted = [(before(v), v, after(v)) for v in hidden]
    for plane in range(3):
        pair = shifted[plane // 2]
        for par in (0, 1):
            slot = (plane % 2) * 2 + par
            v = three(*(rotated(pair[t], t - slot) for t in range(3)))
            at = (plane * 3 + 1 + par) * 128
            window[:, at : at + 128] = v.astype(bf16)
            if par:
                window[:, plane * 384 : plane * 384 + 128] = row_down(v).astype(bf16)
    total = dot(window[...], w2[...], NT)
    for h in (0, 1):
        full[h] = total[:, h * 128 : h * 128 + 128]
        v = full[h, pl.ds(0, 128, 2), :].astype(bf16)
        for g in range(8):
            out[g, h * 128 : h * 128 + 128, :] = v


def gather_hidden(parts, field, section):
    flt = lax.axis_index("flt_x") * 2 + lax.axis_index("flt_y")
    for h in (0, 1):
        row = pl.ds(pl.multiple_of(h * 128 + flt * 16, 16), 16)
        v = parts[0, row, :].astype(f32)
        for g in range(1, 8):
            v = v + parts[g, row, :].astype(f32)
        v = v * sigmoid(v)
        for i in range(4):
            section[0, i, :, h * 128 : h * 128 + 128] = v[4 * i : 4 * i + 4]
    lane = lanes(ROWS)
    for h in (0, 1):
        blocks = [parts[4 * h + m, ROWS:, :].astype(f32) for m in range(4)]
        for slot in range(4):
            v = rotated(blocks[0], -slot)
            for m in (1, 2, 3):
                v = jnp.where(lane < 32 * m, v, rotated(blocks[m], m - slot))
            field[slot * ROWS : slot * ROWS + ROWS, h * 128 : h * 128 + 128] = v.astype(bf16)


def second_error(parts, got, err):
    for h in (0, 1):
        lane = slice(h * 128, h * 128 + 128)
        row = slice(h * 128, h * 128 + 128)
        v = parts[0, row, :].astype(f32)
        for g in range(1, 8):
            v = v + parts[g, row, :].astype(f32)
        cot = jnp.concatenate(
            [got[g, X_ROWS + h * 16 : X_ROWS + h * 16 + 16, :].astype(f32) for g in range(8)], 0
        )
        err[:, lane] = (cot * silu_slope(v)).astype(bf16)


def spread_out(err, full):
    full[...] = jnp.zeros((ROWS, 128), f32)
    full[pl.ds(0, 128, 2), :] = err
    return full[...]


def second_grad(spread, hidden):
    flt = lax.axis_index("flt_x") * 2 + lax.axis_index("flt_y")
    turn = lax.rem(8 - flt, 4) * 32
    plain, ahead = [], []
    for left, right in spread:
        v = pltpu.roll(jnp.where(flt < 4, left, right), turn, 1)
        v = three(after(v), rotated(v, 1), rotated(before(v), 2))
        plain.append(v.astype(bf16))
        ahead.append(row_up(v).astype(bf16))
    grads = []
    for k0 in range(3):
        q = 1 if k0 == 0 else 0
        for k1 in range(3):
            at = ((1 if k0 == 1 else 3) - (1 if k1 == 1 else 0)) * ROWS
            errs = (ahead if k1 == 0 else plain)[q]
            grads.append(dot(errs, hidden[at : at + ROWS, :], TN))
    return grads


def backward(own, within, across, w2, pre, field, hidden, window, kept, sent, full):
    below, above = below_above(within, across)
    spread, ahead, halves = [], [], []
    for err in (below, own[...], above):
        both = [spread_out(err[:, h * 128 : h * 128 + 128].astype(f32), full) for h in (0, 1)]
        halves.append(both)
        v = jnp.concatenate(both, 1)
        spread.append(v.astype(bf16))
        ahead.append(row_up(v).astype(bf16))
    pieces = []
    for plane in range(4):
        both, extra = None, None
        for q, k0 in (((0, 2), (1, 0)), ((1, 1),), ((1, 2), (2, 0)), ((2, 1),))[plane]:
            at = k0 * 384
            a = dot(spread[q], w2[:, at + 128 : at + 384], NN)
            b = dot(ahead[q], w2[:, at : at + 128], NN)
            both = a if both is None else both + a
            extra = b if extra is None else extra + b
        for v in (both[:, :128], both[:, 128:] + extra):
            pieces.append(tap_sum(after(v), v, before(v)))
    errs = [pair_of(pieces[:4]), pair_of(pieces[4:])]
    errs = [errs[i] * silu_slope(pre[i * ROWS : i * ROWS + ROWS, :]) for i in (0, 1)]
    errs[0] = without_edge(errs[0])
    errs = [v.astype(bf16).astype(f32) for v in errs]
    shifted = [(after(v), v, before(v)) for v in errs]
    for plane in range(4):
        pair = shifted[plane // 2]
        taps = [
            three(*(rotated(pair[t], t - (plane % 2) * 2 - par) for t in range(3)))
            for par in (0, 1)
        ]
        even, odd = taps
        sources = ((odd, even, row_down(odd)), (row_up(even), odd, even))
        for par in (0, 1):
            for k1 in range(3):
                v = sources[par][k1].astype(bf16)
                for k0 in range(3):
                    target = plane + k0 - 1
                    if target in (1, 2):
                        at = (2 * (target - 1) + par) * ROWS
                        lane = (k0 * 3 + k1) * 128
                        window[at : at + ROWS, lane : lane + 128] = v
    first = dot(window[...], field[...], TN)
    second = second_grad(halves[1:], hidden)
    first_core = lax.axis_index("core") == 0
    for h in (0, 1):
        lane = slice(h * 128, h * 128 + 128)
        for k in range(9):
            at = h * 864 + k * 96
            a, b = first[k * 128 : k * 128 + 96, lane], second[k][:96, lane]
            kept[at : at + 96, :] = jnp.where(first_core, a, b)
            sent[at : at + 96, :] = jnp.where(first_core, b, a).astype(bf16)
    kept[GRAD_ROWS:, :] = jnp.zeros((GRAD_PAD - GRAD_ROWS, 128), f32)
    sent[GRAD_ROWS:, :] = jnp.zeros((GRAD_PAD - GRAD_ROWS, 128), bf16)


def input_grad(window, tall, kept, sent, blocks):
    for p in (0, 1):
        even = dot(window[2 * p * ROWS : (2 * p + 1) * ROWS, :], tall[...], NN)
        odd = dot(window[(2 * p + 1) * ROWS : (2 * p + 2) * ROWS, :], tall[...], NN)
        for g in range(8):
            a = even[g * 32 : g * 32 + 32].reshape(4, 1, 8, 256)
            b = odd[g * 32 : g * 32 + 32].reshape(4, 1, 8, 256)
            v = jnp.concatenate([a, b], 1).reshape(64, 256)
            blocks[g // 2, g % 2, p * 64 : p * 64 + 64, :] = v
    x = lax.axis_index("flt_x")
    partner = x + 1 - 2 * lax.rem(x, 2)
    kept[0] = blocks[x]
    kept[1] = blocks[3 - x]
    sent[0] = blocks[partner].astype(bf16)
    sent[1] = blocks[3 - partner].astype(bf16)


def add_pairs(kept, came, still, sent):
    still[...] = kept[0] + came[0].astype(f32)
    sent[...] = (kept[1] + came[1].astype(f32)).astype(bf16)


def add_halves(kept, came, still, sent):
    y = lax.axis_index("flt_y")
    still[...] = kept[y] + came[y].astype(f32)
    sent[...] = (kept[1 - y] + came[1 - y].astype(f32)).astype(bf16)


def add_last(kept, came, out):
    out[...] = kept[...] + came[...].astype(f32)


def add_core(kept, came, out):
    v = kept[...] + came[...].astype(f32)
    out[...] = v.astype(bf16).reshape(16, GRAD_PAD // 16, 128)


def add_chips(parts, out):
    v = parts[0].astype(f32)
    for i in range(1, 16):
        v = v + parts[i].astype(f32)
    v = v.astype(bf16)
    for i in range(16):
        out[i] = v


def finish_part(rows, first, second, near, sems, to_first):
    pieces = [pl.ds(i * 144, 144) for i in range(6)]
    for i, piece in enumerate(pieces):
        for h in (0, 1):
            at = h * 864 + i * 144
            near[piece, h * 128 : h * 128 + 128] = rows[at : at + 144, :].astype(f32)
        for target, wanted in ((first, to_first), (second, jnp.logical_not(to_first))):

            @pl.when(wanted)
            def _(target=target):
                pltpu.make_async_copy(near.at[piece], target.at[piece], sems.at[i]).start()

    for target, wanted in ((first, to_first), (second, jnp.logical_not(to_first))):

        @pl.when(wanted)
        def _(target=target):
            for i, piece in enumerate(pieces):
                pltpu.make_async_copy(near.at[piece], target.at[piece], sems.at[i]).wait()


def finish_own(rows, first, second, near, sems):
    finish_part(rows, first, second, near, sems, lax.axis_index("core") == 0)


def finish_other(rows, first_in, second_in, first, second, near, sems):
    finish_part(rows, first, second, near, sems, lax.axis_index("core") == 1)


def exchange(v, axis):
    return lax.all_to_all(v, axis, 0, 0, tiled=True)


def swapped(v, axis="core"):
    n = lax.axis_size(axis)
    return lax.ppermute(v, axis, [(i, i ^ 1) for i in range(n)])


def mirrored(v, axis):
    n = lax.axis_size(axis)
    return lax.ppermute(v, axis, [(i, n - 1 - i) for i in range(n)])


def next_chip(v):
    pairs = [(i, i + 1) for i in range(1, lax.axis_size(SP) - 1, 2)]
    return lax.ppermute(v, SP, pairs + [(b, a) for a, b in pairs])


def as_rows(w):
    return jnp.transpose(w, (1, 2, 3, 0, 4)).reshape(864, 256)


def as_filters(rows):
    return jnp.transpose(rows.reshape(3, 3, 3, 32, 256), (3, 0, 1, 2, 4))


def per_device(activations, w_first, w_second, cotangent):
    wide, tall = kernel_call(
        prepare_first, [shape((384, 768), bf16), shape((1152, 256), bf16)], 0, as_rows(w_first)
    )
    (packed,) = kernel_call(
        pack_inputs,
        [shape((8, PACK, 128), bf16)],
        0,
        activations.reshape(128, 256),
        as_rows(w_second),
        cotangent,
        scratch=[
            pltpu.VMEM((128, 256), bf16),
            pltpu.VMEM((864, 256), bf16),
            pltpu.VMEM((1, 4, 4, 256), bf16),
            pltpu.VMEM((COT_ROWS, 128), bf16),
            pltpu.VMEM((8, W_ROWS, 128), bf16),
            pltpu.SemaphoreType.DMA((35,)),
        ],
        space=pltpu.HBM,
        target=pltpu.HBM,
        limit=60,
    )
    got = exchange(packed, FLT)
    pair = shape((ROWS, 128), f32)
    low, high, within, across, field, part = kernel_call(
        first_conv,
        [pair, pair, pair, pair, shape((1024, 256), bf16), shape((8, W_ROWS, 128), bf16)],
        2 * 1024 * 768 * 384,
        got,
        wide,
        scratch=[pltpu.VMEM((1024, 768), bf16)],
    )
    across, within = next_chip(across), swapped(within)
    (w2,) = kernel_call(gather_second, [shape((256, 1152), bf16)], 0, part, swapped(part))
    pre, partial = kernel_call(
        second_conv,
        [shape((512, 128), f32), shape((8, 512, 128), bf16)],
        2 * 256 * 1152 * 256,
        low,
        high,
        within,
        across,
        w2,
        scratch=[pltpu.VMEM((ROWS, 1152), bf16), pltpu.VMEM((2, ROWS, 128), f32)],
    )
    parts = exchange(partial, FLT)
    (err,) = kernel_call(second_error, [shape((128, 256), bf16)], 0, parts, got)
    across, within = next_chip(err), swapped(err)
    hidden, section_out = kernel_call(
        gather_hidden, [shape((1024, 256), bf16), shape((1, 4, 4, 256), f32)], 0, parts
    )
    window, kept, sent = kernel_call(
        backward,
        [shape((1024, 1152), bf16), shape((GRAD_PAD, 128), f32), shape((GRAD_PAD, 128), bf16)],
        2 * 1024 * 1152 * 256 + 2 * 256 * 256 * 384 * 6,
        err,
        within,
        across,
        w2,
        pre,
        field,
        hidden,
        scratch=[pltpu.VMEM((ROWS, 128), f32)],
    )
    came = swapped(sent)
    kept_in, sent_in = kernel_call(
        input_grad,
        [shape((2, 2, 128, 256), f32), shape((2, 2, 128, 256), bf16)],
        2 * 1024 * 1152 * 256,
        window,
        tall,
        scratch=[pltpu.VMEM((4, 2, 128, 256), f32)],
    )
    chunk = shape((16, GRAD_PAD // 16, 128), bf16)
    (mine,) = kernel_call(add_core, [chunk], 0, kept, came)
    mine, sent_in = lax.optimization_barrier((mine, sent_in))
    came_in = swapped(sent_in, "flt_x")
    (mine,) = kernel_call(add_chips, [chunk], 0, exchange(mine, CHIPS))
    kept_in, sent_in = kernel_call(
        add_pairs, [shape((2, 128, 256), f32), shape((2, 128, 256), bf16)], 0, kept_in, came_in
    )
    mine, sent_in = lax.optimization_barrier((mine, sent_in))
    came_in = mirrored(sent_in, "flt_x")
    mine = exchange(mine, CHIPS).reshape(GRAD_PAD, 128)
    kept_in, sent_in = kernel_call(
        add_halves, [shape((128, 256), f32), shape((128, 256), bf16)], 0, kept_in, came_in
    )
    came_in = swapped(sent_in, "flt_y")
    (grad_input,) = kernel_call(add_last, [shape((128, 256), f32)], 0, kept_in, came_in)
    mine, grad_input = lax.optimization_barrier((mine, grad_input))
    full = [shape((864, 256), f32)] * 2
    scratch = [pltpu.VMEM((864, 256), f32), pltpu.SemaphoreType.DMA((6,))]
    other = swapped(mine)
    grads = kernel_call(finish_own, full, 0, mine, scratch=scratch, target=pltpu.HBM)
    grads = kernel_call(
        finish_other, full, 0, other, *grads, scratch=scratch, target=pltpu.HBM, alias={1: 0, 2: 1}
    )
    return (section_out, grad_input.reshape(2, 8, 8, 256), *(as_filters(g) for g in grads))


def solution(mesh):
    torus = Mesh(mesh.devices.reshape(8, 2, 2, 4, 2), (*SP, *FLT))
    whole = P(FLT, None, None, None, None)
    rows = P(SP, FLT, None, None)
    return jax.shard_map(
        per_device,
        mesh=torus,
        in_specs=(rows, whole, whole, rows),
        out_specs=(rows, rows, whole, whole),
        check_vma=False,
    )
```

```python
import jax
import jax.numpy as jnp
from jax import lax
from jax.experimental import pallas as pl
from jax.experimental.pallas import tpu as pltpu
from jax.sharding import Mesh
from jax.sharding import PartitionSpec as P

SP = ("sp_z", "sp_y", "core")
CHIPS = ("sp_z", "sp_y")
FLT = ("flt_x", "flt_y")
bf16, f32 = jnp.bfloat16, jnp.float32

ROWS = 256
X_ROWS, COT_ROWS, W_ROWS = 256, 32, 128
PACK = X_ROWS + COT_ROWS + W_ROWS
GRAD_ROWS, GRAD_PAD = 1728, 1792
NT = (((1,), (1,)), ((), ()))
NN = (((1,), (0,)), ((), ()))
TN = (((0,), (0,)), ((), ()))


def dot(a, b, dims):
    return lax.dot_general(a, b, dims, preferred_element_type=f32)


def kernel_call(
    body, outs, flops, *args, scratch=(), space=pltpu.VMEM, target=pltpu.VMEM, limit=16, alias={}
):
    spaces = [pltpu.HBM if i in alias else space for i in range(len(args))]
    moved = sum(a.size * a.dtype.itemsize for a in (*args, *outs))
    return pl.pallas_call(
        body,
        out_shape=outs,
        in_specs=[pl.BlockSpec(memory_space=s) for s in spaces],
        out_specs=[pl.BlockSpec(memory_space=target)] * len(outs),
        scratch_shapes=scratch,
        input_output_aliases=alias,
        compiler_params=pltpu.CompilerParams(vmem_limit_bytes=limit << 20),
        cost_estimate=pl.CostEstimate(flops=flops, bytes_accessed=moved, transcendentals=0),
    )(*args)


def shape(dims, dtype):
    return jax.ShapeDtypeStruct(dims, dtype)


def lanes(rows):
    return lax.broadcasted_iota(jnp.int32, (rows, 128), 1)


def cells(rows):
    return lax.rem(lax.broadcasted_iota(jnp.int32, (rows, 128), 0), 8)


def before(v):
    return jnp.where(cells(v.shape[0]) == 0, 0.0, pltpu.roll(v, 1, 0))


def after(v):
    return jnp.where(cells(v.shape[0]) == 7, 0.0, pltpu.roll(v, v.shape[0] - 1, 0))


def rotated(v, slots):
    by = (32 * slots) % 128
    return pltpu.roll(v, by, 1) if by else v


def three(a, b, c):
    lane = lanes(a.shape[0])
    return jnp.where(lane < 32, a, jnp.where(lane < 64, b, jnp.where(lane < 96, c, 0.0)))


def row_down(v):
    return jnp.concatenate([jnp.zeros((8, v.shape[1]), v.dtype), v[:-8]], 0)


def row_up(v):
    return jnp.concatenate([v[8:], jnp.zeros((8, v.shape[1]), v.dtype)], 0)


def tap_sum(first, middle, last):
    lane = lanes(ROWS)
    t = jnp.where(lane < 32, first, jnp.where(lane < 64, middle, last))
    return t + rotated(t, -1) + rotated(t, -2)


def pair_of(pieces):
    lane = lanes(ROWS)
    v = pieces[0]
    for slot in (1, 2, 3):
        v = jnp.where(lane < 32 * slot, v, rotated(pieces[slot], slot))
    return v


def sigmoid(v):
    return jax.nn.sigmoid(v)


def silu_slope(v):
    s = sigmoid(v)
    return s * (1.0 + v * (1.0 - s))


def pack_inputs(x_far, w_far, cot_far, out, x, w, cot_near, cot, blocks, sems):
    loads = [
        pltpu.make_async_copy(x_far, x, sems.at[0]),
        pltpu.make_async_copy(cot_far, cot_near, sems.at[1]),
        pltpu.make_async_copy(w_far, w, sems.at[2]),
    ]
    for copy in loads:
        copy.start()
    sent = []

    def send(source, f, at, size):
        target = out.at[f, pl.ds(at, size), :]
        copy = pltpu.make_async_copy(source, target, sems.at[3 + len(sent)])
        copy.start()
        sent.append(copy)

    loads[0].wait()
    for f in range(8):
        for h in (0, 1):
            send(x.at[:, pl.ds(h * 128, 128)], f, h * 128, 128)
    loads[1].wait()
    for h in (0, 1):
        rows = [cot_near[0, i, :, h * 128 : h * 128 + 128].astype(f32) for i in range(4)]
        cot[h * 16 : h * 16 + 16, :] = jnp.concatenate(rows, 0).astype(bf16)
    for f in range(8):
        send(cot, f, X_ROWS, COT_ROWS)
    loads[2].wait()
    first_core = lax.axis_index("core") == 0
    lane = lanes(32)

    def block(k, m, h):
        at = pl.multiple_of(96 * k, 32)
        taps = [w[pl.ds(at + 32 * t, 32), h * 128 : h * 128 + 128].astype(f32) for t in range(3)]
        return three(*(rotated(taps[t], t - m) for t in range(3)))

    for h in (0, 1):
        for b in range(4):
            extra = w[(12 + min(b, 2)) * 32 : (13 + min(b, 2)) * 32, h * 128 : h * 128 + 128]
            extra = extra.astype(f32)
            for m in range(4):
                v = block(jnp.where(first_core, b, b + 5), m, h)
                v = jnp.where(lane < 96, v, rotated(extra, 3 - m))
                blocks[4 * h + m, b * 32 : b * 32 + 32, :] = v.astype(bf16)
        for m in range(4):
            send(blocks.at[4 * h + m], 4 * h + m, X_ROWS + COT_ROWS, W_ROWS)
    for copy in sent:
        copy.wait()


def prepare_first(w, wide, tall):
    zero = jnp.zeros((32, 256), bf16)
    for k0 in range(3):
        for k1 in range(3):
            for t in range(4):
                at = ((k0 * 3 + k1) * 3 + t) * 32
                v = w[at : at + 32, :] if t < 3 else zero
                wide[k0 * 128 + t * 32 : k0 * 128 + t * 32 + 32, k1 * 256 : k1 * 256 + 256] = v
                row = (k0 * 3 + k1) * 128 + t * 32
                tall[row : row + 32, :] = v


def first_conv(got, wide, low, high, within, across, field, window):
    for g in range(8):
        at = ROWS + g * W_ROWS
        within[at : at + W_ROWS, :] = got[g, X_ROWS + COT_ROWS :, :].astype(f32)
    parts = {}
    for h in (0, 1):
        for p in (0, 1):
            blocks = ([], [])
            for g in range(8):
                at = h * 128 + p * 64
                v = got[g, at : at + 64, :].astype(f32).reshape(4, 2, 8, 128)
                for par in (0, 1):
                    blocks[par].append(v[:, par].reshape(32, 128))
            for par in (0, 1):
                parts[p, par, h] = jnp.concatenate(blocks[par], 0)
    for p in (0, 1):
        for h in (0, 1):
            even, odd = parts[p, 0, h], parts[p, 1, h]
            sources = ((row_down(odd), even, odd), (even, odd, row_up(even)))
            for par in (0, 1):
                at = (2 * p + par) * ROWS
                for k1 in range(3):
                    lane = k1 * 256 + h * 128
                    window[at : at + ROWS, lane : lane + 128] = sources[par][k1].astype(bf16)
                field[at : at + ROWS, h * 128 : h * 128 + 128] = sources[par][1].astype(bf16)
    sums = [dot(window[i * ROWS : i * ROWS + ROWS, :], wide[...], NT) for i in range(4)]
    pieces = []
    for plane in range(4):
        for par in (0, 1):
            terms = [
                sums[2 * p + par][:, k0 * 128 : k0 * 128 + 128]
                for p in (0, 1)
                for k0 in range(3)
                if p - k0 + 2 == plane
            ]
            v = terms[0] if len(terms) == 1 else terms[0] + terms[1]
            pieces.append(tap_sum(before(v), v, after(v)))
    a, b = pair_of(pieces[:4]), pair_of(pieces[4:])
    first_core = lax.axis_index("core") == 0
    low[...] = a
    high[...] = b
    within[:ROWS, :] = jnp.where(first_core, b, a)
    across[...] = jnp.where(first_core, a, b)


def gather_second(got, within, w2):
    first_core = lax.axis_index("core") == 0
    for g in range(8):
        row = slice(g * 32, g * 32 + 32)
        blocks = []
        for b in range(4):
            at = X_ROWS + COT_ROWS + b * 32
            x = got[g, at : at + 32, :].astype(f32)
            at = ROWS + g * W_ROWS + b * 32
            y = within[at : at + 32, :]
            early, late = jnp.where(first_core, x, y), jnp.where(first_core, y, x)
            w2[row, b * 128 : b * 128 + 128] = early.astype(bf16)
            w2[row, (b + 5) * 128 : (b + 6) * 128] = late.astype(bf16)
            blocks.append(early)
        v = three(*(rotated(blocks[t], t - 3) for t in range(3)))
        w2[row, 512:640] = v.astype(bf16)


def at_first_plane():
    return sum(lax.axis_index(name) for name in SP) == 0


def without_edge(v):
    return jnp.where(jnp.logical_and(at_first_plane(), lanes(ROWS) < 64), 0.0, v)


def below_above(within, across):
    first_core = lax.axis_index("core") == 0
    a, b = within[: across.shape[0], :], across[...]
    return jnp.where(first_core, b, a), jnp.where(first_core, a, b)


def second_conv(low, high, within, across, w2, pre, out, window, full):
    below, above = below_above(within, across)
    pairs = [low[...] + below, high[...] + above]
    pre[0:ROWS, :] = pairs[0]
    pre[ROWS:, :] = pairs[1]
    hidden = [v * sigmoid(v) for v in pairs]
    own = jnp.where(lanes(ROWS) < 64, rotated(hidden[0], 2), rotated(hidden[1], 2)).astype(bf16)
    for g in range(8):
        out[g, ROWS:, :] = own
    hidden[0] = without_edge(hidden[0])
    hidden = [v.astype(bf16).astype(f32) for v in hidden]
    shifted = [(before(v), v, after(v)) for v in hidden]
    for plane in range(3):
        pair = shifted[plane // 2]
        for par in (0, 1):
            slot = (plane % 2) * 2 + par
            v = three(*(rotated(pair[t], t - slot) for t in range(3)))
            at = (plane * 3 + 1 + par) * 128
            window[:, at : at + 128] = v.astype(bf16)
            if par:
                window[:, plane * 384 : plane * 384 + 128] = row_down(v).astype(bf16)
    total = dot(window[...], w2[...], NT)
    for h in (0, 1):
        full[h] = total[:, h * 128 : h * 128 + 128]
        v = full[h, pl.ds(0, 128, 2), :].astype(bf16)
        for g in range(8):
            out[g, h * 128 : h * 128 + 128, :] = v


def gather_hidden(parts, field, section):
    flt = lax.axis_index("flt_x") * 2 + lax.axis_index("flt_y")
    for h in (0, 1):
        row = pl.ds(pl.multiple_of(h * 128 + flt * 16, 16), 16)
        v = parts[0, row, :].astype(f32)
        for g in range(1, 8):
            v = v + parts[g, row, :].astype(f32)
        v = v * sigmoid(v)
        for i in range(4):
            section[0, i, :, h * 128 : h * 128 + 128] = v[4 * i : 4 * i + 4]
    lane = lanes(ROWS)
    for h in (0, 1):
        blocks = [parts[4 * h + m, ROWS:, :].astype(f32) for m in range(4)]
        for slot in range(4):
            v = rotated(blocks[0], -slot)
            for m in (1, 2, 3):
                v = jnp.where(lane < 32 * m, v, rotated(blocks[m], m - slot))
            field[slot * ROWS : slot * ROWS + ROWS, h * 128 : h * 128 + 128] = v.astype(bf16)


def second_error(parts, got, err):
    for h in (0, 1):
        lane = slice(h * 128, h * 128 + 128)
        row = slice(h * 128, h * 128 + 128)
        v = parts[0, row, :].astype(f32)
        for g in range(1, 8):
            v = v + parts[g, row, :].astype(f32)
        cot = jnp.concatenate(
            [got[g, X_ROWS + h * 16 : X_ROWS + h * 16 + 16, :].astype(f32) for g in range(8)], 0
        )
        err[:, lane] = (cot * silu_slope(v)).astype(bf16)


def spread_out(err, full):
    full[...] = jnp.zeros((ROWS, 128), f32)
    full[pl.ds(0, 128, 2), :] = err
    return full[...]


def second_grad(spread, hidden):
    flt = lax.axis_index("flt_x") * 2 + lax.axis_index("flt_y")
    turn = lax.rem(8 - flt, 4) * 32
    plain, ahead = [], []
    for left, right in spread:
        v = pltpu.roll(jnp.where(flt < 4, left, right), turn, 1)
        v = three(after(v), rotated(v, 1), rotated(before(v), 2))
        plain.append(v.astype(bf16))
        ahead.append(row_up(v).astype(bf16))
    grads = []
    for k0 in range(3):
        q = 1 if k0 == 0 else 0
        for k1 in range(3):
            at = ((1 if k0 == 1 else 3) - (1 if k1 == 1 else 0)) * ROWS
            errs = (ahead if k1 == 0 else plain)[q]
            grads.append(dot(errs, hidden[at : at + ROWS, :], TN))
    return grads


def backward(own, within, across, w2, pre, field, hidden, window, kept, sent, full):
    below, above = below_above(within, across)
    spread, ahead, halves = [], [], []
    for err in (below, own[...], above):
        both = [spread_out(err[:, h * 128 : h * 128 + 128].astype(f32), full) for h in (0, 1)]
        halves.append(both)
        v = jnp.concatenate(both, 1)
        spread.append(v.astype(bf16))
        ahead.append(row_up(v).astype(bf16))
    pieces = []
    for plane in range(4):
        both, extra = None, None
        for q, k0 in (((0, 2), (1, 0)), ((1, 1),), ((1, 2), (2, 0)), ((2, 1),))[plane]:
            at = k0 * 384
            a = dot(spread[q], w2[:, at + 128 : at + 384], NN)
            b = dot(ahead[q], w2[:, at : at + 128], NN)
            both = a if both is None else both + a
            extra = b if extra is None else extra + b
        for v in (both[:, :128], both[:, 128:] + extra):
            pieces.append(tap_sum(after(v), v, before(v)))
    errs = [pair_of(pieces[:4]), pair_of(pieces[4:])]
    errs = [errs[i] * silu_slope(pre[i * ROWS : i * ROWS + ROWS, :]) for i in (0, 1)]
    errs[0] = without_edge(errs[0])
    errs = [v.astype(bf16).astype(f32) for v in errs]
    shifted = [(after(v), v, before(v)) for v in errs]
    for plane in range(4):
        pair = shifted[plane // 2]
        taps = [
            three(*(rotated(pair[t], t - (plane % 2) * 2 - par) for t in range(3)))
            for par in (0, 1)
        ]
        even, odd = taps
        sources = ((odd, even, row_down(odd)), (row_up(even), odd, even))
        for par in (0, 1):
            for k1 in range(3):
                v = sources[par][k1].astype(bf16)
                for k0 in range(3):
                    target = plane + k0 - 1
                    if target in (1, 2):
                        at = (2 * (target - 1) + par) * ROWS
                        lane = (k0 * 3 + k1) * 128
                        window[at : at + ROWS, lane : lane + 128] = v
    first = dot(window[...], field[...], TN)
    second = second_grad(halves[1:], hidden)
    first_core = lax.axis_index("core") == 0
    for h in (0, 1):
        lane = slice(h * 128, h * 128 + 128)
        for k in range(9):
            at = h * 864 + k * 96
            a, b = first[k * 128 : k * 128 + 96, lane], second[k][:96, lane]
            kept[at : at + 96, :] = jnp.where(first_core, a, b)
            sent[at : at + 96, :] = jnp.where(first_core, b, a).astype(bf16)
    kept[GRAD_ROWS:, :] = jnp.zeros((GRAD_PAD - GRAD_ROWS, 128), f32)
    sent[GRAD_ROWS:, :] = jnp.zeros((GRAD_PAD - GRAD_ROWS, 128), bf16)


def input_grad(window, tall, kept, sent, blocks):
    for p in (0, 1):
        even = dot(window[2 * p * ROWS : (2 * p + 1) * ROWS, :], tall[...], NN)
        odd = dot(window[(2 * p + 1) * ROWS : (2 * p + 2) * ROWS, :], tall[...], NN)
        for g in range(8):
            a = even[g * 32 : g * 32 + 32].reshape(4, 1, 8, 256)
            b = odd[g * 32 : g * 32 + 32].reshape(4, 1, 8, 256)
            v = jnp.concatenate([a, b], 1).reshape(64, 256)
            blocks[g // 2, g % 2, p * 64 : p * 64 + 64, :] = v
    x = lax.axis_index("flt_x")
    partner = x + 1 - 2 * lax.rem(x, 2)
    kept[0] = blocks[x]
    kept[1] = blocks[3 - x]
    sent[0] = blocks[partner].astype(bf16)
    sent[1] = blocks[3 - partner].astype(bf16)


def add_pairs(kept, came, still, sent):
    still[...] = kept[0] + came[0].astype(f32)
    sent[...] = (kept[1] + came[1].astype(f32)).astype(bf16)


def add_halves(kept, came, still, sent):
    y = lax.axis_index("flt_y")
    still[...] = kept[y] + came[y].astype(f32)
    sent[...] = (kept[1 - y] + came[1 - y].astype(f32)).astype(bf16)


def add_last(kept, came, out):
    out[...] = kept[...] + came[...].astype(f32)


def add_core(kept, came, out):
    v = kept[...] + came[...].astype(f32)
    out[...] = v.astype(bf16).reshape(16, GRAD_PAD // 16, 128)


def add_chips(parts, out):
    v = parts[0].astype(f32)
    for i in range(1, 16):
        v = v + parts[i].astype(f32)
    v = v.astype(bf16)
    for i in range(16):
        out[i] = v


def finish_part(rows, first, second, near, sems, to_first):
    pieces = [pl.ds(i * 144, 144) for i in range(6)]
    for i, piece in enumerate(pieces):
        for h in (0, 1):
            at = h * 864 + i * 144
            near[piece, h * 128 : h * 128 + 128] = rows[at : at + 144, :].astype(f32)
        for target, wanted in ((first, to_first), (second, jnp.logical_not(to_first))):

            @pl.when(wanted)
            def _(target=target):
                pltpu.make_async_copy(near.at[piece], target.at[piece], sems.at[i]).start()

    for target, wanted in ((first, to_first), (second, jnp.logical_not(to_first))):

        @pl.when(wanted)
        def _(target=target):
            for i, piece in enumerate(pieces):
                pltpu.make_async_copy(near.at[piece], target.at[piece], sems.at[i]).wait()


def finish_own(rows, first, second, near, sems):
    finish_part(rows, first, second, near, sems, lax.axis_index("core") == 0)


def finish_other(rows, first_in, second_in, first, second, near, sems):
    finish_part(rows, first, second, near, sems, lax.axis_index("core") == 1)


def exchange(v, axis):
    return lax.all_to_all(v, axis, 0, 0, tiled=True)


def swapped(v, axis="core"):
    n = lax.axis_size(axis)
    return lax.ppermute(v, axis, [(i, i ^ 1) for i in range(n)])


def mirrored(v, axis):
    n = lax.axis_size(axis)
    return lax.ppermute(v, axis, [(i, n - 1 - i) for i in range(n)])


def next_chip(v):
    pairs = [(i, i + 1) for i in range(1, lax.axis_size(SP) - 1, 2)]
    return lax.ppermute(v, SP, pairs + [(b, a) for a, b in pairs])


def as_rows(w):
    return jnp.transpose(w, (1, 2, 3, 0, 4)).reshape(864, 256)


def as_filters(rows):
    return jnp.transpose(rows.reshape(3, 3, 3, 32, 256), (3, 0, 1, 2, 4))


def per_device(activations, w_first, w_second, cotangent):
    wide, tall = kernel_call(
        prepare_first, [shape((384, 768), bf16), shape((1152, 256), bf16)], 0, as_rows(w_first)
    )
    (packed,) = kernel_call(
        pack_inputs,
        [shape((8, PACK, 128), bf16)],
        0,
        activations.reshape(128, 256),
        as_rows(w_second),
        cotangent,
        scratch=[
            pltpu.VMEM((128, 256), bf16),
            pltpu.VMEM((864, 256), bf16),
            pltpu.VMEM((1, 4, 4, 256), bf16),
            pltpu.VMEM((COT_ROWS, 128), bf16),
            pltpu.VMEM((8, W_ROWS, 128), bf16),
            pltpu.SemaphoreType.DMA((35,)),
        ],
        space=pltpu.HBM,
        target=pltpu.HBM,
        limit=60,
    )
    got = exchange(packed, FLT)
    pair = shape((ROWS, 128), f32)
    with_filters = shape((ROWS + 8 * W_ROWS, 128), f32)
    low, high, within, across, field = kernel_call(
        first_conv,
        [pair, pair, with_filters, pair, shape((1024, 256), bf16)],
        2 * 1024 * 768 * 384,
        got,
        wide,
        scratch=[pltpu.VMEM((1024, 768), bf16)],
    )
    across, within = next_chip(across), swapped(within)
    (w2,) = kernel_call(gather_second, [shape((256, 1152), bf16)], 0, got, within)
    pre, partial = kernel_call(
        second_conv,
        [shape((512, 128), f32), shape((8, 512, 128), bf16)],
        2 * 256 * 1152 * 256,
        low,
        high,
        within,
        across,
        w2,
        scratch=[pltpu.VMEM((ROWS, 1152), bf16), pltpu.VMEM((2, ROWS, 128), f32)],
    )
    parts = exchange(partial, FLT)
    (err,) = kernel_call(second_error, [shape((128, 256), bf16)], 0, parts, got)
    across, within = next_chip(err), swapped(err)
    hidden, section_out = kernel_call(
        gather_hidden, [shape((1024, 256), bf16), shape((1, 4, 4, 256), f32)], 0, parts
    )
    window, kept, sent = kernel_call(
        backward,
        [shape((1024, 1152), bf16), shape((GRAD_PAD, 128), f32), shape((GRAD_PAD, 128), bf16)],
        2 * 1024 * 1152 * 256 + 2 * 256 * 256 * 384 * 6,
        err,
        within,
        across,
        w2,
        pre,
        field,
        hidden,
        scratch=[pltpu.VMEM((ROWS, 128), f32)],
    )
    came = swapped(sent)
    kept_in, sent_in = kernel_call(
        input_grad,
        [shape((2, 2, 128, 256), f32), shape((2, 2, 128, 256), bf16)],
        2 * 1024 * 1152 * 256,
        window,
        tall,
        scratch=[pltpu.VMEM((4, 2, 128, 256), f32)],
    )
    chunk = shape((16, GRAD_PAD // 16, 128), bf16)
    (mine,) = kernel_call(add_core, [chunk], 0, kept, came)
    mine, sent_in = lax.optimization_barrier((mine, sent_in))
    came_in = swapped(sent_in, "flt_x")
    (mine,) = kernel_call(add_chips, [chunk], 0, exchange(mine, CHIPS))
    kept_in, sent_in = kernel_call(
        add_pairs, [shape((2, 128, 256), f32), shape((2, 128, 256), bf16)], 0, kept_in, came_in
    )
    mine, sent_in = lax.optimization_barrier((mine, sent_in))
    came_in = mirrored(sent_in, "flt_x")
    mine = exchange(mine, CHIPS).reshape(GRAD_PAD, 128)
    kept_in, sent_in = kernel_call(
        add_halves, [shape((128, 256), f32), shape((128, 256), bf16)], 0, kept_in, came_in
    )
    came_in = swapped(sent_in, "flt_y")
    (grad_input,) = kernel_call(add_last, [shape((128, 256), f32)], 0, kept_in, came_in)
    mine, grad_input = lax.optimization_barrier((mine, grad_input))
    full = [shape((864, 256), f32)] * 2
    scratch = [pltpu.VMEM((864, 256), f32), pltpu.SemaphoreType.DMA((6,))]
    other = swapped(mine)
    grads = kernel_call(finish_own, full, 0, mine, scratch=scratch, target=pltpu.HBM)
    grads = kernel_call(
        finish_other, full, 0, other, *grads, scratch=scratch, target=pltpu.HBM, alias={1: 0, 2: 1}
    )
    return (section_out, grad_input.reshape(2, 8, 8, 256), *(as_filters(g) for g in grads))


def solution(mesh):
    torus = Mesh(mesh.devices.reshape(8, 2, 2, 4, 2), (*SP, *FLT))
    whole = P(FLT, None, None, None, None)
    rows = P(SP, FLT, None, None)
    return jax.shard_map(
        per_device,
        mesh=torus,
        in_specs=(rows, whole, whole, rows),
        out_specs=(rows, rows, whole, whole),
        check_vma=False,
    )
```

```python
import jax
import jax.numpy as jnp
from jax import lax
from jax.experimental import pallas as pl
from jax.experimental.pallas import tpu as pltpu
from jax.sharding import Mesh
from jax.sharding import PartitionSpec as P

SP = ("sp_z", "sp_y", "core")
CHIPS = ("sp_z", "sp_y")
FLT = ("flt_x", "flt_y")
bf16, f32 = jnp.bfloat16, jnp.float32

ROWS = 256
X_ROWS, COT_ROWS, W_ROWS = 256, 32, 128
PACK = X_ROWS + COT_ROWS + W_ROWS
GRAD_ROWS, GRAD_PAD = 1728, 1792
NT = (((1,), (1,)), ((), ()))
NN = (((1,), (0,)), ((), ()))
TN = (((0,), (0,)), ((), ()))


def dot(a, b, dims):
    return lax.dot_general(a, b, dims, preferred_element_type=f32)


def kernel_call(
    body, outs, flops, *args, scratch=(), space=pltpu.VMEM, target=pltpu.VMEM, limit=16, alias={}
):
    spaces = [pltpu.HBM if i in alias else space for i in range(len(args))]
    moved = sum(a.size * a.dtype.itemsize for a in (*args, *outs))
    return pl.pallas_call(
        body,
        out_shape=outs,
        in_specs=[pl.BlockSpec(memory_space=s) for s in spaces],
        out_specs=[pl.BlockSpec(memory_space=target)] * len(outs),
        scratch_shapes=scratch,
        input_output_aliases=alias,
        compiler_params=pltpu.CompilerParams(vmem_limit_bytes=limit << 20),
        cost_estimate=pl.CostEstimate(flops=flops, bytes_accessed=moved, transcendentals=0),
    )(*args)


def shape(dims, dtype):
    return jax.ShapeDtypeStruct(dims, dtype)


def lanes(rows):
    return lax.broadcasted_iota(jnp.int32, (rows, 128), 1)


def cells(rows):
    return lax.rem(lax.broadcasted_iota(jnp.int32, (rows, 128), 0), 8)


def before(v):
    return jnp.where(cells(v.shape[0]) == 0, 0.0, pltpu.roll(v, 1, 0))


def after(v):
    return jnp.where(cells(v.shape[0]) == 7, 0.0, pltpu.roll(v, v.shape[0] - 1, 0))


def rotated(v, slots):
    by = (32 * slots) % 128
    return pltpu.roll(v, by, 1) if by else v


def three(a, b, c):
    lane = lanes(a.shape[0])
    return jnp.where(lane < 32, a, jnp.where(lane < 64, b, jnp.where(lane < 96, c, 0.0)))


def row_down(v):
    return jnp.concatenate([jnp.zeros((8, v.shape[1]), v.dtype), v[:-8]], 0)


def row_up(v):
    return jnp.concatenate([v[8:], jnp.zeros((8, v.shape[1]), v.dtype)], 0)


def tap_sum(first, middle, last):
    lane = lanes(ROWS)
    t = jnp.where(lane < 32, first, jnp.where(lane < 64, middle, last))
    return t + rotated(t, -1) + rotated(t, -2)


def pair_of(pieces):
    lane = lanes(ROWS)
    v = pieces[0]
    for slot in (1, 2, 3):
        v = jnp.where(lane < 32 * slot, v, rotated(pieces[slot], slot))
    return v


def sigmoid(v):
    return jax.nn.sigmoid(v)


def silu_slope(v):
    s = sigmoid(v)
    return s * (1.0 + v * (1.0 - s))


def pack_inputs(x_far, w_far, cot_far, out, x, w, cot_near, cot, blocks, sems):
    loads = [
        pltpu.make_async_copy(x_far, x, sems.at[0]),
        pltpu.make_async_copy(cot_far, cot_near, sems.at[1]),
        pltpu.make_async_copy(w_far, w, sems.at[2]),
    ]
    for copy in loads:
        copy.start()
    sent = []

    def send(source, f, at, size):
        target = out.at[f, pl.ds(at, size), :]
        copy = pltpu.make_async_copy(source, target, sems.at[3 + len(sent)])
        copy.start()
        sent.append(copy)

    loads[0].wait()
    for f in range(8):
        for h in (0, 1):
            send(x.at[:, pl.ds(h * 128, 128)], f, h * 128, 128)
    loads[1].wait()
    for h in (0, 1):
        rows = [cot_near[0, i, :, h * 128 : h * 128 + 128].astype(f32) for i in range(4)]
        cot[h * 16 : h * 16 + 16, :] = jnp.concatenate(rows, 0).astype(bf16)
    for f in range(8):
        send(cot, f, X_ROWS, COT_ROWS)
    loads[2].wait()
    first_core = lax.axis_index("core") == 0
    lane = lanes(32)

    def block(k, m, h):
        at = pl.multiple_of(96 * k, 32)
        taps = [w[pl.ds(at + 32 * t, 32), h * 128 : h * 128 + 128].astype(f32) for t in range(3)]
        return three(*(rotated(taps[t], t - m) for t in range(3)))

    for h in (0, 1):
        for b in range(4):
            extra = w[(12 + min(b, 2)) * 32 : (13 + min(b, 2)) * 32, h * 128 : h * 128 + 128]
            extra = extra.astype(f32)
            for m in range(4):
                v = block(jnp.where(first_core, b, b + 5), m, h)
                v = jnp.where(lane < 96, v, rotated(extra, 3 - m))
                blocks[4 * h + m, b * 32 : b * 32 + 32, :] = v.astype(bf16)
        for m in range(4):
            send(blocks.at[4 * h + m], 4 * h + m, X_ROWS + COT_ROWS, W_ROWS)
    for copy in sent:
        copy.wait()


def prepare_first(w, wide, tall):
    zero = jnp.zeros((32, 256), bf16)
    for k0 in range(3):
        for k1 in range(3):
            for t in range(4):
                at = ((k0 * 3 + k1) * 3 + t) * 32
                v = w[at : at + 32, :] if t < 3 else zero
                wide[k0 * 128 + t * 32 : k0 * 128 + t * 32 + 32, k1 * 256 : k1 * 256 + 256] = v
                row = (k0 * 3 + k1) * 128 + t * 32
                tall[row : row + 32, :] = v


def first_conv(got, wide, low, high, within, across, field, part, window):
    part[...] = got[:, X_ROWS + COT_ROWS :, :]
    parts = {}
    for h in (0, 1):
        for p in (0, 1):
            blocks = ([], [])
            for g in range(8):
                at = h * 128 + p * 64
                v = got[g, at : at + 64, :].astype(f32).reshape(4, 2, 8, 128)
                for par in (0, 1):
                    blocks[par].append(v[:, par].reshape(32, 128))
            for par in (0, 1):
                parts[p, par, h] = jnp.concatenate(blocks[par], 0)
    for p in (0, 1):
        for h in (0, 1):
            even, odd = parts[p, 0, h], parts[p, 1, h]
            sources = ((row_down(odd), even, odd), (even, odd, row_up(even)))
            for par in (0, 1):
                at = (2 * p + par) * ROWS
                for k1 in range(3):
                    lane = k1 * 256 + h * 128
                    window[at : at + ROWS, lane : lane + 128] = sources[par][k1].astype(bf16)
                field[at : at + ROWS, h * 128 : h * 128 + 128] = sources[par][1].astype(bf16)
    sums = [dot(window[i * ROWS : i * ROWS + ROWS, :], wide[...], NT) for i in range(4)]
    pieces = []
    for plane in range(4):
        for par in (0, 1):
            terms = [
                sums[2 * p + par][:, k0 * 128 : k0 * 128 + 128]
                for p in (0, 1)
                for k0 in range(3)
                if p - k0 + 2 == plane
            ]
            v = terms[0] if len(terms) == 1 else terms[0] + terms[1]
            pieces.append(tap_sum(before(v), v, after(v)))
    a, b = pair_of(pieces[:4]), pair_of(pieces[4:])
    first_core = lax.axis_index("core") == 0
    low[...] = a
    high[...] = b
    within[...] = jnp.where(first_core, b, a)
    across[...] = jnp.where(first_core, a, b)


def gather_second(own, other, w2):
    first_core = lax.axis_index("core") == 0
    for g in range(8):
        row = slice(g * 32, g * 32 + 32)
        blocks = []
        for b in range(4):
            at = slice(b * 32, b * 32 + 32)
            x, y = own[g, at, :].astype(f32), other[g, at, :].astype(f32)
            early, late = jnp.where(first_core, x, y), jnp.where(first_core, y, x)
            w2[row, b * 128 : b * 128 + 128] = early.astype(bf16)
            w2[row, (b + 5) * 128 : (b + 6) * 128] = late.astype(bf16)
            blocks.append(early)
        v = three(*(rotated(blocks[t], t - 3) for t in range(3)))
        w2[row, 512:640] = v.astype(bf16)


def at_first_plane():
    return sum(lax.axis_index(name) for name in SP) == 0


def without_edge(v):
    return jnp.where(jnp.logical_and(at_first_plane(), lanes(ROWS) < 64), 0.0, v)


def below_above(within, across):
    first_core = lax.axis_index("core") == 0
    a, b = within[...], across[...]
    return jnp.where(first_core, b, a), jnp.where(first_core, a, b)


def second_conv(low, high, within, across, w2, pre, out, window, full):
    below, above = below_above(within, across)
    pairs = [low[...] + below, high[...] + above]
    pre[0:ROWS, :] = pairs[0]
    pre[ROWS:, :] = pairs[1]
    hidden = [v * sigmoid(v) for v in pairs]
    own = jnp.where(lanes(ROWS) < 64, rotated(hidden[0], 2), rotated(hidden[1], 2)).astype(bf16)
    for g in range(8):
        out[g, ROWS:, :] = own
    hidden[0] = without_edge(hidden[0])
    hidden = [v.astype(bf16).astype(f32) for v in hidden]
    shifted = [(before(v), v, after(v)) for v in hidden]
    for plane in range(3):
        pair = shifted[plane // 2]
        for par in (0, 1):
            slot = (plane % 2) * 2 + par
            v = three(*(rotated(pair[t], t - slot) for t in range(3)))
            at = (plane * 3 + 1 + par) * 128
            window[:, at : at + 128] = v.astype(bf16)
            if par:
                window[:, plane * 384 : plane * 384 + 128] = row_down(v).astype(bf16)
    total = dot(window[...], w2[...], NT)
    for h in (0, 1):
        full[h] = total[:, h * 128 : h * 128 + 128]
        v = full[h, pl.ds(0, 128, 2), :].astype(bf16)
        for g in range(8):
            out[g, h * 128 : h * 128 + 128, :] = v


def gather_hidden(parts, field, section):
    flt = lax.axis_index("flt_x") * 2 + lax.axis_index("flt_y")
    for h in (0, 1):
        row = pl.ds(pl.multiple_of(h * 128 + flt * 16, 16), 16)
        v = parts[0, row, :].astype(f32)
        for g in range(1, 8):
            v = v + parts[g, row, :].astype(f32)
        v = v * sigmoid(v)
        for i in range(4):
            section[0, i, :, h * 128 : h * 128 + 128] = v[4 * i : 4 * i + 4]
    lane = lanes(ROWS)
    for h in (0, 1):
        blocks = [parts[4 * h + m, ROWS:, :].astype(f32) for m in range(4)]
        for slot in range(4):
            v = rotated(blocks[0], -slot)
            for m in (1, 2, 3):
                v = jnp.where(lane < 32 * m, v, rotated(blocks[m], m - slot))
            field[slot * ROWS : slot * ROWS + ROWS, h * 128 : h * 128 + 128] = v.astype(bf16)


def second_error(parts, got, err):
    for h in (0, 1):
        lane = slice(h * 128, h * 128 + 128)
        row = slice(h * 128, h * 128 + 128)
        v = parts[0, row, :].astype(f32)
        for g in range(1, 8):
            v = v + parts[g, row, :].astype(f32)
        cot = jnp.concatenate(
            [got[g, X_ROWS + h * 16 : X_ROWS + h * 16 + 16, :].astype(f32) for g in range(8)], 0
        )
        err[:, lane] = (cot * silu_slope(v)).astype(bf16)


def spread_out(err, full):
    full[...] = jnp.zeros((ROWS, 128), f32)
    full[pl.ds(0, 128, 2), :] = err
    return full[...]


def second_grad(spread, hidden):
    flt = lax.axis_index("flt_x") * 2 + lax.axis_index("flt_y")
    turn = lax.rem(8 - flt, 4) * 32
    plain, ahead = [], []
    for left, right in spread:
        v = pltpu.roll(jnp.where(flt < 4, left, right), turn, 1)
        v = three(after(v), rotated(v, 1), rotated(before(v), 2))
        plain.append(v.astype(bf16))
        ahead.append(row_up(v).astype(bf16))
    grads = []
    for k0 in range(3):
        q = 1 if k0 == 0 else 0
        for k1 in range(3):
            at = ((1 if k0 == 1 else 3) - (1 if k1 == 1 else 0)) * ROWS
            errs = (ahead if k1 == 0 else plain)[q]
            grads.append(dot(errs, hidden[at : at + ROWS, :], TN))
    return grads


def backward(own, within, across, w2, pre, field, hidden, window, kept, sent, full):
    below, above = below_above(within, across)
    spread, ahead, halves = [], [], []
    for err in (below, own[...], above):
        both = [spread_out(err[:, h * 128 : h * 128 + 128].astype(f32), full) for h in (0, 1)]
        halves.append(both)
        v = jnp.concatenate(both, 1)
        spread.append(v.astype(bf16))
        ahead.append(row_up(v).astype(bf16))
    pieces = []
    for plane in range(4):
        both, extra = None, None
        for q, k0 in (((0, 2), (1, 0)), ((1, 1),), ((1, 2), (2, 0)), ((2, 1),))[plane]:
            at = k0 * 384
            a = dot(spread[q], w2[:, at + 128 : at + 384], NN)
            b = dot(ahead[q], w2[:, at : at + 128], NN)
            both = a if both is None else both + a
            extra = b if extra is None else extra + b
        for v in (both[:, :128], both[:, 128:] + extra):
            pieces.append(tap_sum(after(v), v, before(v)))
    errs = [pair_of(pieces[:4]), pair_of(pieces[4:])]
    errs = [errs[i] * silu_slope(pre[i * ROWS : i * ROWS + ROWS, :]) for i in (0, 1)]
    errs[0] = without_edge(errs[0])
    errs = [v.astype(bf16).astype(f32) for v in errs]
    shifted = [(after(v), v, before(v)) for v in errs]
    for plane in range(4):
        pair = shifted[plane // 2]
        taps = [
            three(*(rotated(pair[t], t - (plane % 2) * 2 - par) for t in range(3)))
            for par in (0, 1)
        ]
        even, odd = taps
        sources = ((odd, even, row_down(odd)), (row_up(even), odd, even))
        for par in (0, 1):
            for k1 in range(3):
                v = sources[par][k1].astype(bf16)
                for k0 in range(3):
                    target = plane + k0 - 1
                    if target in (1, 2):
                        at = (2 * (target - 1) + par) * ROWS
                        lane = (k0 * 3 + k1) * 128
                        window[at : at + ROWS, lane : lane + 128] = v
    first = dot(window[...], field[...], TN)
    second = second_grad(halves[1:], hidden)
    first_core = lax.axis_index("core") == 0
    for h in (0, 1):
        lane = slice(h * 128, h * 128 + 128)
        for k in range(9):
            at = h * 864 + k * 96
            a, b = first[k * 128 : k * 128 + 96, lane], second[k][:96, lane]
            kept[at : at + 96, :] = jnp.where(first_core, a, b)
            sent[at : at + 96, :] = jnp.where(first_core, b, a).astype(bf16)
    kept[GRAD_ROWS:, :] = jnp.zeros((GRAD_PAD - GRAD_ROWS, 128), f32)
    sent[GRAD_ROWS:, :] = jnp.zeros((GRAD_PAD - GRAD_ROWS, 128), bf16)


def input_grad(window, tall, kept, sent, blocks):
    for p in (0, 1):
        even = dot(window[2 * p * ROWS : (2 * p + 1) * ROWS, :], tall[...], NN)
        odd = dot(window[(2 * p + 1) * ROWS : (2 * p + 2) * ROWS, :], tall[...], NN)
        for g in range(8):
            a = even[g * 32 : g * 32 + 32].reshape(4, 1, 8, 256)
            b = odd[g * 32 : g * 32 + 32].reshape(4, 1, 8, 256)
            v = jnp.concatenate([a, b], 1).reshape(64, 256)
            blocks[g // 2, g % 2, p * 64 : p * 64 + 64, :] = v
    x = lax.axis_index("flt_x")
    partner = x + 1 - 2 * lax.rem(x, 2)
    kept[0] = blocks[x]
    kept[1] = blocks[3 - x]
    sent[0] = blocks[partner].astype(bf16)
    sent[1] = blocks[3 - partner].astype(bf16)


def add_pairs(kept, came, still, sent):
    still[...] = kept[0] + came[0].astype(f32)
    sent[...] = (kept[1] + came[1].astype(f32)).astype(bf16)


def add_halves(kept, came, still, sent):
    y = lax.axis_index("flt_y")
    still[...] = kept[y] + came[y].astype(f32)
    sent[...] = (kept[1 - y] + came[1 - y].astype(f32)).astype(bf16)


def add_last(kept, came, out):
    out[...] = kept[...] + came[...].astype(f32)


def add_core(kept, came, out):
    v = kept[...] + came[...].astype(f32)
    out[...] = v.astype(bf16).reshape(16, GRAD_PAD // 16, 128)


def add_chips(parts, out):
    v = parts[0].astype(f32)
    for i in range(1, 16):
        v = v + parts[i].astype(f32)
    v = v.astype(bf16)
    for i in range(16):
        out[i] = v


def finish_part(rows, first, second, near, sems, to_first):
    pieces = [pl.ds(i * 144, 144) for i in range(6)]
    for i, piece in enumerate(pieces):
        for h in (0, 1):
            at = h * 864 + i * 144
            near[piece, h * 128 : h * 128 + 128] = rows[at : at + 144, :].astype(f32)
        for target, wanted in ((first, to_first), (second, jnp.logical_not(to_first))):

            @pl.when(wanted)
            def _(target=target):
                pltpu.make_async_copy(near.at[piece], target.at[piece], sems.at[i]).start()

    for target, wanted in ((first, to_first), (second, jnp.logical_not(to_first))):

        @pl.when(wanted)
        def _(target=target):
            for i, piece in enumerate(pieces):
                pltpu.make_async_copy(near.at[piece], target.at[piece], sems.at[i]).wait()


def finish_own(rows, first, second, near, sems):
    finish_part(rows, first, second, near, sems, lax.axis_index("core") == 0)


def finish_other(rows, first_in, second_in, first, second, near, sems):
    finish_part(rows, first, second, near, sems, lax.axis_index("core") == 1)


def exchange(v, axis):
    return lax.all_to_all(v, axis, 0, 0, tiled=True)


def swapped(v, axis="core"):
    n = lax.axis_size(axis)
    return lax.ppermute(v, axis, [(i, i ^ 1) for i in range(n)])


def mirrored(v, axis):
    n = lax.axis_size(axis)
    return lax.ppermute(v, axis, [(i, n - 1 - i) for i in range(n)])


def next_chip(v):
    pairs = [(i, i + 1) for i in range(1, lax.axis_size(SP) - 1, 2)]
    return lax.ppermute(v, SP, pairs + [(b, a) for a, b in pairs])


def as_rows(w):
    return jnp.transpose(w, (1, 2, 3, 0, 4)).reshape(864, 256)


def as_filters(rows):
    return jnp.transpose(rows.reshape(3, 3, 3, 32, 256), (3, 0, 1, 2, 4))


def per_device(activations, w_first, w_second, cotangent):
    wide, tall = kernel_call(
        prepare_first, [shape((384, 768), bf16), shape((1152, 256), bf16)], 0, as_rows(w_first)
    )
    (packed,) = kernel_call(
        pack_inputs,
        [shape((8, PACK, 128), bf16)],
        0,
        activations.reshape(128, 256),
        as_rows(w_second),
        cotangent,
        scratch=[
            pltpu.VMEM((128, 256), bf16),
            pltpu.VMEM((864, 256), bf16),
            pltpu.VMEM((1, 4, 4, 256), bf16),
            pltpu.VMEM((COT_ROWS, 128), bf16),
            pltpu.VMEM((8, W_ROWS, 128), bf16),
            pltpu.SemaphoreType.DMA((35,)),
        ],
        space=pltpu.HBM,
        target=pltpu.HBM,
        limit=60,
    )
    got = exchange(packed, FLT)
    pair = shape((ROWS, 128), f32)
    low, high, within, across, field, part = kernel_call(
        first_conv,
        [pair, pair, pair, pair, shape((1024, 256), bf16), shape((8, W_ROWS, 128), bf16)],
        2 * 1024 * 768 * 384,
        got,
        wide,
        scratch=[pltpu.VMEM((1024, 768), bf16)],
    )
    across, within = next_chip(across), swapped(within)
    (w2,) = kernel_call(gather_second, [shape((256, 1152), bf16)], 0, part, swapped(part))
    pre, partial = kernel_call(
        second_conv,
        [shape((512, 128), f32), shape((8, 512, 128), bf16)],
        2 * 256 * 1152 * 256,
        low,
        high,
        within,
        across,
        w2,
        scratch=[pltpu.VMEM((ROWS, 1152), bf16), pltpu.VMEM((2, ROWS, 128), f32)],
    )
    parts = exchange(partial, FLT)
    (err,) = kernel_call(second_error, [shape((128, 256), bf16)], 0, parts, got)
    across, within = next_chip(err), swapped(err)
    hidden, section_out = kernel_call(
        gather_hidden, [shape((1024, 256), bf16), shape((1, 4, 4, 256), f32)], 0, parts
    )
    window, kept, sent = kernel_call(
        backward,
        [shape((1024, 1152), bf16), shape((GRAD_PAD, 128), f32), shape((GRAD_PAD, 128), bf16)],
        2 * 1024 * 1152 * 256 + 2 * 256 * 256 * 384 * 6,
        err,
        within,
        across,
        w2,
        pre,
        field,
        hidden,
        scratch=[pltpu.VMEM((ROWS, 128), f32)],
    )
    came = swapped(sent)
    chunk = shape((16, GRAD_PAD // 16, 128), bf16)
    (mine,) = kernel_call(add_core, [chunk], 0, kept, came)
    mine, window = lax.optimization_barrier((mine, window))
    kept_in, sent_in = kernel_call(
        input_grad,
        [shape((2, 2, 128, 256), f32), shape((2, 2, 128, 256), bf16)],
        2 * 1024 * 1152 * 256,
        window,
        tall,
        scratch=[pltpu.VMEM((4, 2, 128, 256), f32)],
    )
    came_in = swapped(sent_in, "flt_x")
    (mine,) = kernel_call(add_chips, [chunk], 0, exchange(mine, CHIPS))
    kept_in, sent_in = kernel_call(
        add_pairs, [shape((2, 128, 256), f32), shape((2, 128, 256), bf16)], 0, kept_in, came_in
    )
    mine, sent_in = lax.optimization_barrier((mine, sent_in))
    came_in = mirrored(sent_in, "flt_x")
    mine = exchange(mine, CHIPS).reshape(GRAD_PAD, 128)
    kept_in, sent_in = kernel_call(
        add_halves, [shape((128, 256), f32), shape((128, 256), bf16)], 0, kept_in, came_in
    )
    came_in = swapped(sent_in, "flt_y")
    (grad_input,) = kernel_call(add_last, [shape((128, 256), f32)], 0, kept_in, came_in)
    mine, grad_input = lax.optimization_barrier((mine, grad_input))
    full = [shape((864, 256), f32)] * 2
    scratch = [pltpu.VMEM((864, 256), f32), pltpu.SemaphoreType.DMA((6,))]
    other = swapped(mine)
    grads = kernel_call(finish_own, full, 0, mine, scratch=scratch, target=pltpu.HBM)
    grads = kernel_call(
        finish_other, full, 0, other, *grads, scratch=scratch, target=pltpu.HBM, alias={1: 0, 2: 1}
    )
    return (section_out, grad_input.reshape(2, 8, 8, 256), *(as_filters(g) for g in grads))


def solution(mesh):
    torus = Mesh(mesh.devices.reshape(8, 2, 2, 4, 2), (*SP, *FLT))
    whole = P(FLT, None, None, None, None)
    rows = P(SP, FLT, None, None)
    return jax.shard_map(
        per_device,
        mesh=torus,
        in_specs=(rows, whole, whole, rows),
        out_specs=(rows, rows, whole, whole),
        check_vma=False,
    )
```

```python
import jax
import jax.numpy as jnp
from jax import lax
from jax.experimental import pallas as pl
from jax.experimental.pallas import tpu as pltpu
from jax.sharding import Mesh
from jax.sharding import PartitionSpec as P

SP = ("sp_z", "sp_y", "core")
CHIPS = ("sp_z", "sp_y")
FLT = ("flt_x", "flt_y")
bf16, f32 = jnp.bfloat16, jnp.float32

ROWS = 256
X_ROWS, COT_ROWS, W_ROWS = 256, 32, 128
PACK = X_ROWS + COT_ROWS + W_ROWS
GRAD_ROWS, GRAD_PAD = 1728, 1792
NT = (((1,), (1,)), ((), ()))
NN = (((1,), (0,)), ((), ()))
TN = (((0,), (0,)), ((), ()))


def dot(a, b, dims):
    return lax.dot_general(a, b, dims, preferred_element_type=f32)


def kernel_call(
    body, outs, flops, *args, scratch=(), space=pltpu.VMEM, target=pltpu.VMEM, limit=16, alias={}
):
    spaces = [pltpu.HBM if i in alias else space for i in range(len(args))]
    moved = sum(a.size * a.dtype.itemsize for a in (*args, *outs))
    return pl.pallas_call(
        body,
        out_shape=outs,
        in_specs=[pl.BlockSpec(memory_space=s) for s in spaces],
        out_specs=[pl.BlockSpec(memory_space=target)] * len(outs),
        scratch_shapes=scratch,
        input_output_aliases=alias,
        compiler_params=pltpu.CompilerParams(vmem_limit_bytes=limit << 20),
        cost_estimate=pl.CostEstimate(flops=flops, bytes_accessed=moved, transcendentals=0),
    )(*args)


def shape(dims, dtype):
    return jax.ShapeDtypeStruct(dims, dtype)


def lanes(rows):
    return lax.broadcasted_iota(jnp.int32, (rows, 128), 1)


def cells(rows):
    return lax.rem(lax.broadcasted_iota(jnp.int32, (rows, 128), 0), 8)


def before(v):
    return jnp.where(cells(v.shape[0]) == 0, 0.0, pltpu.roll(v, 1, 0))


def after(v):
    return jnp.where(cells(v.shape[0]) == 7, 0.0, pltpu.roll(v, v.shape[0] - 1, 0))


def rotated(v, slots):
    by = (32 * slots) % 128
    return pltpu.roll(v, by, 1) if by else v


def three(a, b, c):
    lane = lanes(a.shape[0])
    return jnp.where(lane < 32, a, jnp.where(lane < 64, b, jnp.where(lane < 96, c, 0.0)))


def row_down(v):
    return jnp.concatenate([jnp.zeros((8, v.shape[1]), v.dtype), v[:-8]], 0)


def row_up(v):
    return jnp.concatenate([v[8:], jnp.zeros((8, v.shape[1]), v.dtype)], 0)


def tap_sum(first, middle, last):
    lane = lanes(ROWS)
    t = jnp.where(lane < 32, first, jnp.where(lane < 64, middle, last))
    return t + rotated(t, -1) + rotated(t, -2)


def pair_of(pieces):
    lane = lanes(ROWS)
    v = pieces[0]
    for slot in (1, 2, 3):
        v = jnp.where(lane < 32 * slot, v, rotated(pieces[slot], slot))
    return v


def sigmoid(v):
    return jax.nn.sigmoid(v)


def silu_slope(v):
    s = sigmoid(v)
    return s * (1.0 + v * (1.0 - s))


def pack_inputs(x_far, w_far, cot_far, out, x, w, cot_near, cot, blocks, sems):
    loads = [
        pltpu.make_async_copy(x_far, x, sems.at[0]),
        pltpu.make_async_copy(cot_far, cot_near, sems.at[1]),
        pltpu.make_async_copy(w_far, w, sems.at[2]),
    ]
    for copy in loads:
        copy.start()
    sent = []

    def send(source, f, at, size):
        target = out.at[f, pl.ds(at, size), :]
        copy = pltpu.make_async_copy(source, target, sems.at[3 + len(sent)])
        copy.start()
        sent.append(copy)

    loads[0].wait()
    for f in range(8):
        for h in (0, 1):
            send(x.at[:, pl.ds(h * 128, 128)], f, h * 128, 128)
    loads[1].wait()
    for h in (0, 1):
        rows = [cot_near[0, i, :, h * 128 : h * 128 + 128].astype(f32) for i in range(4)]
        cot[h * 16 : h * 16 + 16, :] = jnp.concatenate(rows, 0).astype(bf16)
    for f in range(8):
        send(cot, f, X_ROWS, COT_ROWS)
    loads[2].wait()
    first_core = lax.axis_index("core") == 0
    lane = lanes(32)

    def block(k, m, h):
        at = pl.multiple_of(96 * k, 32)
        taps = [w[pl.ds(at + 32 * t, 32), h * 128 : h * 128 + 128].astype(f32) for t in range(3)]
        return three(*(rotated(taps[t], t - m) for t in range(3)))

    for h in (0, 1):
        for b in range(4):
            extra = w[(12 + min(b, 2)) * 32 : (13 + min(b, 2)) * 32, h * 128 : h * 128 + 128]
            extra = extra.astype(f32)
            for m in range(4):
                v = block(jnp.where(first_core, b, b + 5), m, h)
                v = jnp.where(lane < 96, v, rotated(extra, 3 - m))
                blocks[4 * h + m, b * 32 : b * 32 + 32, :] = v.astype(bf16)
        for m in range(4):
            send(blocks.at[4 * h + m], 4 * h + m, X_ROWS + COT_ROWS, W_ROWS)
    for copy in sent:
        copy.wait()


def prepare_first(w, wide, tall):
    zero = jnp.zeros((32, 256), bf16)
    for k0 in range(3):
        for k1 in range(3):
            for t in range(4):
                at = ((k0 * 3 + k1) * 3 + t) * 32
                v = w[at : at + 32, :] if t < 3 else zero
                wide[k0 * 128 + t * 32 : k0 * 128 + t * 32 + 32, k1 * 256 : k1 * 256 + 256] = v
                row = (k0 * 3 + k1) * 128 + t * 32
                tall[row : row + 32, :] = v


def first_conv(got, wide, low, high, within, across, field, part, window):
    part[...] = got[:, X_ROWS + COT_ROWS :, :]
    parts = {}
    for h in (0, 1):
        for p in (0, 1):
            blocks = ([], [])
            for g in range(8):
                at = h * 128 + p * 64
                v = got[g, at : at + 64, :].astype(f32).reshape(4, 2, 8, 128)
                for par in (0, 1):
                    blocks[par].append(v[:, par].reshape(32, 128))
            for par in (0, 1):
                parts[p, par, h] = jnp.concatenate(blocks[par], 0)
    for p in (0, 1):
        for h in (0, 1):
            even, odd = parts[p, 0, h], parts[p, 1, h]
            sources = ((row_down(odd), even, odd), (even, odd, row_up(even)))
            for par in (0, 1):
                at = (2 * p + par) * ROWS
                for k1 in range(3):
                    lane = k1 * 256 + h * 128
                    window[at : at + ROWS, lane : lane + 128] = sources[par][k1].astype(bf16)
                field[at : at + ROWS, h * 128 : h * 128 + 128] = sources[par][1].astype(bf16)
    sums = [dot(window[i * ROWS : i * ROWS + ROWS, :], wide[...], NT) for i in range(4)]
    pieces = []
    for plane in range(4):
        for par in (0, 1):
            terms = [
                sums[2 * p + par][:, k0 * 128 : k0 * 128 + 128]
                for p in (0, 1)
                for k0 in range(3)
                if p - k0 + 2 == plane
            ]
            v = terms[0] if len(terms) == 1 else terms[0] + terms[1]
            pieces.append(tap_sum(before(v), v, after(v)))
    a, b = pair_of(pieces[:4]), pair_of(pieces[4:])
    first_core = lax.axis_index("core") == 0
    low[...] = a
    high[...] = b
    within[...] = jnp.where(first_core, b, a)
    across[...] = jnp.where(first_core, a, b)


def gather_second(own, other, w2):
    first_core = lax.axis_index("core") == 0
    for g in range(8):
        row = slice(g * 32, g * 32 + 32)
        blocks = []
        for b in range(4):
            at = slice(b * 32, b * 32 + 32)
            x, y = own[g, at, :].astype(f32), other[g, at, :].astype(f32)
            early, late = jnp.where(first_core, x, y), jnp.where(first_core, y, x)
            w2[row, b * 128 : b * 128 + 128] = early.astype(bf16)
            w2[row, (b + 5) * 128 : (b + 6) * 128] = late.astype(bf16)
            blocks.append(early)
        v = three(*(rotated(blocks[t], t - 3) for t in range(3)))
        w2[row, 512:640] = v.astype(bf16)


def at_first_plane():
    return sum(lax.axis_index(name) for name in SP) == 0


def without_edge(v):
    return jnp.where(jnp.logical_and(at_first_plane(), lanes(ROWS) < 64), 0.0, v)


def below_above(within, across):
    first_core = lax.axis_index("core") == 0
    a, b = within[...], across[...]
    return jnp.where(first_core, b, a), jnp.where(first_core, a, b)


def second_conv(low, high, within, across, w2, pre, out, window, full):
    below, above = below_above(within, across)
    pairs = [low[...] + below, high[...] + above]
    pre[0:ROWS, :] = pairs[0]
    pre[ROWS:, :] = pairs[1]
    hidden = [v * sigmoid(v) for v in pairs]
    own = jnp.where(lanes(ROWS) < 64, rotated(hidden[0], 2), rotated(hidden[1], 2)).astype(bf16)
    for g in range(8):
        out[g, ROWS:, :] = own
    hidden[0] = without_edge(hidden[0])
    hidden = [v.astype(bf16).astype(f32) for v in hidden]
    shifted = [(before(v), v, after(v)) for v in hidden]
    for plane in range(3):
        pair = shifted[plane // 2]
        for par in (0, 1):
            slot = (plane % 2) * 2 + par
            v = three(*(rotated(pair[t], t - slot) for t in range(3)))
            at = (plane * 3 + 1 + par) * 128
            window[:, at : at + 128] = v.astype(bf16)
            if par:
                window[:, plane * 384 : plane * 384 + 128] = row_down(v).astype(bf16)
    total = dot(window[...], w2[...], NT)
    for h in (0, 1):
        full[h] = total[:, h * 128 : h * 128 + 128]
        v = full[h, pl.ds(0, 128, 2), :].astype(bf16)
        for g in range(8):
            out[g, h * 128 : h * 128 + 128, :] = v


def section_rows(parts, section):
    flt = lax.axis_index("flt_x") * 2 + lax.axis_index("flt_y")
    for h in (0, 1):
        row = pl.ds(pl.multiple_of(h * 128 + flt * 16, 16), 16)
        v = parts[0, row, :].astype(f32)
        for g in range(1, 8):
            v = v + parts[g, row, :].astype(f32)
        v = v * sigmoid(v)
        for i in range(4):
            section[0, i, :, h * 128 : h * 128 + 128] = v[4 * i : 4 * i + 4]


def gather_hidden(parts, field):
    lane = lanes(ROWS)
    for h in (0, 1):
        blocks = [parts[4 * h + m, ROWS:, :].astype(f32) for m in range(4)]
        for slot in range(4):
            v = rotated(blocks[0], -slot)
            for m in (1, 2, 3):
                v = jnp.where(lane < 32 * m, v, rotated(blocks[m], m - slot))
            field[slot * ROWS : slot * ROWS + ROWS, h * 128 : h * 128 + 128] = v.astype(bf16)


def second_error(parts, got, err):
    for h in (0, 1):
        lane = slice(h * 128, h * 128 + 128)
        row = slice(h * 128, h * 128 + 128)
        v = parts[0, row, :].astype(f32)
        for g in range(1, 8):
            v = v + parts[g, row, :].astype(f32)
        cot = jnp.concatenate(
            [got[g, X_ROWS + h * 16 : X_ROWS + h * 16 + 16, :].astype(f32) for g in range(8)], 0
        )
        err[:, lane] = (cot * silu_slope(v)).astype(bf16)


def spread_out(err, full):
    full[...] = jnp.zeros((ROWS, 128), f32)
    full[pl.ds(0, 128, 2), :] = err
    return full[...]


def second_grad(spread, hidden):
    flt = lax.axis_index("flt_x") * 2 + lax.axis_index("flt_y")
    turn = lax.rem(8 - flt, 4) * 32
    plain, ahead = [], []
    for left, right in spread:
        v = pltpu.roll(jnp.where(flt < 4, left, right), turn, 1)
        v = three(after(v), rotated(v, 1), rotated(before(v), 2))
        plain.append(v.astype(bf16))
        ahead.append(row_up(v).astype(bf16))
    grads = []
    for k0 in range(3):
        q = 1 if k0 == 0 else 0
        for k1 in range(3):
            at = ((1 if k0 == 1 else 3) - (1 if k1 == 1 else 0)) * ROWS
            errs = (ahead if k1 == 0 else plain)[q]
            grads.append(dot(errs, hidden[at : at + ROWS, :], TN))
    return grads


def backward(own, within, across, w2, pre, field, hidden, window, kept, sent, full):
    below, above = below_above(within, across)
    spread, ahead, halves = [], [], []
    for err in (below, own[...], above):
        both = [spread_out(err[:, h * 128 : h * 128 + 128].astype(f32), full) for h in (0, 1)]
        halves.append(both)
        v = jnp.concatenate(both, 1)
        spread.append(v.astype(bf16))
        ahead.append(row_up(v).astype(bf16))
    pieces = []
    for plane in range(4):
        both, extra = None, None
        for q, k0 in (((0, 2), (1, 0)), ((1, 1),), ((1, 2), (2, 0)), ((2, 1),))[plane]:
            at = k0 * 384
            a = dot(spread[q], w2[:, at + 128 : at + 384], NN)
            b = dot(ahead[q], w2[:, at : at + 128], NN)
            both = a if both is None else both + a
            extra = b if extra is None else extra + b
        for v in (both[:, :128], both[:, 128:] + extra):
            pieces.append(tap_sum(after(v), v, before(v)))
    errs = [pair_of(pieces[:4]), pair_of(pieces[4:])]
    errs = [errs[i] * silu_slope(pre[i * ROWS : i * ROWS + ROWS, :]) for i in (0, 1)]
    errs[0] = without_edge(errs[0])
    errs = [v.astype(bf16).astype(f32) for v in errs]
    shifted = [(after(v), v, before(v)) for v in errs]
    for plane in range(4):
        pair = shifted[plane // 2]
        taps = [
            three(*(rotated(pair[t], t - (plane % 2) * 2 - par) for t in range(3)))
            for par in (0, 1)
        ]
        even, odd = taps
        sources = ((odd, even, row_down(odd)), (row_up(even), odd, even))
        for par in (0, 1):
            for k1 in range(3):
                v = sources[par][k1].astype(bf16)
                for k0 in range(3):
                    target = plane + k0 - 1
                    if target in (1, 2):
                        at = (2 * (target - 1) + par) * ROWS
                        lane = (k0 * 3 + k1) * 128
                        window[at : at + ROWS, lane : lane + 128] = v
    first = dot(window[...], field[...], TN)
    second = second_grad(halves[1:], hidden)
    first_core = lax.axis_index("core") == 0
    for h in (0, 1):
        lane = slice(h * 128, h * 128 + 128)
        for k in range(9):
            at = h * 864 + k * 96
            a, b = first[k * 128 : k * 128 + 96, lane], second[k][:96, lane]
            kept[at : at + 96, :] = jnp.where(first_core, a, b)
            sent[at : at + 96, :] = jnp.where(first_core, b, a).astype(bf16)
    kept[GRAD_ROWS:, :] = jnp.zeros((GRAD_PAD - GRAD_ROWS, 128), f32)
    sent[GRAD_ROWS:, :] = jnp.zeros((GRAD_PAD - GRAD_ROWS, 128), bf16)


def input_grad(window, tall, kept, sent, blocks):
    for p in (0, 1):
        even = dot(window[2 * p * ROWS : (2 * p + 1) * ROWS, :], tall[...], NN)
        odd = dot(window[(2 * p + 1) * ROWS : (2 * p + 2) * ROWS, :], tall[...], NN)
        for g in range(8):
            a = even[g * 32 : g * 32 + 32].reshape(4, 1, 8, 256)
            b = odd[g * 32 : g * 32 + 32].reshape(4, 1, 8, 256)
            v = jnp.concatenate([a, b], 1).reshape(64, 256)
            blocks[g // 2, g % 2, p * 64 : p * 64 + 64, :] = v
    x = lax.axis_index("flt_x")
    partner = x + 1 - 2 * lax.rem(x, 2)
    kept[0] = blocks[x]
    kept[1] = blocks[3 - x]
    sent[0] = blocks[partner].astype(bf16)
    sent[1] = blocks[3 - partner].astype(bf16)


def add_pairs(kept, came, still, sent):
    still[...] = kept[0] + came[0].astype(f32)
    sent[...] = (kept[1] + came[1].astype(f32)).astype(bf16)


def add_halves(kept, came, still, sent):
    y = lax.axis_index("flt_y")
    still[...] = kept[y] + came[y].astype(f32)
    sent[...] = (kept[1 - y] + came[1 - y].astype(f32)).astype(bf16)


def add_last(kept, came, out):
    out[...] = kept[...] + came[...].astype(f32)


def add_core(kept, came, out):
    v = kept[...] + came[...].astype(f32)
    out[...] = v.astype(bf16).reshape(16, GRAD_PAD // 16, 128)


def add_chips(parts, out):
    v = parts[0].astype(f32)
    for i in range(1, 16):
        v = v + parts[i].astype(f32)
    v = v.astype(bf16)
    for i in range(16):
        out[i] = v


def finish_part(rows, first, second, near, sems, to_first):
    pieces = [pl.ds(i * 144, 144) for i in range(6)]
    for i, piece in enumerate(pieces):
        for h in (0, 1):
            at = h * 864 + i * 144
            near[piece, h * 128 : h * 128 + 128] = rows[at : at + 144, :].astype(f32)
        for target, wanted in ((first, to_first), (second, jnp.logical_not(to_first))):

            @pl.when(wanted)
            def _(target=target):
                pltpu.make_async_copy(near.at[piece], target.at[piece], sems.at[i]).start()

    for target, wanted in ((first, to_first), (second, jnp.logical_not(to_first))):

        @pl.when(wanted)
        def _(target=target):
            for i, piece in enumerate(pieces):
                pltpu.make_async_copy(near.at[piece], target.at[piece], sems.at[i]).wait()


def finish_own(rows, first, second, near, sems):
    finish_part(rows, first, second, near, sems, lax.axis_index("core") == 0)


def finish_other(rows, first_in, second_in, first, second, near, sems):
    finish_part(rows, first, second, near, sems, lax.axis_index("core") == 1)


def exchange(v, axis):
    return lax.all_to_all(v, axis, 0, 0, tiled=True)


def swapped(v, axis="core"):
    n = lax.axis_size(axis)
    return lax.ppermute(v, axis, [(i, i ^ 1) for i in range(n)])


def mirrored(v, axis):
    n = lax.axis_size(axis)
    return lax.ppermute(v, axis, [(i, n - 1 - i) for i in range(n)])


def next_chip(v):
    pairs = [(i, i + 1) for i in range(1, lax.axis_size(SP) - 1, 2)]
    return lax.ppermute(v, SP, pairs + [(b, a) for a, b in pairs])


def as_rows(w):
    return jnp.transpose(w, (1, 2, 3, 0, 4)).reshape(864, 256)


def as_filters(rows):
    return jnp.transpose(rows.reshape(3, 3, 3, 32, 256), (3, 0, 1, 2, 4))


def per_device(activations, w_first, w_second, cotangent):
    wide, tall = kernel_call(
        prepare_first, [shape((384, 768), bf16), shape((1152, 256), bf16)], 0, as_rows(w_first)
    )
    (packed,) = kernel_call(
        pack_inputs,
        [shape((8, PACK, 128), bf16)],
        0,
        activations.reshape(128, 256),
        as_rows(w_second),
        cotangent,
        scratch=[
            pltpu.VMEM((128, 256), bf16),
            pltpu.VMEM((864, 256), bf16),
            pltpu.VMEM((1, 4, 4, 256), bf16),
            pltpu.VMEM((COT_ROWS, 128), bf16),
            pltpu.VMEM((8, W_ROWS, 128), bf16),
            pltpu.SemaphoreType.DMA((35,)),
        ],
        space=pltpu.HBM,
        target=pltpu.HBM,
        limit=60,
    )
    got = exchange(packed, FLT)
    pair = shape((ROWS, 128), f32)
    low, high, within, across, field, part = kernel_call(
        first_conv,
        [pair, pair, pair, pair, shape((1024, 256), bf16), shape((8, W_ROWS, 128), bf16)],
        2 * 1024 * 768 * 384,
        got,
        wide,
        scratch=[pltpu.VMEM((1024, 768), bf16)],
    )
    across, within = next_chip(across), swapped(within)
    (w2,) = kernel_call(gather_second, [shape((256, 1152), bf16)], 0, part, swapped(part))
    pre, partial = kernel_call(
        second_conv,
        [shape((512, 128), f32), shape((8, 512, 128), bf16)],
        2 * 256 * 1152 * 256,
        low,
        high,
        within,
        across,
        w2,
        scratch=[pltpu.VMEM((ROWS, 1152), bf16), pltpu.VMEM((2, ROWS, 128), f32)],
    )
    parts = exchange(partial, FLT)
    (err,) = kernel_call(second_error, [shape((128, 256), bf16)], 0, parts, got)
    across, within = next_chip(err), swapped(err)
    (hidden,) = kernel_call(gather_hidden, [shape((1024, 256), bf16)], 0, parts)
    window, kept, sent = kernel_call(
        backward,
        [shape((1024, 1152), bf16), shape((GRAD_PAD, 128), f32), shape((GRAD_PAD, 128), bf16)],
        2 * 1024 * 1152 * 256 + 2 * 256 * 256 * 384 * 6,
        err,
        within,
        across,
        w2,
        pre,
        field,
        hidden,
        scratch=[pltpu.VMEM((ROWS, 128), f32)],
    )
    came = swapped(sent)
    kept_in, sent_in = kernel_call(
        input_grad,
        [shape((2, 2, 128, 256), f32), shape((2, 2, 128, 256), bf16)],
        2 * 1024 * 1152 * 256,
        window,
        tall,
        scratch=[pltpu.VMEM((4, 2, 128, 256), f32)],
    )
    chunk = shape((16, GRAD_PAD // 16, 128), bf16)
    (mine,) = kernel_call(add_core, [chunk], 0, kept, came)
    mine, sent_in, parts = lax.optimization_barrier((mine, sent_in, parts))
    (section_out,) = kernel_call(section_rows, [shape((1, 4, 4, 256), f32)], 0, parts)
    came_in = swapped(sent_in, "flt_x")
    (mine,) = kernel_call(add_chips, [chunk], 0, exchange(mine, CHIPS))
    kept_in, sent_in = kernel_call(
        add_pairs, [shape((2, 128, 256), f32), shape((2, 128, 256), bf16)], 0, kept_in, came_in
    )
    mine, sent_in, section_out = lax.optimization_barrier((mine, sent_in, section_out))
    came_in = mirrored(sent_in, "flt_x")
    mine = exchange(mine, CHIPS).reshape(GRAD_PAD, 128)
    kept_in, sent_in = kernel_call(
        add_halves, [shape((128, 256), f32), shape((128, 256), bf16)], 0, kept_in, came_in
    )
    came_in = swapped(sent_in, "flt_y")
    (grad_input,) = kernel_call(add_last, [shape((128, 256), f32)], 0, kept_in, came_in)
    mine, grad_input = lax.optimization_barrier((mine, grad_input))
    full = [shape((864, 256), f32)] * 2
    scratch = [pltpu.VMEM((864, 256), f32), pltpu.SemaphoreType.DMA((6,))]
    other = swapped(mine)
    grads = kernel_call(finish_own, full, 0, mine, scratch=scratch, target=pltpu.HBM)
    grads = kernel_call(
        finish_other, full, 0, other, *grads, scratch=scratch, target=pltpu.HBM, alias={1: 0, 2: 1}
    )
    return (section_out, grad_input.reshape(2, 8, 8, 256), *(as_filters(g) for g in grads))


def solution(mesh):
    torus = Mesh(mesh.devices.reshape(8, 2, 2, 4, 2), (*SP, *FLT))
    whole = P(FLT, None, None, None, None)
    rows = P(SP, FLT, None, None)
    return jax.shard_map(
        per_device,
        mesh=torus,
        in_specs=(rows, whole, whole, rows),
        out_specs=(rows, rows, whole, whole),
        check_vma=False,
    )
```
